32 devices in a mesh: curve: 8 (over z, x), tile: 4 (over y, core).
Axes of the slice: x: 2, y: 2, z: 4, core: 2. Of those that a mesh axis runs over, the one named last changes fastest.
Arguments:
- state: float32 [5, 1024, 512], P(None, ('curve', 'tile')), may hold values from -6 to 6
- levels: int32 [1024], P(('curve', 'tile')), may hold values from 0 to 2
- send_faces: int32 [128, 4], P(('curve', 'tile')), may hold values from 0 to 959, as said below
- send_counts: int32 [128], P(('curve', 'tile')), may hold values from 0 to 4, as said below
- recv_faces: int32 [128, 4], P(('curve', 'tile')), may hold values from 0 to 191, as said below
- recv_orients: int32 [128, 4], P(('curve', 'tile')), may hold values from 0 to 7, as said below
- recv_counts: int32 [128], P(('curve', 'tile')), may hold values from 0 to 4
- curve_faces: int32 [64, 16], P(('curve', 'tile')), may hold values from 0 to 191, as said below
- curve_orients: int32 [64, 16], P(('curve', 'tile')), may hold values from 0 to 7, as said below
- curve_counts: int32 [64], P(('curve', 'tile')), may hold values from 0 to 16, as said below
Outputs:
- advanced: float32 [5, 1024, 512], P(None, ('curve', 'tile'))
The draws below stay inside these ranges and needn't reach their ends.
Inputs may be any that keep to these rules, and one draw needn't show every extreme that they name: `send_faces`: row p of device (b, t) lists in its first send_counts entries the pairs it shares with device (b, p): (6 e + f) 5 + c with f 3 or 5 and c 0 to 3 for a half-face mortar of a coarse face, 4 for a whole face; each coarse face listed has its four children 0 to 3 listed once each, possibly with different peers; any other face id appears at most once in all lists of a device; entries past the count are 0. `send_counts`: the count of device (b, t) for peer p equals the receive count of device (b, p) for peer t. `recv_faces`: slot k of row t of device (b, p) is face 6 e + f paired with slot k of row p of device (b, t), with f = 2 where the sender's face is 3 and 4 where it is 5; entries past the count are 0. `recv_orients`: R_o maps the sender's node order into the receiver's; 0 past the count. `curve_faces`: row 0 names faces with f = 0, row 1 faces with f = 1; slot k of row 1 of device (b, t) pairs with slot k of row 0 of device (b + 1, t); entries past the count are 0. `curve_orients`: the two sides of a pair hold mutually inverse orientations; 0 past the count. `curve_counts`: both sides of a pair of rows hold the same count; it is 0 towards a curve index that does not exist.
All inputs are finite; a program needn't handle non-finite values.
Results may differ from the reference program's by a relative error of at most 0.0003.
Values sent between devices are 32-bit elements; how exact they have to be, the bound alone decides.
A program may use at most 64 MiB of HBM per device.

```python
import jax
import jax.numpy as jnp
import numpy as np
from jax import lax

FIELDS = 5
NODES = 512
E_DEV = 32
ELEMS = 1024
CAPM = 4
CAPH = 16
N_CURVE = 8
N_TILE = 4


def orient_inverse():
    perm_table = np.zeros((8, 64), np.int64)
    for orient_code in range(8):
        for first_at in range(8):
            for second_at in range(8):
                if orient_code & 4:
                    upper_at, lower_at = (second_at, first_at)
                else:
                    upper_at, lower_at = (first_at, second_at)
                if orient_code & 1:
                    upper_at = 7 - upper_at
                if orient_code & 2:
                    lower_at = 7 - lower_at
                perm_table[orient_code, 8 * first_at + second_at] = 8 * upper_at + lower_at
    inverse = np.zeros((8,), np.int32)
    for first_at in range(8):
        for second_at in range(8):
            if int(np.sum(perm_table[first_at][perm_table[second_at]] == np.arange(64))) == 64:
                inverse[first_at] = second_at
    return inverse


def shuffles(base_key, row_count, row_width):

    def one_row(row_key):
        return jax.random.permutation(row_key, row_width)
    return jax.vmap(one_row)(jax.random.split(base_key, row_count)).astype(jnp.int32)


def live_ranks(base_key, live_grid):
    row_count, row_width = live_grid.shape
    shuffled = shuffles(base_key, row_count, row_width)
    scores = jnp.where(live_grid, shuffled, shuffled + row_width)
    ranked = jnp.argsort(scores, axis=1, stable=True)
    return jnp.argsort(ranked, axis=1, stable=True).astype(jnp.int32)


def build_lists(base_key):
    subkeys = jax.random.split(jax.random.fold_in(base_key, 91357), 12)
    devices = N_CURVE * N_TILE
    unit_total = N_TILE * CAPM
    busy_tile = jax.random.randint(subkeys[0], (N_CURVE,), 0, N_TILE)
    light_load = jnp.minimum(jax.random.randint(subkeys[1], (N_CURVE, N_TILE, N_TILE), 0, max(2, CAPM // 2 + 1)), CAPM)
    peer_ids = jnp.arange(N_TILE)
    send_count = jnp.where(peer_ids[None, None, :] == busy_tile[:, None, None], CAPM, light_load).astype(jnp.int32)
    live_grid = jnp.arange(CAPM) < send_count[..., None]
    send_live = live_grid.reshape(devices, unit_total)
    send_rank = live_ranks(subkeys[2], send_live)
    live_total = jnp.sum(send_live.astype(jnp.int32), axis=1, keepdims=True)
    coarse_total = live_total // 5
    is_coarse = send_rank < 4 * coarse_total
    unit_ids = jnp.where(is_coarse, send_rank // 4, send_rank - 3 * coarse_total)
    child_ids = jnp.where(is_coarse, send_rank % 4, 4)
    send_elems = jnp.take_along_axis(shuffles(subkeys[3], devices, E_DEV), unit_ids, axis=1)
    unit_bits = jnp.take_along_axis(jax.random.randint(subkeys[4], (devices, unit_total), 0, 2), unit_ids, axis=1)
    send_face = jnp.where(send_live, (send_elems * 6 + 3 + 2 * unit_bits) * 5 + child_ids, 0)
    recv_live = jnp.transpose(live_grid, (0, 2, 1, 3)).reshape(devices, unit_total)
    recv_bits = jnp.transpose(unit_bits.reshape(N_CURVE, N_TILE, N_TILE, CAPM), (0, 2, 1, 3)).reshape(devices, unit_total)
    recv_rank = live_ranks(subkeys[5], recv_live)
    recv_elems = jnp.take_along_axis(shuffles(subkeys[6], devices, E_DEV), recv_rank, axis=1)
    recv_face = jnp.where(recv_live, recv_elems * 6 + 2 + 2 * recv_bits, 0)
    recv_orient = jnp.where(recv_live, jax.random.randint(subkeys[7], (devices, unit_total), 0, 8), 0)
    recv_count = jnp.transpose(send_count, (0, 2, 1))
    edge_count = jax.random.randint(subkeys[8], (N_CURVE - 1, N_TILE), CAPH - CAPH // 2, CAPH + 1)
    full_edge = jax.random.randint(subkeys[9], (N_TILE,), 0, N_CURVE - 1)
    edge_count = jnp.where(jnp.arange(N_CURVE - 1)[:, None] == full_edge[None, :], CAPH, edge_count).astype(jnp.int32)
    zero_row = jnp.zeros((1, N_TILE), jnp.int32)
    curve_count = jnp.stack([jnp.concatenate([zero_row, edge_count], 0), jnp.concatenate([edge_count, zero_row], 0)], axis=2)
    curve_live = jnp.arange(CAPH) < curve_count[..., None]
    edge_orient = jax.random.randint(subkeys[10], (N_CURVE - 1, N_TILE, CAPH), 0, 8)
    inverse = jnp.asarray(orient_inverse(), jnp.int32)
    inverse_edge = jnp.sum((edge_orient[..., None] == jnp.arange(8)).astype(jnp.int32) * inverse, axis=-1)
    zero_plane = jnp.zeros((1, N_TILE, CAPH), jnp.int32)
    curve_orient = jnp.stack([jnp.concatenate([zero_plane, inverse_edge], 0), jnp.concatenate([edge_orient, zero_plane], 0)], axis=2)
    curve_orient = jnp.where(curve_live, curve_orient, 0)
    curve_elems = shuffles(subkeys[11], devices, E_DEV)[:, :CAPH].reshape(N_CURVE, N_TILE, 1, CAPH)
    curve_face = jnp.where(curve_live, curve_elems * 6 + jnp.arange(2).reshape(1, 1, 2, 1), 0)
    return (send_face, send_count, recv_face, recv_orient, recv_count, curve_face, curve_orient, curve_count)


def draw_send_faces(key, part):
    return build_lists(key)[0].reshape(N_CURVE * N_TILE * N_TILE, CAPM).astype(jnp.int32)


def draw_send_counts(key, part):
    return build_lists(key)[1].reshape(-1).astype(jnp.int32)


def draw_recv_faces(key, part):
    return build_lists(key)[2].reshape(N_CURVE * N_TILE * N_TILE, CAPM).astype(jnp.int32)


def draw_recv_orients(key, part):
    return build_lists(key)[3].reshape(N_CURVE * N_TILE * N_TILE, CAPM).astype(jnp.int32)


def draw_recv_counts(key, part):
    return build_lists(key)[4].reshape(-1).astype(jnp.int32)


def draw_curve_faces(key, part):
    return build_lists(key)[5].reshape(N_CURVE * N_TILE * 2, CAPH).astype(jnp.int32)


def draw_curve_orients(key, part):
    return build_lists(key)[6].reshape(N_CURVE * N_TILE * 2, CAPH).astype(jnp.int32)


def draw_curve_counts(key, part):
    return build_lists(key)[7].reshape(-1).astype(jnp.int32)


def with_ends(drawn, stream_key, low, high):
    longest = drawn.shape.index(max(drawn.shape))
    spots = []
    for shift in (0, 1):
        where = [jax.random.randint(jax.random.fold_in(stream_key, axis), (), 0, length) for axis, length in enumerate(drawn.shape)]
        where[longest] = (where[longest] + shift) % drawn.shape[longest]
        spots.append(tuple(where))
    return drawn.at[spots[0]].set(low).at[spots[1]].set(high)


def block_levels(own_key, dims, cuts, smallest, largest):
    def one(axis_at, shards_of):
        heights = jax.random.uniform(jax.random.fold_in(jax.random.fold_in(own_key, 6), axis_at), (shards_of,), jnp.float32, smallest / len(cuts), largest / len(cuts))
        return jnp.repeat(jnp.exp(heights), dims[axis_at] // shards_of).reshape((-1,) + (1,) * (len(dims) - axis_at - 1))

    factor_of = one(*cuts[0])
    for cut in cuts[1:]:
        factor_of = factor_of * one(*cut)
    return factor_of


def normal_values(own_key, extent, scale, limit, cuts=(), kind=jnp.bfloat16):
    values = jax.random.normal(own_key, extent, jnp.float32) * scale
    if len(cuts) > 0:
        values = block_levels(own_key, extent, cuts, -0.22, 0.18) * values
    return jnp.clip(values, min=-limit, max=limit).astype(kind)


def setup_inputs(seed: int = 0) -> dict:
    seeds = jax.random.split(jax.random.key(seed), 11)
    return {
        "state": normal_values(seeds[0], (FIELDS, ELEMS, NODES), 1.0, 6.0, ((1, 32),), jnp.float32),
        "levels": with_ends(jax.random.randint(seeds[1], (ELEMS,), 0, 3), jax.random.fold_in(seeds[1], 1), 0, 2).astype(jnp.int32),
        "send_faces": draw_send_faces(jax.random.fold_in(seeds[10], 71), 0),
        "send_counts": draw_send_counts(jax.random.fold_in(seeds[10], 71), 0),
        "recv_faces": draw_recv_faces(jax.random.fold_in(seeds[10], 71), 0),
        "recv_orients": draw_recv_orients(jax.random.fold_in(seeds[10], 71), 0),
        "recv_counts": draw_recv_counts(jax.random.fold_in(seeds[10], 71), 0),
        "curve_faces": draw_curve_faces(jax.random.fold_in(seeds[10], 71), 0),
        "curve_orients": draw_curve_orients(jax.random.fold_in(seeds[10], 71), 0),
        "curve_counts": draw_curve_counts(jax.random.fold_in(seeds[10], 71), 0),
    }


time_step = 0.002
wave_speed = 1.0
highest = lax.Precision.HIGHEST
inner_nodes = [-0.8717401485096066153374457, -0.5917001814331423021445107, -0.2092992179024788687686573,
               0.2092992179024788687686573, 0.5917001814331423021445107, 0.8717401485096066153374457]


def legendre_seven(abscissa):
    before = abscissa * 0.0 + 1.0
    current = abscissa + 0.0
    for order in range(1, 7):
        before, current = current, ((2 * order + 1) * abscissa * current - order * before) / (order + 1)
    return current


def basis_tables():
    degree = 7
    points = np.array([-1.0] + inner_nodes + [1.0])
    values = legendre_seven(points)
    weights = 2.0 / (degree * (degree + 1) * values ** 2)
    deriv_mat = np.zeros((8, 8))
    for row_at in range(8):
        for col_at in range(8):
            if row_at != col_at:
                deriv_mat[row_at, col_at] = values[row_at] / (values[col_at] * (points[row_at] - points[col_at]))
    deriv_mat[0, 0] = -degree * (degree + 1) / 4.0
    deriv_mat[7, 7] = degree * (degree + 1) / 4.0
    halves = []
    projections = []
    for half_side in range(2):
        targets = (points + 2.0 * half_side - 1.0) / 2.0
        interp = np.ones((8, 8))
        for col_at in range(8):
            for other_at in range(8):
                if other_at != col_at:
                    interp[:, col_at] *= (targets - points[other_at]) / (points[col_at] - points[other_at])
        halves.append(interp)
        projections.append(0.5 * (interp.T * weights[None, :]) / weights[:, None])
    interp_mats = np.stack([np.kron(halves[first_at], halves[second_at]) for first_at in range(2) for second_at in range(2)] + [np.eye(64)])
    proj_mats = np.stack([np.kron(projections[first_at], projections[second_at]) for first_at in range(2) for second_at in range(2)] + [np.eye(64)])
    perm_table = np.zeros((8, 64), np.int32)
    for orient_code in range(8):
        for first_at in range(8):
            for second_at in range(8):
                if orient_code & 4:
                    upper_at, lower_at = second_at, first_at
                else:
                    upper_at, lower_at = first_at, second_at
                if orient_code & 1:
                    upper_at = 7 - upper_at
                if orient_code & 2:
                    lower_at = 7 - lower_at
                perm_table[orient_code, 8 * first_at + second_at] = 8 * upper_at + lower_at
    inverse_table = np.argsort(perm_table, axis=1).astype(np.int32)
    across_y = np.kron(np.eye(2), np.kron(deriv_mat, np.eye(8)))
    along_z = np.kron(np.eye(2), np.kron(np.eye(8), deriv_mat))
    lift_end = float(1.0 / weights[0])
    return (jnp.asarray(deriv_mat, jnp.float32), jnp.asarray(interp_mats, jnp.float32), jnp.asarray(proj_mats, jnp.float32),
            jnp.asarray(perm_table, jnp.int32), jnp.asarray(inverse_table, jnp.int32), lift_end,
            jnp.asarray(across_y, jnp.float32), jnp.asarray(along_z, jnp.float32))


def face_traces(current):
    fields, elements, npoints = current.shape
    cube_vals = current.reshape(fields, elements, 8, 8, 8)
    stacked = jnp.stack([cube_vals[:, :, 0], cube_vals[:, :, 7], cube_vals[:, :, :, 0], cube_vals[:, :, :, 7],
                         cube_vals[:, :, :, :, 0], cube_vals[:, :, :, :, 7]], axis=2)
    return stacked.reshape(fields, elements * 6, 64)


def spread_faces(jump_term, elements):
    fields = jump_term.shape[0]
    face_vals = jump_term.reshape(fields, elements, 6, 8, 8)
    cube_vals = jnp.zeros((fields, elements, 8, 8, 8), jnp.float32)
    cube_vals = cube_vals.at[:, :, 0].add(face_vals[:, :, 0])
    cube_vals = cube_vals.at[:, :, 7].add(face_vals[:, :, 1])
    cube_vals = cube_vals.at[:, :, :, 0].add(face_vals[:, :, 2])
    cube_vals = cube_vals.at[:, :, :, 7].add(face_vals[:, :, 3])
    cube_vals = cube_vals.at[:, :, :, :, 0].add(face_vals[:, :, 4])
    cube_vals = cube_vals.at[:, :, :, :, 7].add(face_vals[:, :, 5])
    return cube_vals.reshape(fields, elements, 512)


def dim_picks(face_ids):
    return (((face_ids % 6) // 2)[None, :] == jnp.arange(3, dtype=jnp.int32)[:, None]).astype(jnp.float32)


def normal_flux(trace_set, face_ids):
    pick_mask = dim_picks(face_ids)
    sign_vals = ((face_ids % 2) * 2 - 1).astype(jnp.float32)[:, None]
    normal_vel = jnp.sum(pick_mask[:, :, None] * trace_set[1:4], axis=0)
    pressure = sign_vals * trace_set[4]
    return jnp.stack([sign_vals * normal_vel, pick_mask[0][:, None] * pressure, pick_mask[1][:, None] * pressure,
                      pick_mask[2][:, None] * pressure, sign_vals * normal_vel])


def wall_state(own_side, face_ids):
    flip_vals = 1.0 - 2.0 * dim_picks(face_ids)
    return jnp.concatenate([own_side[:1], own_side[1:4] * flip_vals[:, :, None], own_side[4:]], axis=0)


def rusanov(own_side, other_side, face_ids):
    average = 0.5 * (normal_flux(own_side, face_ids) + normal_flux(other_side, face_ids))
    return average - 0.5 * wave_speed * (other_side - own_side)


def orient(values, orient_codes, lookup):
    matches = (orient_codes[:, None] == jnp.arange(8, dtype=jnp.int32)[None, :]).astype(jnp.int32)
    gather_index = jnp.sum(matches[:, :, None] * lookup[None, :, :], axis=1)
    return jnp.take_along_axis(values, jnp.broadcast_to(gather_index[None], values.shape), axis=2)


def child_apply(values, child_ids, matrices):
    mapped = jnp.einsum('fnj,cij->cfni', values, matrices, precision=highest)
    pick_mask = (child_ids[None, :] == jnp.arange(5, dtype=jnp.int32)[:, None]).astype(jnp.float32)
    return jnp.sum(pick_mask[:, None, :, None] * mapped, axis=0)


def volume_term(current, deriv_mat):
    fields, elements, npoints = current.shape
    cube_vals = current.reshape(fields, elements, 8, 8, 8)
    grad_x = jnp.einsum('im,femjk->feijk', deriv_mat, cube_vals[1:5:3], precision=highest).reshape(2, elements, 512)
    grad_y = jnp.einsum('jm,feimk->feijk', deriv_mat, cube_vals[2:5:2], precision=highest).reshape(2, elements, 512)
    grad_z = jnp.einsum('km,feijm->feijk', deriv_mat, cube_vals[3:5], precision=highest).reshape(2, elements, 512)
    diverge = grad_x[0] + grad_y[0] + grad_z[0]
    return -jnp.stack([diverge, grad_x[1], grad_y[1], grad_z[1], diverge])


def reference(state, levels, send_faces, send_counts, recv_faces, recv_orients, recv_counts, curve_faces, curve_orients, curve_counts):
    deriv_mat, interp_mats, proj_mats, perm_table, inverse_table, lift_end, across_y, along_z = basis_tables()
    fields, elements, npoints = state.shape
    face_total = elements * 6
    offsets = (jnp.arange(N_CURVE * N_TILE, dtype=jnp.int32) * (6 * E_DEV)).reshape(N_CURVE, N_TILE)
    scales = jnp.exp2(levels.astype(jnp.float32))
    face_scales = jnp.repeat(scales, 6) * lift_end
    slot_range = jnp.arange(CAPM, dtype=jnp.int32)
    send_grid = send_faces.reshape(N_CURVE, N_TILE, N_TILE, CAPM)
    send_live = slot_range < send_counts.reshape(N_CURVE, N_TILE, N_TILE)[..., None]
    send_ids = jnp.where(send_live, offsets[:, :, None, None] + send_grid // 5, face_total).reshape(-1).astype(jnp.int32)
    child_ids = (send_grid % 5).reshape(-1).astype(jnp.int32)
    send_mask = send_live.reshape(-1).astype(jnp.float32)[None, :, None]
    recv_grid = recv_faces.reshape(N_CURVE, N_TILE, N_TILE, CAPM)
    recv_live = slot_range < recv_counts.reshape(N_CURVE, N_TILE, N_TILE)[..., None]
    recv_ids = jnp.where(recv_live, offsets[:, :, None, None] + recv_grid, face_total).reshape(-1).astype(jnp.int32)
    recv_codes = recv_orients.reshape(-1).astype(jnp.int32)
    recv_mask = recv_live.reshape(-1).astype(jnp.float32)[None, :, None]
    rim_range = jnp.arange(CAPH, dtype=jnp.int32)
    curve_grid = curve_faces.reshape(N_CURVE, N_TILE, 2, CAPH)
    curve_live = rim_range < curve_counts.reshape(N_CURVE, N_TILE, 2)[..., None]
    curve_ids = jnp.where(curve_live, offsets[:, :, None, None] + curve_grid, face_total).reshape(-1).astype(jnp.int32)
    curve_codes = curve_orients.reshape(-1).astype(jnp.int32)
    curve_mask = curve_live.reshape(-1).astype(jnp.float32)[None, :, None]
    all_faces = jnp.arange(face_total, dtype=jnp.int32)
    slot_shape = (fields, N_CURVE, N_TILE, N_TILE, CAPM, 64)

    def rhs(current):
        traces = face_traces(current)
        padded = jnp.concatenate([traces, jnp.zeros((fields, 1, 64), jnp.float32)], axis=1)
        mortar = child_apply(padded[:, send_ids], child_ids, interp_mats) * send_mask
        arrived = jnp.transpose(mortar.reshape(slot_shape), (0, 1, 3, 2, 4, 5)).reshape(fields, -1, 64)
        fine_flux = rusanov(padded[:, recv_ids], orient(arrived, recv_codes, perm_table), recv_ids) * recv_mask
        returned = orient(fine_flux, recv_codes, inverse_table)
        coarse_flux = -jnp.transpose(returned.reshape(slot_shape), (0, 1, 3, 2, 4, 5)).reshape(fields, -1, 64) * send_mask
        own_curve = padded[:, curve_ids].reshape(fields, N_CURVE, N_TILE, 2, CAPH, 64)
        empty_rim = jnp.zeros((fields, 1, N_TILE, CAPH, 64), jnp.float32)
        from_left = jnp.concatenate([empty_rim, own_curve[:, :-1, :, 1]], axis=1)
        from_right = jnp.concatenate([own_curve[:, 1:, :, 0], empty_rim], axis=1)
        neighbours = jnp.stack([from_left, from_right], axis=3).reshape(fields, -1, 64)
        curve_flux = rusanov(own_curve.reshape(fields, -1, 64), orient(neighbours, curve_codes, perm_table), curve_ids) * curve_mask
        accumulated = jnp.zeros((fields, face_total + 1, 64), jnp.float32)
        accumulated = accumulated.at[:, send_ids].add(child_apply(coarse_flux, child_ids, proj_mats))
        accumulated = accumulated.at[:, recv_ids].add(fine_flux)
        accumulated = accumulated.at[:, curve_ids].add(curve_flux)
        listed = jnp.zeros((face_total + 1,), jnp.float32)
        listed = listed.at[send_ids].add(1.0).at[recv_ids].add(1.0).at[curve_ids].add(1.0)
        wall_flux = rusanov(traces, wall_state(traces, all_faces), all_faces)
        flux_star = jnp.where(listed[None, :face_total, None] > 0.0, accumulated[:, :face_total], wall_flux)
        jump_term = (normal_flux(traces, all_faces) - flux_star) * face_scales[None, :, None]
        return volume_term(current, deriv_mat) * scales[None, :, None] + spread_faces(jump_term, elements)

    section_one = state + time_step * rhs(state)
    section_two = 0.75 * state + 0.25 * (section_one + time_step * rhs(section_one))
    return state / 3.0 + (2.0 / 3.0) * (section_two + time_step * rhs(section_two))
```

```python
import functools

import jax
import jax.numpy as jnp
import ml_dtypes
import numpy as np
from jax import lax
from jax.experimental import pallas as pl
from jax.experimental.pallas import tpu as pltpu
from jax.sharding import PartitionSpec as P

time_step = 0.002
half_type = jnp.bfloat16
MESH = pl.DeviceIdType.MESH
inner_nodes = [
    -0.8717401485096066,
    -0.5917001814331423,
    -0.20929921790247888,
    0.20929921790247888,
    0.5917001814331423,
    0.8717401485096066,
]


def legendre_seven(abscissa):
    before = abscissa * 0.0 + 1.0
    current = abscissa + 0.0
    for order in range(1, 7):
        before, current = (
            current,
            ((2 * order + 1) * abscissa * current - order * before) / (order + 1),
        )
    return current


def two_parts(matrix):
    high = matrix.astype(ml_dtypes.bfloat16)
    low = (matrix - high.astype(np.float64)).astype(ml_dtypes.bfloat16)
    return high, low


def tables():
    points = np.array([-1.0] + inner_nodes + [1.0])
    values = legendre_seven(points)
    weights = 2.0 / (56 * values**2)
    deriv = np.zeros((8, 8))
    for row in range(8):
        for col in range(8):
            if row != col:
                deriv[row, col] = values[row] / (values[col] * (points[row] - points[col]))
    deriv[0, 0] = -14.0
    deriv[7, 7] = 14.0
    halves = []
    projections = []
    for side in range(2):
        targets = (points + 2.0 * side - 1.0) / 2.0
        interp = np.ones((8, 8))
        for col in range(8):
            for other in range(8):
                if other != col:
                    interp[:, col] *= (targets - points[other]) / (points[col] - points[other])
        halves.append(interp)
        projections.append(0.5 * (interp.T * weights[None, :]) / weights[:, None])
    pairs = [(a, b) for a in range(2) for b in range(2)]
    mortar = [np.kron(halves[a], halves[b]) for a, b in pairs]
    project = [np.kron(projections[a], projections[b]) for a, b in pairs]
    turn = np.zeros((8, 64, 64))
    for code in range(8):
        for s in range(8):
            for t in range(8):
                a, c = (t, s) if code & 4 else (s, t)
                a = 7 - a if code & 1 else a
                c = 7 - c if code & 2 else c
                turn[code, 8 * s + t, 8 * a + c] = 1.0
    eye = np.eye(64)
    send = mortar + [eye] + [turn[o].T for o in range(8)] + [np.zeros((64, 64))]
    send += [0.25 * eye - q @ m for q, m in zip(project, mortar)]
    take = [turn[o] for o in range(8)] + project + [eye, np.zeros((64, 64))]

    def stacked(mats):
        wide = np.concatenate([m.T for m in mats], axis=1)
        high, low = two_parts(wide)
        return np.concatenate([high, high, low, np.zeros_like(low)], axis=0)

    pick = np.zeros((512, 256))
    for s in range(8):
        for t in range(8):
            column = 8 * s + t
            pick[64 * s + t, column] = 1.0
            pick[64 * s + 8 * t, 64 + column] = 1.0
            pick[64 * s + 56 + t, 128 + column] = 1.0
            pick[64 * s + 8 * t + 7, 192 + column] = 1.0
    along_x = np.concatenate(two_parts(np.kron(deriv.T, np.eye(64))), axis=0)
    along_y = np.concatenate(two_parts(np.kron(np.eye(4), np.kron(deriv.T, np.eye(8)))), axis=0)
    along_z = np.concatenate(two_parts(np.kron(np.eye(32), deriv.T)), axis=0)
    return [
        jnp.asarray(m.astype(ml_dtypes.bfloat16))
        for m in (
            pick,
            pick.T,
            stacked(send),
            stacked(take),
            along_x,
            along_y,
            along_z,
        )
    ]


def dot(left, right):
    return jnp.dot(left, right, preferred_element_type=jnp.float32)


def split(value):
    high = value.astype(half_type)
    return high, (value - high.astype(jnp.float32)).astype(half_type)


def div_five(value):
    return (value * 52429) >> 18


def div_six(value):
    return (value * 43691) >> 18


def swap_halves(value):
    return pltpu.roll(value, 64, axis=1)


def section_kernel(
    sizes,
    state_ref,
    levels_ref,
    send_faces_ref,
    send_counts_ref,
    recv_faces_ref,
    recv_orients_ref,
    recv_counts_ref,
    curve_faces_ref,
    curve_orients_ref,
    curve_counts_ref,
    pick_ref,
    spread_ref,
    send_mat_ref,
    take_mat_ref,
    along_x_ref,
    along_y_ref,
    along_z_ref,
    out_ref,
    tile_out,
    tile_in,
    curve_out,
    curve_in,
    tile_send_sem,
    tile_recv_sem,
    curve_send_sem,
    curve_recv_sem,
):
    curves, tiles, elements, cap_tile, cap_curve, half_rows = sizes
    block = 2 * half_rows
    tile_rows = tiles * block
    curve_rows = 2 * cap_curve
    b = lax.axis_index("curve")
    t = lax.axis_index("tile")
    to_peer = [lax.rem(t + off, tiles) for off in range(tiles)]
    from_peer = [lax.rem(t + tiles - off, tiles) for off in range(tiles)]
    has_prev = b > 0
    has_next = b < curves - 1

    barrier = pltpu.get_barrier_semaphore()
    for off in range(1, tiles):
        pl.semaphore_signal(barrier, inc=1, device_id=(b, to_peer[off]), device_id_type=MESH)

    @pl.when(has_prev)
    def _():
        pl.semaphore_signal(barrier, inc=1, device_id=(b - 1, t), device_id_type=MESH)

    @pl.when(has_next)
    def _():
        pl.semaphore_signal(barrier, inc=1, device_id=(b + 1, t), device_id_type=MESH)

    @pl.when(jnp.logical_not(has_prev))
    def _():
        curve_in[:, 0] = jnp.zeros_like(curve_in[:, 0])

    @pl.when(jnp.logical_not(has_next))
    def _():
        curve_in[:, 1] = jnp.zeros_like(curve_in[:, 1])

    def send_key(peer, slot):
        if slot >= cap_tile:
            return jnp.int32(-1)
        return jnp.where(slot < send_counts_ref[peer], send_faces_ref[peer, slot] * 16, -1)

    def recv_key(peer, slot):
        if slot >= cap_tile:
            return jnp.int32(-1)
        value = recv_faces_ref[peer, slot] * 16 + recv_orients_ref[peer, slot]
        return jnp.where(slot < recv_counts_ref[peer], value, -1)

    def curve_key(side, slot):
        value = curve_faces_ref[side, slot] * 16 + curve_orients_ref[side, slot]
        return jnp.where(slot < curve_counts_ref[side], value, -1)

    out_keys = []
    in_keys = []
    for off in range(tiles):
        out_keys += [send_key(to_peer[off], slot) for slot in range(half_rows)]
        out_keys += [recv_key(to_peer[off], slot) for slot in range(half_rows)]
        in_keys += [recv_key(from_peer[off], slot) for slot in range(half_rows)]
        in_keys += [send_key(from_peer[off], slot) for slot in range(half_rows)]
    rim_keys = [curve_key(side, slot) for side in range(2) for slot in range(cap_curve)]

    sub_iota = lax.broadcasted_iota(jnp.int32, (8, 128), 0)

    def down_rows(keys):
        blocks = []
        for start in range(0, len(keys), 8):
            value = jnp.full((8, 128), -1, jnp.int32)
            for at in range(8):
                value = jnp.where(sub_iota == at, keys[start + at], value)
            blocks.append(value)
        return jnp.concatenate(blocks, axis=0)

    def along_lanes(keys):
        lane = lax.broadcasted_iota(jnp.int32, (8, len(keys)), 1)
        value = jnp.full((8, len(keys)), -1, jnp.int32)
        for at, key in enumerate(keys):
            value = jnp.where(lane == at, key, value)
        return jnp.concatenate([value] * (elements // 8), axis=0)

    def decode(keys, from_send):
        live = keys >= 0
        raw = jnp.maximum(keys, 0) >> 4
        turned = jnp.maximum(keys, 0) & 15
        face_id = jnp.where(from_send, div_five(raw), raw)
        child = raw - 5 * face_id
        element = div_six(face_id)
        face = face_id - 6 * element
        return jnp.where(live, element, -1), face, child, turned

    def half_flags(shape, axis, first):
        at = lax.broadcasted_iota(jnp.int32, shape, axis)
        return (at & (block - 1)) < half_rows if first else (at & (block - 1)) >= half_rows

    lane_t = lax.broadcasted_iota(jnp.int32, (tile_rows, 128), 1)
    low_t = lane_t < 64
    out_is_send = half_flags((tile_rows, 128), 0, True)
    in_is_send = half_flags((tile_rows, 128), 0, False)
    out_elem, out_face, out_child, out_turn = decode(down_rows(out_keys), out_is_send)
    in_elem, in_face, in_child, in_turn = decode(down_rows(in_keys), in_is_send)
    out_y = out_face < 4
    in_y = in_face < 4
    out_code = jnp.where(out_is_send, out_child, 5 + out_turn)
    in_code = jnp.where(in_is_send, 8 + in_child, in_turn)
    upper_t = jnp.where(low_t, 0, 1)
    out_masks = [jnp.where(out_code == 2 * j + upper_t, 1.0, 0.0) for j in range(7)]
    extra_masks = [
        jnp.where(jnp.logical_and(out_is_send, out_code == 2 * j + upper_t), 1.0, 0.0)
        for j in range(2)
    ]
    out_sign = jnp.where(out_is_send, -1.0, 1.0)
    in_sign_half = jnp.where(in_is_send, 0.5, -0.5)
    out_match = low_t == out_y
    in_match = low_t == in_y
    in_low_faces = jnp.where(jnp.logical_and(in_match, jnp.logical_not(in_is_send)), 1.0, 0.0)
    in_high_faces = jnp.where(jnp.logical_and(in_match, in_is_send), 1.0, 0.0)
    out_high_faces = jnp.where(jnp.logical_and(out_match, out_is_send), 1.0, 0.0)

    rim_row = lax.broadcasted_iota(jnp.int32, (curve_rows, 128), 0)
    lane_c = lax.broadcasted_iota(jnp.int32, (curve_rows, 128), 1)
    low_c = lane_c < 64
    rim_elem, _, _, rim_turn = decode(down_rows(rim_keys), rim_row < 0)
    rim_first = rim_row < cap_curve
    rim_match = low_c == rim_first
    rim_sign = jnp.where(rim_first, 1.0, -1.0)
    both_codes = jnp.concatenate([in_code, rim_turn], axis=0)
    upper_b = jnp.where(lax.broadcasted_iota(jnp.int32, both_codes.shape, 1) < 64, 0, 1)
    both_masks = [jnp.where(both_codes == 2 * j + upper_b, 1.0, 0.0) for j in range(7)]
    rim_place = jnp.where(rim_match, 1.0, 0.0)

    def one_hot(flags):
        return jnp.where(flags, 1.0, 0.0).astype(half_type)

    gather_lane = lax.broadcasted_iota(jnp.int32, (tile_rows, 2 * elements), 1) % elements
    out_gather = one_hot(gather_lane == out_elem[:, : 2 * elements])
    rim_lane = lax.broadcasted_iota(jnp.int32, (curve_rows, 2 * elements), 1) % elements
    rim_gather = one_hot(rim_lane == rim_elem[:, : 2 * elements])

    lane_shape = (elements, 4 * tile_rows)
    lane_s = lax.broadcasted_iota(jnp.int32, lane_shape, 1)
    in_part = lane_s < 2 * tile_rows
    first_half = (lane_s & (block - 1)) < half_rows
    lane_from_send = first_half != in_part
    t_elem, t_face, _, _ = decode(along_lanes(in_keys * 2 + out_keys * 2), lane_from_send)
    t_hit = t_elem == lax.broadcasted_iota(jnp.int32, lane_shape, 0)
    tile_scatter = one_hot(t_hit)
    rim_shape = (elements, 2 * curve_rows)
    c_elem, c_face, _, _ = decode(
        along_lanes(rim_keys * 2), lax.broadcasted_iota(jnp.int32, rim_shape, 1) < 0
    )
    c_hit = c_elem == lax.broadcasted_iota(jnp.int32, rim_shape, 0)
    rim_scatter = one_hot(c_hit)

    def any_lane(flags):
        return jnp.max(jnp.where(flags, 1.0, 0.0), axis=1, keepdims=True)

    listed = [any_lane(jnp.logical_and(c_hit, c_face == f)) for f in (0, 1)]
    listed += [any_lane(jnp.logical_and(t_hit, t_face == f)) for f in (2, 3, 4, 5)]

    scale_blocks = []
    for start in range(0, elements, 8):
        value = jnp.zeros((8, 128), jnp.int32)
        for at in range(8):
            value = jnp.where(sub_iota == at, jnp.int32(1) << levels_ref[start + at], value)
        scale_blocks.append(value.astype(jnp.float32))
    scale = jnp.concatenate(scale_blocks, axis=0)
    scale = jnp.concatenate([scale] * 4, axis=1)
    vol_scale = scale * (-time_step)
    lift = scale * (28.0 * time_step)

    node = lax.broadcasted_iota(jnp.int32, (elements, 512), 1)
    vel_to_sum = []
    pres_to_vel = []
    own_damp = []
    side_damp = []
    for dim in range(3):
        place = (node >> (6 - 3 * dim)) & 7
        low_end = place == 0
        high_end = place == 7
        on_face = jnp.logical_or(low_end, high_end)
        known = jnp.where(low_end, listed[2 * dim], listed[2 * dim + 1])
        strong = jnp.where(on_face, lift * (1.0 - 0.5 * known), 0.0)
        weak = jnp.where(on_face, lift * (0.5 * known), 0.0)
        vel_to_sum.append(jnp.where(low_end, -strong, strong))
        pres_to_vel.append(jnp.where(low_end, -weak, weak))
        own_damp.append(strong)
        side_damp.append(weak)
    total_damp = side_damp[0] + side_damp[1] + side_damp[2]
    vel_damp = [own_damp[d] + (total_damp - side_damp[d]) for d in range(3)]

    def tile_copies(stage):
        return [
            pltpu.make_async_remote_copy(
                src_ref=tile_out.at[stage, off],
                dst_ref=tile_in.at[stage, off],
                send_sem=tile_send_sem.at[stage, off],
                recv_sem=tile_recv_sem.at[stage, off],
                device_id=(b, to_peer[off]),
                device_id_type=MESH,
            )
            for off in range(1, tiles)
        ]

    def curve_copy(stage, side):
        return pltpu.make_async_remote_copy(
            src_ref=curve_out.at[stage, side],
            dst_ref=curve_in.at[stage, 1 - side],
            send_sem=curve_send_sem.at[stage, side],
            recv_sem=curve_recv_sem.at[stage, 1 - side],
            device_id=(b - 1 + 2 * side, t),
            device_id_type=MESH,
        )

    def packed(first, second, low):
        return jnp.where(low, first, second)

    def pair_rows(value, low):
        high = value.astype(half_type).astype(jnp.float32)
        return jnp.concatenate([jnp.where(low, high, value - high), high], axis=1).astype(half_type)

    def rates(current, stage):
        parts = [split(value) for value in current]
        highs = [part[0] for part in parts]
        lows = [part[1] for part in parts]

        low_e = lax.broadcasted_iota(jnp.int32, (elements, 128), 1) < 64
        ends = [split(jnp.where(low_e, v[:, :128], v[:, 384:])) for v in current]
        ends = jnp.concatenate([jnp.concatenate(e, axis=0) for e in ends], axis=1)
        rim = dot(rim_gather, ends)
        rim_vals = []
        for f in range(5):
            kept = jnp.where(rim_match, rim[:, 128 * f : 128 * f + 128], 0.0)
            rim_vals.append(kept + swap_halves(kept))
        sum_part = rim_sign * rim_vals[1] - rim_vals[0]
        vel_part = rim_sign * rim_vals[4] - rim_vals[1]
        rim_send = jnp.concatenate(
            [packed(sum_part, vel_part, low_c), packed(rim_vals[2], rim_vals[3], low_c)], axis=1
        )
        curve_out[stage] = rim_send.reshape(2, cap_curve, 256)
        if stage == 0:
            pl.semaphore_wait(
                barrier, tiles - 1 + has_prev.astype(jnp.int32) + has_next.astype(jnp.int32)
            )

        @pl.when(has_prev)
        def _():
            curve_copy(stage, 0).start()

        @pl.when(has_next)
        def _():
            curve_copy(stage, 1).start()

        traces = dot(jnp.concatenate(highs + lows, axis=0), pick_ref[...]).astype(half_type)
        columns = []
        for f in range(5):
            at = f * elements
            low_at = (5 + f) * elements
            columns.append(
                jnp.concatenate(
                    [traces[at : at + elements], traces[low_at : low_at + elements]], axis=0
                )
            )
        own = dot(out_gather, jnp.concatenate(columns, axis=1))
        own_rows = []
        for f in range(5):
            side = jnp.where(
                out_is_send, own[:, 256 * f + 128 : 256 * f + 256], own[:, 256 * f : 256 * f + 128]
            )
            kept = jnp.where(out_match, side, 0.0)
            own_rows.append(pair_rows(kept + swap_halves(kept), low_t))
        coded = dot(jnp.concatenate(own_rows, axis=0), send_mat_ref[...])

        def choose(source, rows_at, rows, masks, first):
            total = None
            for j, mask in enumerate(masks):
                at = 128 * (first + j)
                term = mask * source[rows_at : rows_at + rows, at : at + 128]
                total = term if total is None else total + term
            return total + swap_halves(total)

        mortar = [choose(coded, f * tile_rows, tile_rows, out_masks, 0) for f in range(5)]
        normal = jnp.where(out_y, mortar[2], mortar[3])
        other = jnp.where(out_y, mortar[3], mortar[2])
        sum_part = out_sign * normal - mortar[0]
        vel_part = out_sign * mortar[4] - normal
        tile_send = jnp.concatenate(
            [packed(sum_part, vel_part, low_t), packed(mortar[1], other, low_t)], axis=1
        )
        tile_send = tile_send.reshape(tiles, block, 256)
        tile_out[stage] = tile_send
        tile_in[stage, 0] = tile_send[0]
        copies = tile_copies(stage)
        for copy in copies:
            copy.start()

        rest = [choose(coded, f * tile_rows, tile_rows, extra_masks, 7) for f in range(5)]
        rest_n = jnp.where(out_y, rest[2], rest[3])
        rest_o = jnp.where(out_y, rest[3], rest[2])
        rest_p = 0.5 * (rest[4] + rest_n)
        rest_n = 0.5 * (rest_n + rest[4])
        rest_o = 0.5 * rest_o
        rest_fields = [
            0.5 * (rest[0] + jnp.where(out_y, rest[2], rest[3])),
            0.5 * rest[1],
            jnp.where(out_y, rest_n, rest_o),
            jnp.where(out_y, rest_o, rest_n),
            rest_p,
        ]
        rest_parts = [split(value * out_high_faces) for value in rest_fields]

        grad = dot(
            jnp.concatenate([highs[1], highs[4], lows[1], lows[4]], axis=0), along_x_ref[:512]
        )
        n2 = 2 * elements
        grad_x = grad[:n2] + grad[n2:]
        grad_x = grad_x + dot(jnp.concatenate([highs[1], highs[4]], axis=0), along_x_ref[512:])

        def halves(f, source):
            return [source[f][:, :256], source[f][:, 256:]]

        def banded(f, mat_ref):
            high_rows = jnp.concatenate(halves(f, highs) + halves(4, highs), axis=0)
            low_rows = jnp.concatenate(halves(f, lows) + halves(4, lows), axis=0)
            first = dot(jnp.concatenate([high_rows, low_rows], axis=0), mat_ref[:256])
            n4 = 4 * elements
            total = first[:n4] + first[n4:] + dot(high_rows, mat_ref[256:])
            vel = jnp.concatenate([total[:elements], total[elements:n2]], axis=1)
            pres = jnp.concatenate([total[n2 : 3 * elements], total[3 * elements :]], axis=1)
            return vel, pres

        vel_y, pres_y = banded(2, along_y_ref)
        vel_z, pres_z = banded(3, along_z_ref)
        diverge = vol_scale * (grad_x[:elements] + vel_y + vel_z)
        to_sum = diverge
        for d in range(3):
            to_sum = to_sum + vel_to_sum[d] * current[1 + d]
        pres_grads = (grad_x[elements:], pres_y, pres_z)
        result = [to_sum - total_damp * current[0]]
        for d in range(3):
            result.append(
                vol_scale * pres_grads[d]
                + pres_to_vel[d] * current[4]
                - vel_damp[d] * current[1 + d]
            )
        result.append(to_sum - total_damp * current[4])

        for copy in copies:
            copy.wait()

        @pl.when(has_prev)
        def _():
            copy = curve_copy(stage, 0)
            copy.wait_send()
            curve_copy(stage, 1).wait_recv()

        @pl.when(has_next)
        def _():
            copy = curve_copy(stage, 1)
            copy.wait_send()
            curve_copy(stage, 0).wait_recv()

        arrived = jnp.concatenate(
            [
                tile_in[stage].reshape(tile_rows, 256),
                curve_in[stage].reshape(curve_rows, 256),
            ],
            axis=0,
        )
        rows = tile_rows + curve_rows
        low_b = lax.broadcasted_iota(jnp.int32, (rows, 128), 1) < 64
        fields = []
        for at in range(2):
            value = arrived[:, 128 * at : 128 * at + 128]
            turned = swap_halves(value)
            fields.append(pair_rows(jnp.where(low_b, value, turned), low_b))
            fields.append(pair_rows(jnp.where(low_b, turned, value), low_b))
        taken = dot(jnp.concatenate(fields, axis=0), take_mat_ref[...])
        chosen = [choose(taken, f * rows, rows, both_masks, 0) for f in range(4)]

        rim_in = [value[tile_rows:] * rim_place for value in chosen]
        rim_cols = [jnp.concatenate(split(value), axis=0) for value in rim_in]
        placed = dot(rim_scatter, jnp.concatenate(rim_cols, axis=1))
        place_sum = -0.5 * placed[:, :128]
        place_vel = -0.5 * placed[:, 128:256]
        place_pres = jnp.where(low_e, place_vel, -place_vel)
        rim_fields = [
            place_sum,
            place_vel,
            0.5 * placed[:, 256:384],
            0.5 * placed[:, 384:512],
            place_pres,
        ]

        tile_vals = [value[:tile_rows] for value in chosen]
        put_sum = -0.5 * tile_vals[0]
        put_n = -0.5 * tile_vals[1]
        put_o = 0.5 * tile_vals[3]
        put = [
            put_sum,
            0.5 * tile_vals[2],
            jnp.where(in_y, put_n, put_o),
            jnp.where(in_y, put_o, put_n),
            in_sign_half * tile_vals[1],
        ]
        zero_part = jnp.zeros((tile_rows, 128), half_type)
        columns = []
        for f in range(5):
            first = split(put[f] * in_low_faces)
            second = split(put[f] * in_high_faces)
            high, low = rest_parts[f]
            columns.append(jnp.concatenate([first[0], first[1], zero_part, zero_part], axis=0))
            columns.append(jnp.concatenate([second[0], second[1], high, low], axis=0))
        on_faces = dot(tile_scatter, jnp.concatenate(columns, axis=1))
        face_parts = [split(on_faces[:, 256 * f : 256 * f + 256]) for f in range(5)]
        spread = dot(
            jnp.concatenate([p[0] for p in face_parts] + [p[1] for p in face_parts], axis=0),
            spread_ref[...],
        )
        finished = []
        zero_middle = jnp.zeros((elements, 256), jnp.float32)
        for f in range(5):
            at = f * elements
            low_at = (5 + f) * elements
            nodes = spread[at : at + elements] + spread[low_at : low_at + elements]
            rim_nodes = jnp.concatenate(
                [
                    jnp.where(low_e, rim_fields[f], 0.0),
                    zero_middle,
                    jnp.where(low_e, 0.0, rim_fields[f]),
                ],
                axis=1,
            )
            finished.append(result[f] + lift * (nodes + rim_nodes))
        return finished

    current = [state_ref[f] for f in range(5)]
    change = rates(current, 0)
    current = [current[f] + change[f] for f in range(5)]
    change = rates(current, 1)
    current = [0.75 * state_ref[f] + 0.25 * (current[f] + change[f]) for f in range(5)]
    change = rates(current, 2)
    for f in range(5):
        out_ref[f] = state_ref[f] / 3.0 + (2.0 / 3.0) * (current[f] + change[f])


def shards(
    state,
    levels,
    send_faces,
    send_counts,
    recv_faces,
    recv_orients,
    recv_counts,
    curve_faces,
    curve_orients,
    curve_counts,
):
    curves = lax.axis_size("curve")
    tiles, cap_tile = send_faces.shape
    cap_curve = curve_faces.shape[1]
    elements = state.shape[1]
    half_rows = -(-cap_tile // 4) * 4
    sizes = (curves, tiles, elements, cap_tile, cap_curve, half_rows)
    smem = pl.BlockSpec(memory_space=pltpu.SMEM)
    vmem = pl.BlockSpec(memory_space=pltpu.VMEM)
    block = 2 * half_rows
    return pl.pallas_call(
        functools.partial(section_kernel, sizes),
        out_shape=jax.ShapeDtypeStruct(state.shape, state.dtype),
        in_specs=[vmem] + [smem] * 9 + [vmem] * 7,
        out_specs=vmem,
        scratch_shapes=[
            pltpu.VMEM((3, tiles, block, 256), jnp.float32),
            pltpu.VMEM((3, tiles, block, 256), jnp.float32),
            pltpu.VMEM((3, 2, cap_curve, 256), jnp.float32),
            pltpu.VMEM((3, 2, cap_curve, 256), jnp.float32),
            pltpu.SemaphoreType.DMA((3, tiles)),
            pltpu.SemaphoreType.DMA((3, tiles)),
            pltpu.SemaphoreType.DMA((3, 2)),
            pltpu.SemaphoreType.DMA((3, 2)),
        ],
        compiler_params=pltpu.CompilerParams(
            collective_id=0, has_side_effects=True, vmem_limit_bytes=40 * 1024 * 1024
        ),
    )(
        state,
        levels,
        send_faces,
        send_counts,
        recv_faces,
        recv_orients,
        recv_counts,
        curve_faces,
        curve_orients,
        curve_counts,
        *tables(),
    )


def solution(mesh):
    return jax.shard_map(
        shards,
        mesh=mesh,
        in_specs=(
            P(None, ("curve", "tile"), None),
            P(("curve", "tile")),
            P(("curve", "tile"), None),
            P(("curve", "tile")),
            P(("curve", "tile"), None),
            P(("curve", "tile"), None),
            P(("curve", "tile")),
            P(("curve", "tile"), None),
            P(("curve", "tile"), None),
            P(("curve", "tile")),
        ),
        out_specs=P(None, ("curve", "tile"), None),
        check_vma=False,
    )
```

```python
import functools

import jax
import jax.numpy as jnp
import ml_dtypes
import numpy as np
from jax import lax
from jax.experimental import pallas as pl
from jax.experimental.pallas import tpu as pltpu
from jax.sharding import PartitionSpec as P

time_step = 0.002
half_type = jnp.bfloat16
MESH = pl.DeviceIdType.MESH
operand_count = 17
load_order = [3, 2, 5, 4, 6, 8, 7, 9, 1, 0, 10, 12, 14, 15, 16, 13, 11]
inner_nodes = [
    -0.8717401485096066,
    -0.5917001814331423,
    -0.20929921790247888,
    0.20929921790247888,
    0.5917001814331423,
    0.8717401485096066,
]


def legendre_seven(abscissa):
    before = abscissa * 0.0 + 1.0
    current = abscissa + 0.0
    for order in range(1, 7):
        before, current = (
            current,
            ((2 * order + 1) * abscissa * current - order * before) / (order + 1),
        )
    return current


def tables():
    points = np.array([-1.0] + inner_nodes + [1.0])
    values = legendre_seven(points)
    weights = 2.0 / (56 * values**2)
    deriv = np.zeros((8, 8))
    for row in range(8):
        for col in range(8):
            if row != col:
                deriv[row, col] = values[row] / (values[col] * (points[row] - points[col]))
    deriv[0, 0] = -14.0
    deriv[7, 7] = 14.0
    halves = []
    projections = []
    for side in range(2):
        targets = (points + 2.0 * side - 1.0) / 2.0
        interp = np.ones((8, 8))
        for col in range(8):
            for other in range(8):
                if other != col:
                    interp[:, col] *= (targets - points[other]) / (points[col] - points[other])
        halves.append(interp)
        projections.append(0.5 * (interp.T * weights[None, :]) / weights[:, None])
    pairs = [(a, b) for a in range(2) for b in range(2)]
    mortar = [np.kron(halves[a], halves[b]) for a, b in pairs]
    project = [np.kron(projections[a], projections[b]) for a, b in pairs]
    turn = np.zeros((8, 64, 64))
    for code in range(8):
        for s in range(8):
            for t in range(8):
                a, c = (t, s) if code & 4 else (s, t)
                a = 7 - a if code & 1 else a
                c = 7 - c if code & 2 else c
                turn[code, 8 * s + t, 8 * a + c] = 1.0
    eye = np.eye(64)
    send = mortar + [eye] + [turn[o].T for o in range(8)] + [np.zeros((64, 64))]
    send += [0.25 * eye - q @ m for q, m in zip(project, mortar)]
    take = [turn[o] for o in range(8)] + project + [eye, np.zeros((64, 64))]

    pick = np.zeros((512, 256))
    for s in range(8):
        for t in range(8):
            column = 8 * s + t
            pick[64 * s + t, column] = 1.0
            pick[64 * s + 8 * t, 64 + column] = 1.0
            pick[64 * s + 56 + t, 128 + column] = 1.0
            pick[64 * s + 8 * t + 7, 192 + column] = 1.0
    return [
        jnp.asarray(m.astype(np.float32))
        for m in (
            pick,
            pick.T,
            np.concatenate([m.T for m in send], axis=1),
            np.concatenate([m.T for m in take], axis=1),
            np.kron(deriv.T, np.eye(64)),
            np.kron(np.eye(4), np.kron(deriv.T, np.eye(8))),
            np.kron(np.eye(32), deriv.T),
        )
    ]


def dot(left, right):
    return jnp.dot(left, right, preferred_element_type=jnp.float32)


def split(value):
    high = value.astype(half_type)
    return high, (value - high.astype(jnp.float32)).astype(half_type)


def div_five(value):
    return (value * 52429) >> 18


def div_six(value):
    return (value * 43691) >> 18


def swap_halves(value):
    return pltpu.roll(value, 64, axis=1)


def section_kernel(
    sizes,
    *refs,
):
    given = refs[:operand_count]
    out_ref = refs[operand_count]
    held = refs[operand_count + 1 : 2 * operand_count + 1]
    (
        tile_out,
        tile_in,
        curve_out,
        curve_in,
        tile_send_sem,
        tile_recv_sem,
        curve_send_sem,
        curve_recv_sem,
        load_sem,
        *ready,
    ) = refs[2 * operand_count + 1 :]
    pick_ref, spread_ref, send_mat_ref, take_mat_ref, along_x_ref, along_y_ref, along_z_ref = ready
    (
        state_ref,
        levels_ref,
        send_faces_ref,
        send_counts_ref,
        recv_faces_ref,
        recv_orients_ref,
        recv_counts_ref,
        curve_faces_ref,
        curve_orients_ref,
        curve_counts_ref,
        *wide,
    ) = held
    loads = [
        pltpu.make_async_copy(source, target, load_sem.at[at])
        for at, (source, target) in enumerate(zip(given, held))
    ]
    for at in load_order:
        loads[at].start()
    curves, tiles, elements, cap_tile, cap_curve, half_rows = sizes
    block = 2 * half_rows
    tile_rows = tiles * block
    curve_rows = 2 * cap_curve
    b = lax.axis_index("curve")
    t = lax.axis_index("tile")
    to_peer = [lax.rem(t + off, tiles) for off in range(tiles)]
    from_peer = [lax.rem(t + tiles - off, tiles) for off in range(tiles)]
    has_prev = b > 0
    has_next = b < curves - 1

    barrier = pltpu.get_barrier_semaphore()
    for off in range(1, tiles):
        pl.semaphore_signal(barrier, inc=1, device_id=(b, to_peer[off]), device_id_type=MESH)

    @pl.when(has_prev)
    def _():
        pl.semaphore_signal(barrier, inc=1, device_id=(b - 1, t), device_id_type=MESH)

    @pl.when(has_next)
    def _():
        pl.semaphore_signal(barrier, inc=1, device_id=(b + 1, t), device_id_type=MESH)

    @pl.when(jnp.logical_not(has_prev))
    def _():
        curve_in[:, 0] = jnp.zeros_like(curve_in[:, 0])

    @pl.when(jnp.logical_not(has_next))
    def _():
        curve_in[:, 1] = jnp.zeros_like(curve_in[:, 1])

    for at in range(1, 10):
        loads[at].wait()

    def send_key(peer, slot):
        if slot >= cap_tile:
            return jnp.int32(-1)
        return jnp.where(slot < send_counts_ref[peer], send_faces_ref[peer, slot] * 16, -1)

    def recv_key(peer, slot):
        if slot >= cap_tile:
            return jnp.int32(-1)
        value = recv_faces_ref[peer, slot] * 16 + recv_orients_ref[peer, slot]
        return jnp.where(slot < recv_counts_ref[peer], value, -1)

    def curve_key(side, slot):
        value = curve_faces_ref[side, slot] * 16 + curve_orients_ref[side, slot]
        return jnp.where(slot < curve_counts_ref[side], value, -1)

    out_keys = []
    in_keys = []
    for off in range(tiles):
        out_keys += [send_key(to_peer[off], slot) for slot in range(half_rows)]
        out_keys += [recv_key(to_peer[off], slot) for slot in range(half_rows)]
        in_keys += [recv_key(from_peer[off], slot) for slot in range(half_rows)]
        in_keys += [send_key(from_peer[off], slot) for slot in range(half_rows)]
    rim_keys = [curve_key(side, slot) for side in range(2) for slot in range(cap_curve)]

    sub_iota = lax.broadcasted_iota(jnp.int32, (8, 128), 0)

    def down_rows(keys):
        blocks = []
        for start in range(0, len(keys), 8):
            value = jnp.full((8, 128), -1, jnp.int32)
            for at in range(8):
                value = jnp.where(sub_iota == at, keys[start + at], value)
            blocks.append(value)
        return jnp.concatenate(blocks, axis=0)

    def along_lanes(keys):
        lane = lax.broadcasted_iota(jnp.int32, (8, len(keys)), 1)
        value = jnp.full((8, len(keys)), -1, jnp.int32)
        for at, key in enumerate(keys):
            value = jnp.where(lane == at, key, value)
        return jnp.concatenate([value] * (elements // 8), axis=0)

    def decode(keys, from_send):
        live = keys >= 0
        raw = jnp.maximum(keys, 0) >> 4
        turned = jnp.maximum(keys, 0) & 15
        face_id = jnp.where(from_send, div_five(raw), raw)
        child = raw - 5 * face_id
        element = div_six(face_id)
        face = face_id - 6 * element
        return jnp.where(live, element, -1), face, child, turned

    def half_flags(shape, axis, first):
        at = lax.broadcasted_iota(jnp.int32, shape, axis)
        return (at & (block - 1)) < half_rows if first else (at & (block - 1)) >= half_rows

    lane_t = lax.broadcasted_iota(jnp.int32, (tile_rows, 128), 1)
    low_t = lane_t < 64
    out_is_send = half_flags((tile_rows, 128), 0, True)
    in_is_send = half_flags((tile_rows, 128), 0, False)
    out_elem, out_face, out_child, out_turn = decode(down_rows(out_keys), out_is_send)
    in_elem, in_face, in_child, in_turn = decode(down_rows(in_keys), in_is_send)
    out_y = out_face < 4
    in_y = in_face < 4
    out_code = jnp.where(out_is_send, out_child, 5 + out_turn)
    in_code = jnp.where(in_is_send, 8 + in_child, in_turn)
    upper_t = jnp.where(low_t, 0, 1)
    out_masks = [jnp.where(out_code == 2 * j + upper_t, 1.0, 0.0) for j in range(7)]
    extra_masks = [
        jnp.where(jnp.logical_and(out_is_send, out_code == 2 * j + upper_t), 1.0, 0.0)
        for j in range(2)
    ]
    out_sign = jnp.where(out_is_send, -1.0, 1.0)
    in_sign_half = jnp.where(in_is_send, 0.5, -0.5)
    out_match = low_t == out_y
    in_match = low_t == in_y
    in_low_faces = jnp.where(jnp.logical_and(in_match, jnp.logical_not(in_is_send)), 1.0, 0.0)
    in_high_faces = jnp.where(jnp.logical_and(in_match, in_is_send), 1.0, 0.0)
    out_high_faces = jnp.where(jnp.logical_and(out_match, out_is_send), 1.0, 0.0)

    rim_row = lax.broadcasted_iota(jnp.int32, (curve_rows, 128), 0)
    lane_c = lax.broadcasted_iota(jnp.int32, (curve_rows, 128), 1)
    low_c = lane_c < 64
    rim_elem, _, _, rim_turn = decode(down_rows(rim_keys), rim_row < 0)
    rim_first = rim_row < cap_curve
    rim_match = low_c == rim_first
    rim_sign = jnp.where(rim_first, 1.0, -1.0)
    both_codes = jnp.concatenate([in_code, rim_turn], axis=0)
    upper_b = jnp.where(lax.broadcasted_iota(jnp.int32, both_codes.shape, 1) < 64, 0, 1)
    both_masks = [jnp.where(both_codes == 2 * j + upper_b, 1.0, 0.0) for j in range(7)]
    rim_place = jnp.where(rim_match, 1.0, 0.0)

    def one_hot(flags):
        return jnp.where(flags, 1.0, 0.0).astype(half_type)

    gather_lane = lax.broadcasted_iota(jnp.int32, (tile_rows, 2 * elements), 1) % elements
    out_gather = one_hot(gather_lane == out_elem[:, : 2 * elements])
    rim_lane = lax.broadcasted_iota(jnp.int32, (curve_rows, 2 * elements), 1) % elements
    rim_gather = one_hot(rim_lane == rim_elem[:, : 2 * elements])

    lane_shape = (elements, 4 * tile_rows)
    lane_s = lax.broadcasted_iota(jnp.int32, lane_shape, 1)
    in_part = lane_s < 2 * tile_rows
    first_half = (lane_s & (block - 1)) < half_rows
    lane_from_send = first_half != in_part
    t_elem, t_face, _, _ = decode(along_lanes(in_keys * 2 + out_keys * 2), lane_from_send)
    t_hit = t_elem == lax.broadcasted_iota(jnp.int32, lane_shape, 0)
    tile_scatter = one_hot(t_hit)
    rim_shape = (elements, 2 * curve_rows)
    c_elem, c_face, _, _ = decode(
        along_lanes(rim_keys * 2), lax.broadcasted_iota(jnp.int32, rim_shape, 1) < 0
    )
    c_hit = c_elem == lax.broadcasted_iota(jnp.int32, rim_shape, 0)
    rim_scatter = one_hot(c_hit)

    def any_lane(flags):
        return jnp.max(jnp.where(flags, 1.0, 0.0), axis=1, keepdims=True)

    listed = [any_lane(jnp.logical_and(c_hit, c_face == f)) for f in (0, 1)]
    listed += [any_lane(jnp.logical_and(t_hit, t_face == f)) for f in (2, 3, 4, 5)]

    scale_blocks = []
    for start in range(0, elements, 8):
        value = jnp.zeros((8, 128), jnp.int32)
        for at in range(8):
            value = jnp.where(sub_iota == at, jnp.int32(1) << levels_ref[start + at], value)
        scale_blocks.append(value.astype(jnp.float32))
    scale = jnp.concatenate(scale_blocks, axis=0)
    scale = jnp.concatenate([scale] * 4, axis=1)
    vol_scale = scale * (-time_step)
    lift = scale * (28.0 * time_step)

    node = lax.broadcasted_iota(jnp.int32, (elements, 512), 1)
    vel_to_sum = []
    pres_to_vel = []
    own_damp = []
    side_damp = []
    for dim in range(3):
        place = (node >> (6 - 3 * dim)) & 7
        low_end = place == 0
        high_end = place == 7
        on_face = jnp.logical_or(low_end, high_end)
        known = jnp.where(low_end, listed[2 * dim], listed[2 * dim + 1])
        strong = jnp.where(on_face, lift * (1.0 - 0.5 * known), 0.0)
        weak = jnp.where(on_face, lift * (0.5 * known), 0.0)
        vel_to_sum.append(jnp.where(low_end, -strong, strong))
        pres_to_vel.append(jnp.where(low_end, -weak, weak))
        own_damp.append(strong)
        side_damp.append(weak)
    total_damp = side_damp[0] + side_damp[1] + side_damp[2]
    vel_damp = [own_damp[d] + (total_damp - side_damp[d]) for d in range(3)]

    def prepare(at):
        loads[10 + at].wait()
        value = wide[at][...]
        high, low = split(value)
        if at < 2:
            ready[at][...] = high
        elif at < 4:
            ready[at][...] = jnp.concatenate([high, high, low, jnp.zeros_like(low)], axis=0)
        else:
            ready[at][...] = jnp.concatenate([high, low], axis=0)

    def tile_copies(stage):
        return [
            pltpu.make_async_remote_copy(
                src_ref=tile_out.at[stage, off],
                dst_ref=tile_in.at[stage, off],
                send_sem=tile_send_sem.at[stage, off],
                recv_sem=tile_recv_sem.at[stage, off],
                device_id=(b, to_peer[off]),
                device_id_type=MESH,
            )
            for off in range(1, tiles)
        ]

    def curve_copy(stage, side):
        return pltpu.make_async_remote_copy(
            src_ref=curve_out.at[stage, side],
            dst_ref=curve_in.at[stage, 1 - side],
            send_sem=curve_send_sem.at[stage, side],
            recv_sem=curve_recv_sem.at[stage, 1 - side],
            device_id=(b - 1 + 2 * side, t),
            device_id_type=MESH,
        )

    def packed(first, second, low):
        return jnp.where(low, first, second)

    def pair_rows(value, low):
        high = value.astype(half_type).astype(jnp.float32)
        return jnp.concatenate([jnp.where(low, high, value - high), high], axis=1).astype(half_type)

    def rates(current, stage):
        parts = [split(value) for value in current]
        highs = [part[0] for part in parts]
        lows = [part[1] for part in parts]

        low_e = lax.broadcasted_iota(jnp.int32, (elements, 128), 1) < 64
        ends = [split(jnp.where(low_e, v[:, :128], v[:, 384:])) for v in current]
        ends = jnp.concatenate([jnp.concatenate(e, axis=0) for e in ends], axis=1)
        rim = dot(rim_gather, ends)
        rim_vals = []
        for f in range(5):
            kept = jnp.where(rim_match, rim[:, 128 * f : 128 * f + 128], 0.0)
            rim_vals.append(kept + swap_halves(kept))
        sum_part = rim_sign * rim_vals[1] - rim_vals[0]
        vel_part = rim_sign * rim_vals[4] - rim_vals[1]
        rim_send = jnp.concatenate(
            [packed(sum_part, vel_part, low_c), packed(rim_vals[2], rim_vals[3], low_c)], axis=1
        )
        curve_out[stage] = rim_send.reshape(2, cap_curve, 256)
        if stage == 0:
            pl.semaphore_wait(
                barrier, tiles - 1 + has_prev.astype(jnp.int32) + has_next.astype(jnp.int32)
            )

        @pl.when(has_prev)
        def _():
            curve_copy(stage, 0).start()

        @pl.when(has_next)
        def _():
            curve_copy(stage, 1).start()

        if stage == 0:
            prepare(0)
        traces = dot(jnp.concatenate(highs + lows, axis=0), pick_ref[...]).astype(half_type)
        columns = []
        for f in range(5):
            at = f * elements
            low_at = (5 + f) * elements
            columns.append(
                jnp.concatenate(
                    [traces[at : at + elements], traces[low_at : low_at + elements]], axis=0
                )
            )
        own = dot(out_gather, jnp.concatenate(columns, axis=1))
        own_rows = []
        for f in range(5):
            side = jnp.where(
                out_is_send, own[:, 256 * f + 128 : 256 * f + 256], own[:, 256 * f : 256 * f + 128]
            )
            kept = jnp.where(out_match, side, 0.0)
            own_rows.append(pair_rows(kept + swap_halves(kept), low_t))
        if stage == 0:
            prepare(2)
        coded = dot(jnp.concatenate(own_rows, axis=0), send_mat_ref[...])

        def choose(source, rows_at, rows, masks, first):
            total = None
            for j, mask in enumerate(masks):
                at = 128 * (first + j)
                term = mask * source[rows_at : rows_at + rows, at : at + 128]
                total = term if total is None else total + term
            return total + swap_halves(total)

        mortar = [choose(coded, f * tile_rows, tile_rows, out_masks, 0) for f in range(5)]
        normal = jnp.where(out_y, mortar[2], mortar[3])
        other = jnp.where(out_y, mortar[3], mortar[2])
        sum_part = out_sign * normal - mortar[0]
        vel_part = out_sign * mortar[4] - normal
        tile_send = jnp.concatenate(
            [packed(sum_part, vel_part, low_t), packed(mortar[1], other, low_t)], axis=1
        )
        tile_send = tile_send.reshape(tiles, block, 256)
        tile_out[stage] = tile_send
        tile_in[stage, 0] = tile_send[0]
        copies = tile_copies(stage)
        for copy in copies:
            copy.start()

        rest = [choose(coded, f * tile_rows, tile_rows, extra_masks, 7) for f in range(5)]
        rest_n = jnp.where(out_y, rest[2], rest[3])
        rest_o = jnp.where(out_y, rest[3], rest[2])
        rest_p = 0.5 * (rest[4] + rest_n)
        rest_n = 0.5 * (rest_n + rest[4])
        rest_o = 0.5 * rest_o
        rest_fields = [
            0.5 * (rest[0] + jnp.where(out_y, rest[2], rest[3])),
            0.5 * rest[1],
            jnp.where(out_y, rest_n, rest_o),
            jnp.where(out_y, rest_o, rest_n),
            rest_p,
        ]
        rest_parts = [split(value * out_high_faces) for value in rest_fields]

        if stage == 0:
            prepare(4)
            prepare(5)
            prepare(6)
        grad = dot(
            jnp.concatenate([highs[1], highs[4], lows[1], lows[4]], axis=0), along_x_ref[:512]
        )
        n2 = 2 * elements
        grad_x = grad[:n2] + grad[n2:]
        grad_x = grad_x + dot(jnp.concatenate([highs[1], highs[4]], axis=0), along_x_ref[512:])

        def halves(f, source):
            return [source[f][:, :256], source[f][:, 256:]]

        def banded(f, mat_ref):
            high_rows = jnp.concatenate(halves(f, highs) + halves(4, highs), axis=0)
            low_rows = jnp.concatenate(halves(f, lows) + halves(4, lows), axis=0)
            first = dot(jnp.concatenate([high_rows, low_rows], axis=0), mat_ref[:256])
            n4 = 4 * elements
            total = first[:n4] + first[n4:] + dot(high_rows, mat_ref[256:])
            vel = jnp.concatenate([total[:elements], total[elements:n2]], axis=1)
            pres = jnp.concatenate([total[n2 : 3 * elements], total[3 * elements :]], axis=1)
            return vel, pres

        vel_y, pres_y = banded(2, along_y_ref)
        vel_z, pres_z = banded(3, along_z_ref)
        diverge = vol_scale * (grad_x[:elements] + vel_y + vel_z)
        to_sum = diverge
        for d in range(3):
            to_sum = to_sum + vel_to_sum[d] * current[1 + d]
        pres_grads = (grad_x[elements:], pres_y, pres_z)
        result = [to_sum - total_damp * current[0]]
        for d in range(3):
            result.append(
                vol_scale * pres_grads[d]
                + pres_to_vel[d] * current[4]
                - vel_damp[d] * current[1 + d]
            )
        result.append(to_sum - total_damp * current[4])

        for copy in copies:
            copy.wait()

        @pl.when(has_prev)
        def _():
            copy = curve_copy(stage, 0)
            copy.wait_send()
            curve_copy(stage, 1).wait_recv()

        @pl.when(has_next)
        def _():
            copy = curve_copy(stage, 1)
            copy.wait_send()
            curve_copy(stage, 0).wait_recv()

        arrived = jnp.concatenate(
            [
                tile_in[stage].reshape(tile_rows, 256),
                curve_in[stage].reshape(curve_rows, 256),
            ],
            axis=0,
        )
        rows = tile_rows + curve_rows
        low_b = lax.broadcasted_iota(jnp.int32, (rows, 128), 1) < 64
        fields = []
        for at in range(2):
            value = arrived[:, 128 * at : 128 * at + 128]
            turned = swap_halves(value)
            fields.append(pair_rows(jnp.where(low_b, value, turned), low_b))
            fields.append(pair_rows(jnp.where(low_b, turned, value), low_b))
        if stage == 0:
            prepare(3)
            prepare(1)
        taken = dot(jnp.concatenate(fields, axis=0), take_mat_ref[...])
        chosen = [choose(taken, f * rows, rows, both_masks, 0) for f in range(4)]

        rim_in = [value[tile_rows:] * rim_place for value in chosen]
        rim_cols = [jnp.concatenate(split(value), axis=0) for value in rim_in]
        placed = dot(rim_scatter, jnp.concatenate(rim_cols, axis=1))
        place_sum = -0.5 * placed[:, :128]
        place_vel = -0.5 * placed[:, 128:256]
        place_pres = jnp.where(low_e, place_vel, -place_vel)
        rim_fields = [
            place_sum,
            place_vel,
            0.5 * placed[:, 256:384],
            0.5 * placed[:, 384:512],
            place_pres,
        ]

        tile_vals = [value[:tile_rows] for value in chosen]
        put_sum = -0.5 * tile_vals[0]
        put_n = -0.5 * tile_vals[1]
        put_o = 0.5 * tile_vals[3]
        put = [
            put_sum,
            0.5 * tile_vals[2],
            jnp.where(in_y, put_n, put_o),
            jnp.where(in_y, put_o, put_n),
            in_sign_half * tile_vals[1],
        ]
        zero_part = jnp.zeros((tile_rows, 128), half_type)
        columns = []
        for f in range(5):
            first = split(put[f] * in_low_faces)
            second = split(put[f] * in_high_faces)
            high, low = rest_parts[f]
            columns.append(jnp.concatenate([first[0], first[1], zero_part, zero_part], axis=0))
            columns.append(jnp.concatenate([second[0], second[1], high, low], axis=0))
        on_faces = dot(tile_scatter, jnp.concatenate(columns, axis=1))
        face_parts = [split(on_faces[:, 256 * f : 256 * f + 256]) for f in range(5)]
        spread = dot(
            jnp.concatenate([p[0] for p in face_parts] + [p[1] for p in face_parts], axis=0),
            spread_ref[...],
        )
        finished = []
        zero_middle = jnp.zeros((elements, 256), jnp.float32)
        for f in range(5):
            at = f * elements
            low_at = (5 + f) * elements
            nodes = spread[at : at + elements] + spread[low_at : low_at + elements]
            rim_nodes = jnp.concatenate(
                [
                    jnp.where(low_e, rim_fields[f], 0.0),
                    zero_middle,
                    jnp.where(low_e, 0.0, rim_fields[f]),
                ],
                axis=1,
            )
            finished.append(result[f] + lift * (nodes + rim_nodes))
        return finished

    loads[0].wait()
    current = [state_ref[f] for f in range(5)]
    change = rates(current, 0)
    current = [current[f] + change[f] for f in range(5)]
    change = rates(current, 1)
    current = [0.75 * state_ref[f] + 0.25 * (current[f] + change[f]) for f in range(5)]
    change = rates(current, 2)
    for f in range(5):
        out_ref[f] = state_ref[f] / 3.0 + (2.0 / 3.0) * (current[f] + change[f])


def shards(
    state,
    levels,
    send_faces,
    send_counts,
    recv_faces,
    recv_orients,
    recv_counts,
    curve_faces,
    curve_orients,
    curve_counts,
):
    curves = lax.axis_size("curve")
    tiles, cap_tile = send_faces.shape
    cap_curve = curve_faces.shape[1]
    elements = state.shape[1]
    half_rows = -(-cap_tile // 4) * 4
    sizes = (curves, tiles, elements, cap_tile, cap_curve, half_rows)
    block = 2 * half_rows
    operands = [
        state,
        levels,
        send_faces,
        send_counts,
        recv_faces,
        recv_orients,
        recv_counts,
        curve_faces,
        curve_orients,
        curve_counts,
        *tables(),
    ]
    held = [
        pltpu.SMEM(value.shape, value.dtype)
        if value.dtype == jnp.int32
        else pltpu.VMEM(value.shape, value.dtype)
        for value in operands
    ]
    return pl.pallas_call(
        functools.partial(section_kernel, sizes),
        out_shape=jax.ShapeDtypeStruct(state.shape, state.dtype),
        in_specs=[pl.BlockSpec(memory_space=pl.ANY)] * operand_count,
        out_specs=pl.BlockSpec(memory_space=pltpu.VMEM),
        scratch_shapes=held
        + [
            pltpu.VMEM((3, tiles, block, 256), jnp.float32),
            pltpu.VMEM((3, tiles, block, 256), jnp.float32),
            pltpu.VMEM((3, 2, cap_curve, 256), jnp.float32),
            pltpu.VMEM((3, 2, cap_curve, 256), jnp.float32),
            pltpu.SemaphoreType.DMA((3, tiles)),
            pltpu.SemaphoreType.DMA((3, tiles)),
            pltpu.SemaphoreType.DMA((3, 2)),
            pltpu.SemaphoreType.DMA((3, 2)),
            pltpu.SemaphoreType.DMA((operand_count,)),
        ]
        + [
            pltpu.VMEM((value.shape[0] * times, value.shape[1]), half_type)
            for value, times in zip(operands[10:], (1, 1, 4, 4, 2, 2, 2))
        ],
        compiler_params=pltpu.CompilerParams(
            collective_id=0, has_side_effects=True, vmem_limit_bytes=60 * 1024 * 1024
        ),
    )(*operands)


def solution(mesh):
    return jax.shard_map(
        shards,
        mesh=mesh,
        in_specs=(
            P(None, ("curve", "tile"), None),
            P(("curve", "tile")),
            P(("curve", "tile"), None),
            P(("curve", "tile")),
            P(("curve", "tile"), None),
            P(("curve", "tile"), None),
            P(("curve", "tile")),
            P(("curve", "tile"), None),
            P(("curve", "tile"), None),
            P(("curve", "tile")),
        ),
        out_specs=P(None, ("curve", "tile"), None),
        check_vma=False,
    )
```

```python
import functools

import jax
import jax.numpy as jnp
import ml_dtypes
import numpy as np
from jax import lax
from jax.experimental import pallas as pl
from jax.experimental.pallas import tpu as pltpu
from jax.sharding import PartitionSpec as P

time_step = 0.002
half_type = jnp.bfloat16
MESH = pl.DeviceIdType.MESH
operand_count = 17
load_order = [3, 2, 5, 4, 6, 8, 7, 9, 1, 0, 10, 12, 14, 15, 16, 13, 11]
inner_nodes = [
    -0.8717401485096066,
    -0.5917001814331423,
    -0.20929921790247888,
    0.20929921790247888,
    0.5917001814331423,
    0.8717401485096066,
]


def legendre_seven(abscissa):
    before = abscissa * 0.0 + 1.0
    current = abscissa + 0.0
    for order in range(1, 7):
        before, current = (
            current,
            ((2 * order + 1) * abscissa * current - order * before) / (order + 1),
        )
    return current


def tables():
    points = np.array([-1.0] + inner_nodes + [1.0])
    values = legendre_seven(points)
    weights = 2.0 / (56 * values**2)
    deriv = np.zeros((8, 8))
    for row in range(8):
        for col in range(8):
            if row != col:
                deriv[row, col] = values[row] / (values[col] * (points[row] - points[col]))
    deriv[0, 0] = -14.0
    deriv[7, 7] = 14.0
    halves = []
    projections = []
    for side in range(2):
        targets = (points + 2.0 * side - 1.0) / 2.0
        interp = np.ones((8, 8))
        for col in range(8):
            for other in range(8):
                if other != col:
                    interp[:, col] *= (targets - points[other]) / (points[col] - points[other])
        halves.append(interp)
        projections.append(0.5 * (interp.T * weights[None, :]) / weights[:, None])
    pairs = [(a, b) for a in range(2) for b in range(2)]
    mortar = [np.kron(halves[a], halves[b]) for a, b in pairs]
    project = [np.kron(projections[a], projections[b]) for a, b in pairs]
    turn = np.zeros((8, 64, 64))
    for code in range(8):
        for s in range(8):
            for t in range(8):
                a, c = (t, s) if code & 4 else (s, t)
                a = 7 - a if code & 1 else a
                c = 7 - c if code & 2 else c
                turn[code, 8 * s + t, 8 * a + c] = 1.0
    eye = np.eye(64)
    send = mortar + [eye] + [turn[o].T for o in range(8)] + [np.zeros((64, 64))]
    send += [0.25 * eye - q @ m for q, m in zip(project, mortar)]
    take = [turn[o] for o in range(8)] + project + [eye, np.zeros((64, 64))]

    pick = np.zeros((512, 256))
    for s in range(8):
        for t in range(8):
            column = 8 * s + t
            pick[64 * s + t, column] = 1.0
            pick[64 * s + 8 * t, 64 + column] = 1.0
            pick[64 * s + 56 + t, 128 + column] = 1.0
            pick[64 * s + 8 * t + 7, 192 + column] = 1.0
    return [
        jnp.asarray(m.astype(np.float32))
        for m in (
            pick,
            pick.T,
            np.concatenate([m.T for m in send], axis=1),
            np.concatenate([m.T for m in take], axis=1),
            np.kron(deriv.T, np.eye(64)),
            np.kron(np.eye(4), np.kron(deriv.T, np.eye(8))),
            np.kron(np.eye(32), deriv.T),
        )
    ]


def dot(left, right):
    return jnp.dot(left, right, preferred_element_type=jnp.float32)


def split(value):
    high = value.astype(half_type)
    return high, (value - high.astype(jnp.float32)).astype(half_type)


def div_five(value):
    return (value * 52429) >> 18


def div_six(value):
    return (value * 43691) >> 18


def swap_halves(value):
    return pltpu.roll(value, 64, axis=1)


def section_kernel(
    sizes,
    *refs,
):
    given = refs[:operand_count]
    out_ref = refs[operand_count]
    held = refs[operand_count + 1 : 2 * operand_count + 1]
    (
        tile_out,
        tile_in,
        curve_out,
        curve_in,
        tile_send_sem,
        tile_recv_sem,
        curve_send_sem,
        curve_recv_sem,
        load_sem,
        held_state,
        *ready,
    ) = refs[2 * operand_count + 1 :]
    pick_ref, spread_ref, send_mat_ref, take_mat_ref, along_x_ref, along_y_ref, along_z_ref = ready
    (
        state_ref,
        levels_ref,
        send_faces_ref,
        send_counts_ref,
        recv_faces_ref,
        recv_orients_ref,
        recv_counts_ref,
        curve_faces_ref,
        curve_orients_ref,
        curve_counts_ref,
        *wide,
    ) = held
    loads = [
        pltpu.make_async_copy(source, target, load_sem.at[at])
        for at, (source, target) in enumerate(zip(given, held))
    ]
    for at in load_order:
        loads[at].start()
    curves, tiles, elements, cap_tile, cap_curve, half_rows = sizes
    block = 2 * half_rows
    tile_rows = tiles * block
    curve_rows = 2 * cap_curve
    b = lax.axis_index("curve")
    t = lax.axis_index("tile")
    to_peer = [lax.rem(t + off, tiles) for off in range(tiles)]
    from_peer = [lax.rem(t + tiles - off, tiles) for off in range(tiles)]
    has_prev = b > 0
    has_next = b < curves - 1

    barrier = pltpu.get_barrier_semaphore()
    for off in range(1, tiles):
        pl.semaphore_signal(barrier, inc=1, device_id=(b, to_peer[off]), device_id_type=MESH)

    @pl.when(has_prev)
    def _():
        pl.semaphore_signal(barrier, inc=1, device_id=(b - 1, t), device_id_type=MESH)

    @pl.when(has_next)
    def _():
        pl.semaphore_signal(barrier, inc=1, device_id=(b + 1, t), device_id_type=MESH)

    @pl.when(jnp.logical_not(has_prev))
    def _():
        curve_in[:, 0] = jnp.zeros_like(curve_in[:, 0])

    @pl.when(jnp.logical_not(has_next))
    def _():
        curve_in[:, 1] = jnp.zeros_like(curve_in[:, 1])

    for at in range(1, 10):
        loads[at].wait()

    def send_key(peer, slot):
        if slot >= cap_tile:
            return jnp.int32(-1)
        return jnp.where(slot < send_counts_ref[peer], send_faces_ref[peer, slot] * 16, -1)

    def recv_key(peer, slot):
        if slot >= cap_tile:
            return jnp.int32(-1)
        value = recv_faces_ref[peer, slot] * 16 + recv_orients_ref[peer, slot]
        return jnp.where(slot < recv_counts_ref[peer], value, -1)

    def curve_key(side, slot):
        value = curve_faces_ref[side, slot] * 16 + curve_orients_ref[side, slot]
        return jnp.where(slot < curve_counts_ref[side], value, -1)

    out_keys = []
    in_keys = []
    for off in range(tiles):
        out_keys += [send_key(to_peer[off], slot) for slot in range(half_rows)]
        out_keys += [recv_key(to_peer[off], slot) for slot in range(half_rows)]
        in_keys += [recv_key(from_peer[off], slot) for slot in range(half_rows)]
        in_keys += [send_key(from_peer[off], slot) for slot in range(half_rows)]
    rim_keys = [curve_key(side, slot) for side in range(2) for slot in range(cap_curve)]

    sub_iota = lax.broadcasted_iota(jnp.int32, (8, 128), 0)

    def down_rows(keys):
        blocks = []
        for start in range(0, len(keys), 8):
            value = jnp.full((8, 128), -1, jnp.int32)
            for at in range(8):
                value = jnp.where(sub_iota == at, keys[start + at], value)
            blocks.append(value)
        return jnp.concatenate(blocks, axis=0)

    def along_lanes(keys, times):
        count = len(keys)
        lane = lax.broadcasted_iota(jnp.int32, (8, times * count), 1) % count
        value = jnp.full((8, times * count), -1, jnp.int32)
        for at, key in enumerate(keys):
            value = jnp.where(lane == at, key, value)
        return jnp.concatenate([value] * (elements // 8), axis=0)

    def decode(keys, from_send):
        live = keys >= 0
        raw = jnp.maximum(keys, 0) >> 4
        turned = jnp.maximum(keys, 0) & 15
        face_id = jnp.where(from_send, div_five(raw), raw)
        child = raw - 5 * face_id
        element = div_six(face_id)
        face = face_id - 6 * element
        return jnp.where(live, element, -1), face, child, turned

    def half_flags(shape, axis, first):
        at = lax.broadcasted_iota(jnp.int32, shape, axis)
        return (at & (block - 1)) < half_rows if first else (at & (block - 1)) >= half_rows

    lane_t = lax.broadcasted_iota(jnp.int32, (tile_rows, 128), 1)
    low_t = lane_t < 64
    out_is_send = half_flags((tile_rows, 128), 0, True)
    in_is_send = half_flags((tile_rows, 128), 0, False)
    out_elem, out_face, out_child, out_turn = decode(down_rows(out_keys), out_is_send)
    in_elem, in_face, in_child, in_turn = decode(down_rows(in_keys), in_is_send)
    out_y = out_face < 4
    in_y = in_face < 4
    out_code = jnp.where(out_is_send, out_child, 5 + out_turn)
    in_code = jnp.where(in_is_send, 8 + in_child, in_turn)
    upper_t = jnp.where(low_t, 0, 1)
    out_masks = [jnp.where(out_code == 2 * j + upper_t, 1.0, 0.0) for j in range(7)]
    extra_masks = [
        jnp.where(jnp.logical_and(out_is_send, out_code == 2 * j + upper_t), 1.0, 0.0)
        for j in range(2)
    ]
    out_sign = jnp.where(out_is_send, -1.0, 1.0)
    in_sign_half = jnp.where(in_is_send, 0.5, -0.5)
    out_match = low_t == out_y
    in_match = low_t == in_y
    in_low_faces = jnp.where(jnp.logical_and(in_match, jnp.logical_not(in_is_send)), 1.0, 0.0)
    in_high_faces = jnp.where(jnp.logical_and(in_match, in_is_send), 1.0, 0.0)
    out_high_faces = jnp.where(jnp.logical_and(out_match, out_is_send), 1.0, 0.0)

    rim_row = lax.broadcasted_iota(jnp.int32, (curve_rows, 128), 0)
    lane_c = lax.broadcasted_iota(jnp.int32, (curve_rows, 128), 1)
    low_c = lane_c < 64
    rim_elem, _, _, rim_turn = decode(down_rows(rim_keys), rim_row < 0)
    rim_first = rim_row < cap_curve
    rim_match = low_c == rim_first
    rim_sign = jnp.where(rim_first, 1.0, -1.0)
    both_codes = jnp.concatenate([in_code, rim_turn], axis=0)
    upper_b = jnp.where(lax.broadcasted_iota(jnp.int32, both_codes.shape, 1) < 64, 0, 1)
    both_masks = [jnp.where(both_codes == 2 * j + upper_b, 1.0, 0.0) for j in range(7)]
    rim_place = jnp.where(rim_match, 1.0, 0.0)

    def one_hot(flags):
        return jnp.where(flags, 1.0, 0.0).astype(half_type)

    gather_lane = lax.broadcasted_iota(jnp.int32, (tile_rows, 2 * elements), 1) % elements
    out_gather = one_hot(gather_lane == out_elem[:, : 2 * elements])
    rim_lane = lax.broadcasted_iota(jnp.int32, (curve_rows, 2 * elements), 1) % elements
    rim_gather = one_hot(rim_lane == rim_elem[:, : 2 * elements])

    lane_shape = (elements, 4 * tile_rows)
    lane_s = lax.broadcasted_iota(jnp.int32, lane_shape, 1)
    in_part = lane_s < 2 * tile_rows
    first_half = (lane_s & (block - 1)) < half_rows
    lane_from_send = first_half != in_part
    t_elem, t_face, _, _ = decode(
        jnp.where(in_part, along_lanes(in_keys, 4), along_lanes(out_keys, 4)), lane_from_send
    )
    t_hit = t_elem == lax.broadcasted_iota(jnp.int32, lane_shape, 0)
    tile_scatter = one_hot(t_hit)
    rim_shape = (elements, 2 * curve_rows)
    c_elem, c_face, _, _ = decode(
        along_lanes(rim_keys, 2), lax.broadcasted_iota(jnp.int32, rim_shape, 1) < 0
    )
    c_hit = c_elem == lax.broadcasted_iota(jnp.int32, rim_shape, 0)
    rim_scatter = one_hot(c_hit)

    def any_lane(flags):
        return jnp.max(jnp.where(flags, 1.0, 0.0), axis=1, keepdims=True)

    listed = [any_lane(jnp.logical_and(c_hit, c_face == f)) for f in (0, 1)]
    listed += [any_lane(jnp.logical_and(t_hit, t_face == f)) for f in (2, 3, 4, 5)]

    scale_blocks = []
    for start in range(0, elements, 8):
        value = jnp.zeros((8, 128), jnp.int32)
        for at in range(8):
            value = jnp.where(sub_iota == at, jnp.int32(1) << levels_ref[start + at], value)
        scale_blocks.append(value.astype(jnp.float32))
    scale = jnp.concatenate(scale_blocks, axis=0)
    scale = jnp.concatenate([scale] * 4, axis=1)
    vol_scale = scale * (-time_step)
    lift = scale * (28.0 * time_step)

    node = lax.broadcasted_iota(jnp.int32, (elements, 512), 1)
    vel_to_sum = []
    pres_to_vel = []
    own_damp = []
    side_damp = []
    for dim in range(3):
        place = (node >> (6 - 3 * dim)) & 7
        low_end = place == 0
        high_end = place == 7
        on_face = jnp.logical_or(low_end, high_end)
        known = jnp.where(low_end, listed[2 * dim], listed[2 * dim + 1])
        strong = jnp.where(on_face, lift * (1.0 - 0.5 * known), 0.0)
        weak = jnp.where(on_face, lift * (0.5 * known), 0.0)
        vel_to_sum.append(jnp.where(low_end, -strong, strong))
        pres_to_vel.append(jnp.where(low_end, -weak, weak))
        own_damp.append(strong)
        side_damp.append(weak)
    total_damp = side_damp[0] + side_damp[1] + side_damp[2]
    vel_damp = [own_damp[d] + (total_damp - side_damp[d]) for d in range(3)]

    def prepare(at):
        loads[10 + at].wait()
        value = wide[at][...]
        high, low = split(value)
        if at < 2:
            ready[at][...] = high
        elif at < 4:
            ready[at][...] = jnp.concatenate([high, high, low, jnp.zeros_like(low)], axis=0)
        else:
            ready[at][...] = jnp.concatenate([high, low], axis=0)

    def tile_copies(stage):
        return [
            pltpu.make_async_remote_copy(
                src_ref=tile_out.at[stage, off],
                dst_ref=tile_in.at[stage, off],
                send_sem=tile_send_sem.at[stage, off],
                recv_sem=tile_recv_sem.at[stage, off],
                device_id=(b, to_peer[off]),
                device_id_type=MESH,
            )
            for off in range(1, tiles)
        ]

    def curve_copy(stage, side):
        return pltpu.make_async_remote_copy(
            src_ref=curve_out.at[stage, side],
            dst_ref=curve_in.at[stage, 1 - side],
            send_sem=curve_send_sem.at[stage, side],
            recv_sem=curve_recv_sem.at[stage, 1 - side],
            device_id=(b - 1 + 2 * side, t),
            device_id_type=MESH,
        )

    def packed(first, second, low):
        return jnp.where(low, first, second)

    def pair_rows(value, low):
        high = value.astype(half_type).astype(jnp.float32)
        return jnp.concatenate([jnp.where(low, high, value - high), high], axis=1).astype(half_type)

    def rates(current, stage):
        parts = [split(value) for value in current]
        highs = [part[0] for part in parts]
        lows = [part[1] for part in parts]

        low_e = lax.broadcasted_iota(jnp.int32, (elements, 128), 1) < 64
        ends = [split(jnp.where(low_e, v[:, :128], v[:, 384:])) for v in current]
        ends = jnp.concatenate([jnp.concatenate(e, axis=0) for e in ends], axis=1)
        rim = dot(rim_gather, ends)
        rim_vals = []
        for f in range(5):
            kept = jnp.where(rim_match, rim[:, 128 * f : 128 * f + 128], 0.0)
            rim_vals.append(kept + swap_halves(kept))
        sum_part = rim_sign * rim_vals[1] - rim_vals[0]
        vel_part = rim_sign * rim_vals[4] - rim_vals[1]
        rim_send = jnp.concatenate(
            [packed(sum_part, vel_part, low_c), packed(rim_vals[2], rim_vals[3], low_c)], axis=1
        )
        curve_out[stage] = rim_send.reshape(2, cap_curve, 256)

        @pl.when(stage == 0)
        def _():
            pl.semaphore_wait(
                barrier, tiles - 1 + has_prev.astype(jnp.int32) + has_next.astype(jnp.int32)
            )

        @pl.when(has_prev)
        def _():
            curve_copy(stage, 0).start()

        @pl.when(has_next)
        def _():
            curve_copy(stage, 1).start()

        @pl.when(stage == 0)
        def _():
            prepare(0)

        traces = dot(jnp.concatenate(highs + lows, axis=0), pick_ref[...]).astype(half_type)
        columns = []
        for f in range(5):
            at = f * elements
            low_at = (5 + f) * elements
            columns.append(
                jnp.concatenate(
                    [traces[at : at + elements], traces[low_at : low_at + elements]], axis=0
                )
            )
        own = dot(out_gather, jnp.concatenate(columns, axis=1))
        own_rows = []
        for f in range(5):
            side = jnp.where(
                out_is_send, own[:, 256 * f + 128 : 256 * f + 256], own[:, 256 * f : 256 * f + 128]
            )
            kept = jnp.where(out_match, side, 0.0)
            own_rows.append(pair_rows(kept + swap_halves(kept), low_t))
        @pl.when(stage == 0)
        def _():
            prepare(2)

        coded = dot(jnp.concatenate(own_rows, axis=0), send_mat_ref[...])

        def choose(source, rows_at, rows, masks, first):
            total = None
            for j, mask in enumerate(masks):
                at = 128 * (first + j)
                term = mask * source[rows_at : rows_at + rows, at : at + 128]
                total = term if total is None else total + term
            return total + swap_halves(total)

        mortar = [choose(coded, f * tile_rows, tile_rows, out_masks, 0) for f in range(5)]
        normal = jnp.where(out_y, mortar[2], mortar[3])
        other = jnp.where(out_y, mortar[3], mortar[2])
        sum_part = out_sign * normal - mortar[0]
        vel_part = out_sign * mortar[4] - normal
        tile_send = jnp.concatenate(
            [packed(sum_part, vel_part, low_t), packed(mortar[1], other, low_t)], axis=1
        )
        tile_send = tile_send.reshape(tiles, block, 256)
        tile_out[stage] = tile_send
        tile_in[stage, 0] = tile_send[0]
        copies = tile_copies(stage)
        for copy in copies:
            copy.start()

        rest = [choose(coded, f * tile_rows, tile_rows, extra_masks, 7) for f in range(5)]
        rest_n = jnp.where(out_y, rest[2], rest[3])
        rest_o = jnp.where(out_y, rest[3], rest[2])
        rest_p = 0.5 * (rest[4] + rest_n)
        rest_n = 0.5 * (rest_n + rest[4])
        rest_o = 0.5 * rest_o
        rest_fields = [
            0.5 * (rest[0] + jnp.where(out_y, rest[2], rest[3])),
            0.5 * rest[1],
            jnp.where(out_y, rest_n, rest_o),
            jnp.where(out_y, rest_o, rest_n),
            rest_p,
        ]
        rest_parts = [split(value * out_high_faces) for value in rest_fields]

        @pl.when(stage == 0)
        def _():
            prepare(4)
            prepare(5)
            prepare(6)

        grad = dot(
            jnp.concatenate([highs[1], highs[4], lows[1], lows[4]], axis=0), along_x_ref[:512]
        )
        n2 = 2 * elements
        grad_x = grad[:n2] + grad[n2:]
        grad_x = grad_x + dot(jnp.concatenate([highs[1], highs[4]], axis=0), along_x_ref[512:])

        def halves(f, source):
            return [source[f][:, :256], source[f][:, 256:]]

        def banded(f, mat_ref):
            high_rows = jnp.concatenate(halves(f, highs) + halves(4, highs), axis=0)
            low_rows = jnp.concatenate(halves(f, lows) + halves(4, lows), axis=0)
            first = dot(jnp.concatenate([high_rows, low_rows], axis=0), mat_ref[:256])
            n4 = 4 * elements
            total = first[:n4] + first[n4:] + dot(high_rows, mat_ref[256:])
            vel = jnp.concatenate([total[:elements], total[elements:n2]], axis=1)
            pres = jnp.concatenate([total[n2 : 3 * elements], total[3 * elements :]], axis=1)
            return vel, pres

        vel_y, pres_y = banded(2, along_y_ref)
        vel_z, pres_z = banded(3, along_z_ref)
        diverge = vol_scale * (grad_x[:elements] + vel_y + vel_z)
        to_sum = diverge
        for d in range(3):
            to_sum = to_sum + vel_to_sum[d] * current[1 + d]
        pres_grads = (grad_x[elements:], pres_y, pres_z)
        result = [to_sum - total_damp * current[0]]
        for d in range(3):
            result.append(
                vol_scale * pres_grads[d]
                + pres_to_vel[d] * current[4]
                - vel_damp[d] * current[1 + d]
            )
        result.append(to_sum - total_damp * current[4])

        for copy in copies:
            copy.wait()

        @pl.when(has_prev)
        def _():
            copy = curve_copy(stage, 0)
            copy.wait_send()
            curve_copy(stage, 1).wait_recv()

        @pl.when(has_next)
        def _():
            copy = curve_copy(stage, 1)
            copy.wait_send()
            curve_copy(stage, 0).wait_recv()

        arrived = jnp.concatenate(
            [
                tile_in[stage].reshape(tile_rows, 256),
                curve_in[stage].reshape(curve_rows, 256),
            ],
            axis=0,
        )
        rows = tile_rows + curve_rows
        low_b = lax.broadcasted_iota(jnp.int32, (rows, 128), 1) < 64
        fields = []
        for at in range(2):
            value = arrived[:, 128 * at : 128 * at + 128]
            turned = swap_halves(value)
            fields.append(pair_rows(jnp.where(low_b, value, turned), low_b))
            fields.append(pair_rows(jnp.where(low_b, turned, value), low_b))
        @pl.when(stage == 0)
        def _():
            prepare(3)
            prepare(1)

        taken = dot(jnp.concatenate(fields, axis=0), take_mat_ref[...])
        chosen = [choose(taken, f * rows, rows, both_masks, 0) for f in range(4)]

        rim_in = [value[tile_rows:] * rim_place for value in chosen]
        rim_cols = [jnp.concatenate(split(value), axis=0) for value in rim_in]
        placed = dot(rim_scatter, jnp.concatenate(rim_cols, axis=1))
        place_sum = -0.5 * placed[:, :128]
        place_vel = -0.5 * placed[:, 128:256]
        place_pres = jnp.where(low_e, place_vel, -place_vel)
        rim_fields = [
            place_sum,
            place_vel,
            0.5 * placed[:, 256:384],
            0.5 * placed[:, 384:512],
            place_pres,
        ]

        tile_vals = [value[:tile_rows] for value in chosen]
        put_sum = -0.5 * tile_vals[0]
        put_n = -0.5 * tile_vals[1]
        put_o = 0.5 * tile_vals[3]
        put = [
            put_sum,
            0.5 * tile_vals[2],
            jnp.where(in_y, put_n, put_o),
            jnp.where(in_y, put_o, put_n),
            in_sign_half * tile_vals[1],
        ]
        zero_part = jnp.zeros((tile_rows, 128), half_type)
        columns = []
        for f in range(5):
            first = split(put[f] * in_low_faces)
            second = split(put[f] * in_high_faces)
            high, low = rest_parts[f]
            columns.append(jnp.concatenate([first[0], first[1], zero_part, zero_part], axis=0))
            columns.append(jnp.concatenate([second[0], second[1], high, low], axis=0))
        on_faces = dot(tile_scatter, jnp.concatenate(columns, axis=1))
        face_parts = [split(on_faces[:, 256 * f : 256 * f + 256]) for f in range(5)]
        spread = dot(
            jnp.concatenate([p[0] for p in face_parts] + [p[1] for p in face_parts], axis=0),
            spread_ref[...],
        )
        finished = []
        zero_middle = jnp.zeros((elements, 256), jnp.float32)
        for f in range(5):
            at = f * elements
            low_at = (5 + f) * elements
            nodes = spread[at : at + elements] + spread[low_at : low_at + elements]
            rim_nodes = jnp.concatenate(
                [
                    jnp.where(low_e, rim_fields[f], 0.0),
                    zero_middle,
                    jnp.where(low_e, 0.0, rim_fields[f]),
                ],
                axis=1,
            )
            finished.append(result[f] + lift * (nodes + rim_nodes))
        return finished

    loads[0].wait()
    held_state[...] = state_ref[...]

    def section(stage, carry):
        current = [held_state[f] for f in range(5)]
        change = rates(current, stage)
        keep = jnp.where(stage == 0, 0.0, jnp.where(stage == 1, 0.75, 1.0 / 3.0))
        move = jnp.where(stage == 0, 1.0, jnp.where(stage == 1, 0.25, 2.0 / 3.0))
        for f in range(5):
            held_state[f] = keep * state_ref[f] + move * (held_state[f] + change[f])
        return carry

    lax.fori_loop(0, 3, section, 0)
    out_ref[...] = held_state[...]


def shards(
    state,
    levels,
    send_faces,
    send_counts,
    recv_faces,
    recv_orients,
    recv_counts,
    curve_faces,
    curve_orients,
    curve_counts,
):
    curves = lax.axis_size("curve")
    tiles, cap_tile = send_faces.shape
    cap_curve = curve_faces.shape[1]
    elements = state.shape[1]
    half_rows = -(-cap_tile // 4) * 4
    sizes = (curves, tiles, elements, cap_tile, cap_curve, half_rows)
    block = 2 * half_rows
    operands = [
        state,
        levels,
        send_faces,
        send_counts,
        recv_faces,
        recv_orients,
        recv_counts,
        curve_faces,
        curve_orients,
        curve_counts,
        *tables(),
    ]
    held = [
        pltpu.SMEM(value.shape, value.dtype)
        if value.dtype == jnp.int32
        else pltpu.VMEM(value.shape, value.dtype)
        for value in operands
    ]
    return pl.pallas_call(
        functools.partial(section_kernel, sizes),
        out_shape=jax.ShapeDtypeStruct(state.shape, state.dtype),
        in_specs=[pl.BlockSpec(memory_space=pl.ANY)] * operand_count,
        out_specs=pl.BlockSpec(memory_space=pltpu.VMEM),
        scratch_shapes=held
        + [
            pltpu.VMEM((3, tiles, block, 256), jnp.float32),
            pltpu.VMEM((3, tiles, block, 256), jnp.float32),
            pltpu.VMEM((3, 2, cap_curve, 256), jnp.float32),
            pltpu.VMEM((3, 2, cap_curve, 256), jnp.float32),
            pltpu.SemaphoreType.DMA((3, tiles)),
            pltpu.SemaphoreType.DMA((3, tiles)),
            pltpu.SemaphoreType.DMA((3, 2)),
            pltpu.SemaphoreType.DMA((3, 2)),
            pltpu.SemaphoreType.DMA((operand_count,)),
            pltpu.VMEM(state.shape, jnp.float32),
        ]
        + [
            pltpu.VMEM((value.shape[0] * times, value.shape[1]), half_type)
            for value, times in zip(operands[10:], (1, 1, 4, 4, 2, 2, 2))
        ],
        compiler_params=pltpu.CompilerParams(
            collective_id=0, has_side_effects=True, vmem_limit_bytes=60 * 1024 * 1024
        ),
    )(*operands)


def solution(mesh):
    return jax.shard_map(
        shards,
        mesh=mesh,
        in_specs=(
            P(None, ("curve", "tile"), None),
            P(("curve", "tile")),
            P(("curve", "tile"), None),
            P(("curve", "tile")),
            P(("curve", "tile"), None),
            P(("curve", "tile"), None),
            P(("curve", "tile")),
            P(("curve", "tile"), None),
            P(("curve", "tile"), None),
            P(("curve", "tile")),
        ),
        out_specs=P(None, ("curve", "tile"), None),
        check_vma=False,
    )
```

```python
import functools

import jax
import jax.numpy as jnp
import ml_dtypes
import numpy as np
from jax import lax
from jax.experimental import pallas as pl
from jax.experimental.pallas import tpu as pltpu
from jax.sharding import PartitionSpec as P

time_step = 0.002
half_type = jnp.bfloat16
MESH = pl.DeviceIdType.MESH
operand_count = 17
load_order = [3, 2, 5, 4, 6, 8, 7, 9, 1, 0, 10, 12, 14, 15, 16, 13, 11]
inner_nodes = [
    -0.8717401485096066,
    -0.5917001814331423,
    -0.20929921790247888,
    0.20929921790247888,
    0.5917001814331423,
    0.8717401485096066,
]


def legendre_seven(abscissa):
    before = abscissa * 0.0 + 1.0
    current = abscissa + 0.0
    for order in range(1, 7):
        before, current = (
            current,
            ((2 * order + 1) * abscissa * current - order * before) / (order + 1),
        )
    return current


def tables():
    points = np.array([-1.0] + inner_nodes + [1.0])
    values = legendre_seven(points)
    weights = 2.0 / (56 * values**2)
    deriv = np.zeros((8, 8))
    for row in range(8):
        for col in range(8):
            if row != col:
                deriv[row, col] = values[row] / (values[col] * (points[row] - points[col]))
    deriv[0, 0] = -14.0
    deriv[7, 7] = 14.0
    halves = []
    projections = []
    for side in range(2):
        targets = (points + 2.0 * side - 1.0) / 2.0
        interp = np.ones((8, 8))
        for col in range(8):
            for other in range(8):
                if other != col:
                    interp[:, col] *= (targets - points[other]) / (points[col] - points[other])
        halves.append(interp)
        projections.append(0.5 * (interp.T * weights[None, :]) / weights[:, None])
    pairs = [(a, b) for a in range(2) for b in range(2)]
    mortar = [np.kron(halves[a], halves[b]) for a, b in pairs]
    project = [np.kron(projections[a], projections[b]) for a, b in pairs]
    turn = np.zeros((8, 64, 64))
    for code in range(8):
        for s in range(8):
            for t in range(8):
                a, c = (t, s) if code & 4 else (s, t)
                a = 7 - a if code & 1 else a
                c = 7 - c if code & 2 else c
                turn[code, 8 * s + t, 8 * a + c] = 1.0
    eye = np.eye(64)
    send = mortar + [eye] + [turn[o].T for o in range(8)] + [np.zeros((64, 64))]
    send += [0.25 * eye - q @ m for q, m in zip(project, mortar)]
    take = [turn[o] for o in range(8)] + project + [eye, np.zeros((64, 64))]

    pick = np.zeros((512, 256))
    for s in range(8):
        for t in range(8):
            column = 8 * s + t
            pick[64 * s + t, column] = 1.0
            pick[64 * s + 8 * t, 64 + column] = 1.0
            pick[64 * s + 56 + t, 128 + column] = 1.0
            pick[64 * s + 8 * t + 7, 192 + column] = 1.0
    return [
        jnp.asarray(m.astype(np.float32))
        for m in (
            pick,
            pick.T,
            np.concatenate([m.T for m in send], axis=1),
            np.concatenate([m.T for m in take], axis=1),
            np.kron(deriv.T, np.eye(64)),
            np.kron(np.eye(4), np.kron(deriv.T, np.eye(8))),
            np.kron(np.eye(32), deriv.T),
        )
    ]


def dot(left, right):
    return jnp.dot(left, right, preferred_element_type=jnp.float32)


def split(value):
    high = value.astype(half_type)
    return high, (value - high.astype(jnp.float32)).astype(half_type)


def div_five(value):
    return (value * 52429) >> 18


def div_six(value):
    return (value * 43691) >> 18


def swap_halves(value):
    return pltpu.roll(value, 64, axis=1)


def section_kernel(
    sizes,
    *refs,
):
    given = refs[:operand_count]
    out_ref = refs[operand_count]
    held = refs[operand_count + 1 : 2 * operand_count + 1]
    (
        tile_out,
        tile_in,
        curve_out,
        curve_in,
        tile_send_sem,
        tile_recv_sem,
        curve_send_sem,
        curve_recv_sem,
        load_sem,
        held_state,
        *ready,
    ) = refs[2 * operand_count + 1 :]
    pick_ref, spread_ref, send_mat_ref, take_mat_ref, along_x_ref, along_y_ref, along_z_ref = ready
    (
        state_ref,
        levels_ref,
        send_faces_ref,
        send_counts_ref,
        recv_faces_ref,
        recv_orients_ref,
        recv_counts_ref,
        curve_faces_ref,
        curve_orients_ref,
        curve_counts_ref,
        *wide,
    ) = held
    loads = [
        pltpu.make_async_copy(source, target, load_sem.at[at])
        for at, (source, target) in enumerate(zip(given, held))
    ]
    for at in load_order:
        loads[at].start()
    curves, tiles, elements, cap_tile, cap_curve, half_rows = sizes
    block = 2 * half_rows
    tile_rows = tiles * block
    curve_rows = 2 * cap_curve
    b = lax.axis_index("curve")
    t = lax.axis_index("tile")
    to_peer = [lax.rem(t + off, tiles) for off in range(tiles)]
    from_peer = [lax.rem(t + tiles - off, tiles) for off in range(tiles)]
    has_prev = b > 0
    has_next = b < curves - 1

    barrier = pltpu.get_barrier_semaphore()
    for off in range(1, tiles):
        pl.semaphore_signal(barrier, inc=1, device_id=(b, to_peer[off]), device_id_type=MESH)

    @pl.when(has_prev)
    def _():
        pl.semaphore_signal(barrier, inc=1, device_id=(b - 1, t), device_id_type=MESH)

    @pl.when(has_next)
    def _():
        pl.semaphore_signal(barrier, inc=1, device_id=(b + 1, t), device_id_type=MESH)

    @pl.when(jnp.logical_not(has_prev))
    def _():
        curve_in[:, 0] = jnp.zeros_like(curve_in[:, 0])

    @pl.when(jnp.logical_not(has_next))
    def _():
        curve_in[:, 1] = jnp.zeros_like(curve_in[:, 1])

    for at in range(1, 10):
        loads[at].wait()

    def spread_down(live_rows, rows):
        column = jnp.sum(live_rows.astype(jnp.float32), axis=1, keepdims=True)
        return jnp.broadcast_to(column - 1.0, (rows, 128))

    tile_lane = lax.broadcasted_iota(jnp.int32, (block, cap_tile), 1)
    tile_sub = lax.broadcasted_iota(jnp.int32, (block, cap_tile), 0)
    tile_first = tile_sub < half_rows
    tile_own = tile_lane == (tile_sub & (half_rows - 1))

    def tile_key_rows(peer, send_first):
        row = pl.ds(peer, 1)
        sent = send_faces_ref[row, :] * 16 + 1
        got = recv_faces_ref[row, :] * 16 + recv_orients_ref[row, :] + 1
        row_lane = lax.broadcasted_iota(jnp.int32, (1, cap_tile), 1)
        sent = jnp.where(row_lane < send_counts_ref[peer], sent, 0)
        got = jnp.where(row_lane < recv_counts_ref[peer], got, 0)
        pair = (sent, got) if send_first else (got, sent)
        both = jnp.where(tile_first, pair[0], pair[1])
        return spread_down(jnp.where(tile_own, both, 0), block)

    def curve_key_rows(side):
        shape = (cap_curve, cap_curve)
        lane = lax.broadcasted_iota(jnp.int32, shape, 1)
        sub = lax.broadcasted_iota(jnp.int32, shape, 0)
        row = curve_faces_ref[side : side + 1, :] * 16 + curve_orients_ref[side : side + 1, :] + 1
        own = jnp.logical_and(lane == sub, lane < curve_counts_ref[side])
        return spread_down(jnp.where(own, row, 0), cap_curve)

    out_keys = jnp.concatenate([tile_key_rows(p, True) for p in to_peer], axis=0)
    in_keys = jnp.concatenate([tile_key_rows(p, False) for p in from_peer], axis=0)
    rim_keys = jnp.concatenate([curve_key_rows(side) for side in range(2)], axis=0)

    sub_iota = lax.broadcasted_iota(jnp.int32, (8, 128), 0)

    def down_rows(keys):
        return keys.astype(jnp.int32)

    def along_lanes(keys, times):
        count = keys.shape[0]
        width = times * count
        shape = (count, width)
        own = lax.broadcasted_iota(jnp.int32, shape, 1) % count == lax.broadcasted_iota(
            jnp.int32, shape, 0
        )
        wide = jnp.concatenate([keys] * (-(-width // 128)), axis=1)[:, :width]
        value = jnp.sum(jnp.where(own, wide, 0.0), axis=0, keepdims=True)
        return jnp.broadcast_to(value, (elements, width)).astype(jnp.int32)

    def decode(keys, from_send):
        live = keys >= 0
        raw = jnp.maximum(keys, 0) >> 4
        turned = jnp.maximum(keys, 0) & 15
        face_id = jnp.where(from_send, div_five(raw), raw)
        child = raw - 5 * face_id
        element = div_six(face_id)
        face = face_id - 6 * element
        return jnp.where(live, element, -1), face, child, turned

    def half_flags(shape, axis, first):
        at = lax.broadcasted_iota(jnp.int32, shape, axis)
        return (at & (block - 1)) < half_rows if first else (at & (block - 1)) >= half_rows

    lane_t = lax.broadcasted_iota(jnp.int32, (tile_rows, 128), 1)
    low_t = lane_t < 64
    out_is_send = half_flags((tile_rows, 128), 0, True)
    in_is_send = half_flags((tile_rows, 128), 0, False)
    out_elem, out_face, out_child, out_turn = decode(down_rows(out_keys), out_is_send)
    in_elem, in_face, in_child, in_turn = decode(down_rows(in_keys), in_is_send)
    out_y = out_face < 4
    in_y = in_face < 4
    out_code = jnp.where(out_is_send, out_child, 5 + out_turn)
    in_code = jnp.where(in_is_send, 8 + in_child, in_turn)
    upper_t = jnp.where(low_t, 0, 1)
    out_masks = [jnp.where(out_code == 2 * j + upper_t, 1.0, 0.0) for j in range(7)]
    extra_masks = [
        jnp.where(jnp.logical_and(out_is_send, out_code == 2 * j + upper_t), 1.0, 0.0)
        for j in range(2)
    ]
    out_sign = jnp.where(out_is_send, -1.0, 1.0)
    in_sign_half = jnp.where(in_is_send, 0.5, -0.5)
    out_match = low_t == out_y
    in_match = low_t == in_y
    in_low_faces = jnp.where(jnp.logical_and(in_match, jnp.logical_not(in_is_send)), 1.0, 0.0)
    in_high_faces = jnp.where(jnp.logical_and(in_match, in_is_send), 1.0, 0.0)
    out_high_faces = jnp.where(jnp.logical_and(out_match, out_is_send), 1.0, 0.0)

    rim_row = lax.broadcasted_iota(jnp.int32, (curve_rows, 128), 0)
    lane_c = lax.broadcasted_iota(jnp.int32, (curve_rows, 128), 1)
    low_c = lane_c < 64
    rim_elem, _, _, rim_turn = decode(down_rows(rim_keys), rim_row < 0)
    rim_first = rim_row < cap_curve
    rim_match = low_c == rim_first
    rim_sign = jnp.where(rim_first, 1.0, -1.0)
    both_codes = jnp.concatenate([in_code, rim_turn], axis=0)
    upper_b = jnp.where(lax.broadcasted_iota(jnp.int32, both_codes.shape, 1) < 64, 0, 1)
    both_masks = [jnp.where(both_codes == 2 * j + upper_b, 1.0, 0.0) for j in range(7)]
    rim_place = jnp.where(rim_match, 1.0, 0.0)

    def one_hot(flags):
        return jnp.where(flags, 1.0, 0.0).astype(half_type)

    gather_lane = lax.broadcasted_iota(jnp.int32, (tile_rows, 2 * elements), 1) % elements
    out_gather = one_hot(gather_lane == out_elem[:, : 2 * elements])
    rim_lane = lax.broadcasted_iota(jnp.int32, (curve_rows, 2 * elements), 1) % elements
    rim_gather = one_hot(rim_lane == rim_elem[:, : 2 * elements])

    lane_shape = (elements, 4 * tile_rows)
    lane_s = lax.broadcasted_iota(jnp.int32, lane_shape, 1)
    in_part = lane_s < 2 * tile_rows
    first_half = (lane_s & (block - 1)) < half_rows
    lane_from_send = first_half != in_part
    t_elem, t_face, _, _ = decode(
        jnp.where(in_part, along_lanes(in_keys, 4), along_lanes(out_keys, 4)), lane_from_send
    )
    t_hit = t_elem == lax.broadcasted_iota(jnp.int32, lane_shape, 0)
    tile_scatter = one_hot(t_hit)
    rim_shape = (elements, 2 * curve_rows)
    c_elem, c_face, _, _ = decode(
        along_lanes(rim_keys, 2), lax.broadcasted_iota(jnp.int32, rim_shape, 1) < 0
    )
    c_hit = c_elem == lax.broadcasted_iota(jnp.int32, rim_shape, 0)
    rim_scatter = one_hot(c_hit)

    def any_lane(flags):
        return jnp.max(jnp.where(flags, 1.0, 0.0), axis=1, keepdims=True)

    listed = [any_lane(jnp.logical_and(c_hit, c_face == f)) for f in (0, 1)]
    listed += [any_lane(jnp.logical_and(t_hit, t_face == f)) for f in (2, 3, 4, 5)]

    scale_blocks = []
    for start in range(0, elements, 8):
        value = jnp.zeros((8, 128), jnp.int32)
        for at in range(8):
            value = jnp.where(sub_iota == at, jnp.int32(1) << levels_ref[start + at], value)
        scale_blocks.append(value.astype(jnp.float32))
    scale = jnp.concatenate(scale_blocks, axis=0)
    scale = jnp.concatenate([scale] * 4, axis=1)
    vol_scale = scale * (-time_step)
    lift = scale * (28.0 * time_step)

    node = lax.broadcasted_iota(jnp.int32, (elements, 512), 1)
    vel_to_sum = []
    pres_to_vel = []
    own_damp = []
    side_damp = []
    for dim in range(3):
        place = (node >> (6 - 3 * dim)) & 7
        low_end = place == 0
        high_end = place == 7
        on_face = jnp.logical_or(low_end, high_end)
        known = jnp.where(low_end, listed[2 * dim], listed[2 * dim + 1])
        strong = jnp.where(on_face, lift * (1.0 - 0.5 * known), 0.0)
        weak = jnp.where(on_face, lift * (0.5 * known), 0.0)
        vel_to_sum.append(jnp.where(low_end, -strong, strong))
        pres_to_vel.append(jnp.where(low_end, -weak, weak))
        own_damp.append(strong)
        side_damp.append(weak)
    total_damp = side_damp[0] + side_damp[1] + side_damp[2]
    vel_damp = [own_damp[d] + (total_damp - side_damp[d]) for d in range(3)]

    def prepare(at):
        loads[10 + at].wait()
        value = wide[at][...]
        high, low = split(value)
        if at < 2:
            ready[at][...] = high
        elif at < 4:
            ready[at][...] = jnp.concatenate([high, high, low, jnp.zeros_like(low)], axis=0)
        else:
            ready[at][...] = jnp.concatenate([high, low], axis=0)

    def tile_copies(stage):
        return [
            pltpu.make_async_remote_copy(
                src_ref=tile_out.at[stage, off],
                dst_ref=tile_in.at[stage, off],
                send_sem=tile_send_sem.at[stage, off],
                recv_sem=tile_recv_sem.at[stage, off],
                device_id=(b, to_peer[off]),
                device_id_type=MESH,
            )
            for off in range(1, tiles)
        ]

    def curve_copy(stage, side):
        return pltpu.make_async_remote_copy(
            src_ref=curve_out.at[stage, side],
            dst_ref=curve_in.at[stage, 1 - side],
            send_sem=curve_send_sem.at[stage, side],
            recv_sem=curve_recv_sem.at[stage, 1 - side],
            device_id=(b - 1 + 2 * side, t),
            device_id_type=MESH,
        )

    def packed(first, second, low):
        return jnp.where(low, first, second)

    def pair_rows(value, low):
        high = value.astype(half_type).astype(jnp.float32)
        return jnp.concatenate([jnp.where(low, high, value - high), high], axis=1).astype(half_type)

    def rates(current, stage):
        parts = [split(value) for value in current]
        highs = [part[0] for part in parts]
        lows = [part[1] for part in parts]

        if stage == 0:
            prepare(0)
            prepare(2)
        low_e = lax.broadcasted_iota(jnp.int32, (elements, 128), 1) < 64
        ends = [split(jnp.where(low_e, v[:, :128], v[:, 384:])) for v in current]
        ends = jnp.concatenate([jnp.concatenate(e, axis=0) for e in ends], axis=1)
        rim = dot(rim_gather, ends)
        traces = dot(jnp.concatenate(highs + lows, axis=0), pick_ref[...]).astype(half_type)
        rim_vals = []
        for f in range(5):
            kept = jnp.where(rim_match, rim[:, 128 * f : 128 * f + 128], 0.0)
            rim_vals.append(kept + swap_halves(kept))
        sum_part = rim_sign * rim_vals[1] - rim_vals[0]
        vel_part = rim_sign * rim_vals[4] - rim_vals[1]
        rim_send = jnp.concatenate(
            [packed(sum_part, vel_part, low_c), packed(rim_vals[2], rim_vals[3], low_c)], axis=1
        )
        curve_out[stage] = rim_send.reshape(2, cap_curve, 256)
        if stage == 0:
            pl.semaphore_wait(
                barrier, tiles - 1 + has_prev.astype(jnp.int32) + has_next.astype(jnp.int32)
            )

        @pl.when(has_prev)
        def _():
            curve_copy(stage, 0).start()

        @pl.when(has_next)
        def _():
            curve_copy(stage, 1).start()

        columns = []
        for f in range(5):
            at = f * elements
            low_at = (5 + f) * elements
            columns.append(
                jnp.concatenate(
                    [traces[at : at + elements], traces[low_at : low_at + elements]], axis=0
                )
            )
        own = dot(out_gather, jnp.concatenate(columns, axis=1))
        own_rows = []
        for f in range(5):
            side = jnp.where(
                out_is_send, own[:, 256 * f + 128 : 256 * f + 256], own[:, 256 * f : 256 * f + 128]
            )
            kept = jnp.where(out_match, side, 0.0)
            own_rows.append(pair_rows(kept + swap_halves(kept), low_t))
        coded = dot(jnp.concatenate(own_rows, axis=0), send_mat_ref[...])

        def choose(source, rows_at, rows, masks, first):
            total = None
            for j, mask in enumerate(masks):
                at = 128 * (first + j)
                term = mask * source[rows_at : rows_at + rows, at : at + 128]
                total = term if total is None else total + term
            return total + swap_halves(total)

        mortar = [choose(coded, f * tile_rows, tile_rows, out_masks, 0) for f in range(5)]
        normal = jnp.where(out_y, mortar[2], mortar[3])
        other = jnp.where(out_y, mortar[3], mortar[2])
        sum_part = out_sign * normal - mortar[0]
        vel_part = out_sign * mortar[4] - normal
        tile_send = jnp.concatenate(
            [packed(sum_part, vel_part, low_t), packed(mortar[1], other, low_t)], axis=1
        )
        tile_send = tile_send.reshape(tiles, block, 256)
        tile_out[stage] = tile_send
        tile_in[stage, 0] = tile_send[0]
        copies = tile_copies(stage)
        for copy in copies:
            copy.start()

        rest = [choose(coded, f * tile_rows, tile_rows, extra_masks, 7) for f in range(5)]
        rest_n = jnp.where(out_y, rest[2], rest[3])
        rest_o = jnp.where(out_y, rest[3], rest[2])
        rest_p = 0.5 * (rest[4] + rest_n)
        rest_n = 0.5 * (rest_n + rest[4])
        rest_o = 0.5 * rest_o
        rest_fields = [
            0.5 * (rest[0] + jnp.where(out_y, rest[2], rest[3])),
            0.5 * rest[1],
            jnp.where(out_y, rest_n, rest_o),
            jnp.where(out_y, rest_o, rest_n),
            rest_p,
        ]
        rest_parts = [split(value * out_high_faces) for value in rest_fields]

        if stage == 0:
            prepare(4)
            prepare(5)
            prepare(6)
        grad = dot(
            jnp.concatenate([highs[1], highs[4], lows[1], lows[4]], axis=0), along_x_ref[:512]
        )
        n2 = 2 * elements
        grad_x = grad[:n2] + grad[n2:]
        grad_x = grad_x + dot(jnp.concatenate([highs[1], highs[4]], axis=0), along_x_ref[512:])

        def halves(f, source):
            return [source[f][:, :256], source[f][:, 256:]]

        def banded(f, mat_ref):
            high_rows = jnp.concatenate(halves(f, highs) + halves(4, highs), axis=0)
            low_rows = jnp.concatenate(halves(f, lows) + halves(4, lows), axis=0)
            first = dot(jnp.concatenate([high_rows, low_rows], axis=0), mat_ref[:256])
            n4 = 4 * elements
            total = first[:n4] + first[n4:] + dot(high_rows, mat_ref[256:])
            vel = jnp.concatenate([total[:elements], total[elements:n2]], axis=1)
            pres = jnp.concatenate([total[n2 : 3 * elements], total[3 * elements :]], axis=1)
            return vel, pres

        vel_y, pres_y = banded(2, along_y_ref)
        vel_z, pres_z = banded(3, along_z_ref)
        diverge = vol_scale * (grad_x[:elements] + vel_y + vel_z)
        to_sum = diverge
        for d in range(3):
            to_sum = to_sum + vel_to_sum[d] * current[1 + d]
        pres_grads = (grad_x[elements:], pres_y, pres_z)
        result = [to_sum - total_damp * current[0]]
        for d in range(3):
            result.append(
                vol_scale * pres_grads[d]
                + pres_to_vel[d] * current[4]
                - vel_damp[d] * current[1 + d]
            )
        result.append(to_sum - total_damp * current[4])

        if stage == 0:
            prepare(3)
            prepare(1)

        @pl.when(has_prev)
        def _():
            curve_copy(stage, 1).wait_recv()

        @pl.when(has_next)
        def _():
            curve_copy(stage, 0).wait_recv()

        for copy in copies:
            copy.wait_recv()

        arrived = jnp.concatenate(
            [
                tile_in[stage].reshape(tile_rows, 256),
                curve_in[stage].reshape(curve_rows, 256),
            ],
            axis=0,
        )
        rows = tile_rows + curve_rows
        low_b = lax.broadcasted_iota(jnp.int32, (rows, 128), 1) < 64
        fields = []
        for at in range(2):
            value = arrived[:, 128 * at : 128 * at + 128]
            turned = swap_halves(value)
            fields.append(pair_rows(jnp.where(low_b, value, turned), low_b))
            fields.append(pair_rows(jnp.where(low_b, turned, value), low_b))
        taken = dot(jnp.concatenate(fields, axis=0), take_mat_ref[...])
        chosen = [choose(taken, f * rows, rows, both_masks, 0) for f in range(4)]

        rim_in = [value[tile_rows:] * rim_place for value in chosen]
        rim_cols = [jnp.concatenate(split(value), axis=0) for value in rim_in]
        placed = dot(rim_scatter, jnp.concatenate(rim_cols, axis=1))
        place_sum = -0.5 * placed[:, :128]
        place_vel = -0.5 * placed[:, 128:256]
        place_pres = jnp.where(low_e, place_vel, -place_vel)
        rim_fields = [
            place_sum,
            place_vel,
            0.5 * placed[:, 256:384],
            0.5 * placed[:, 384:512],
            place_pres,
        ]

        tile_vals = [value[:tile_rows] for value in chosen]
        put_sum = -0.5 * tile_vals[0]
        put_n = -0.5 * tile_vals[1]
        put_o = 0.5 * tile_vals[3]
        put = [
            put_sum,
            0.5 * tile_vals[2],
            jnp.where(in_y, put_n, put_o),
            jnp.where(in_y, put_o, put_n),
            in_sign_half * tile_vals[1],
        ]
        zero_part = jnp.zeros((tile_rows, 128), half_type)
        columns = []
        for f in range(5):
            first = split(put[f] * in_low_faces)
            second = split(put[f] * in_high_faces)
            high, low = rest_parts[f]
            columns.append(jnp.concatenate([first[0], first[1], zero_part, zero_part], axis=0))
            columns.append(jnp.concatenate([second[0], second[1], high, low], axis=0))
        on_faces = dot(tile_scatter, jnp.concatenate(columns, axis=1))
        face_parts = [split(on_faces[:, 256 * f : 256 * f + 256]) for f in range(5)]
        spread = dot(
            jnp.concatenate([p[0] for p in face_parts] + [p[1] for p in face_parts], axis=0),
            spread_ref[...],
        )
        finished = []
        zero_middle = jnp.zeros((elements, 256), jnp.float32)
        for f in range(5):
            at = f * elements
            low_at = (5 + f) * elements
            nodes = spread[at : at + elements] + spread[low_at : low_at + elements]
            rim_nodes = jnp.concatenate(
                [
                    jnp.where(low_e, rim_fields[f], 0.0),
                    zero_middle,
                    jnp.where(low_e, 0.0, rim_fields[f]),
                ],
                axis=1,
            )
            finished.append(result[f] + lift * (nodes + rim_nodes))
        return finished

    loads[0].wait()
    held_state[...] = state_ref[...]

    for stage in range(3):
        current = [held_state[f] for f in range(5)]
        change = rates(current, stage)
        for f in range(5):
            moved = held_state[f] + change[f]
            if stage == 0:
                held_state[f] = moved
            elif stage == 1:
                held_state[f] = 0.75 * state_ref[f] + 0.25 * moved
            else:
                out_ref[f] = state_ref[f] / 3.0 + (2.0 / 3.0) * moved
    for stage in range(3):
        for copy in tile_copies(stage):
            copy.wait_send()

    @pl.when(has_prev)
    def _():
        for stage in range(3):
            curve_copy(stage, 0).wait_send()

    @pl.when(has_next)
    def _():
        for stage in range(3):
            curve_copy(stage, 1).wait_send()


def shards(
    state,
    levels,
    send_faces,
    send_counts,
    recv_faces,
    recv_orients,
    recv_counts,
    curve_faces,
    curve_orients,
    curve_counts,
):
    curves = lax.axis_size("curve")
    tiles, cap_tile = send_faces.shape
    cap_curve = curve_faces.shape[1]
    elements = state.shape[1]
    half_rows = -(-cap_tile // 4) * 4
    sizes = (curves, tiles, elements, cap_tile, cap_curve, half_rows)
    block = 2 * half_rows
    operands = [
        state,
        levels,
        send_faces,
        send_counts,
        recv_faces,
        recv_orients,
        recv_counts,
        curve_faces,
        curve_orients,
        curve_counts,
        *tables(),
    ]
    held = [
        pltpu.SMEM(value.shape, value.dtype)
        if value.ndim == 1
        else pltpu.VMEM(value.shape, value.dtype)
        for value in operands
    ]
    return pl.pallas_call(
        functools.partial(section_kernel, sizes),
        out_shape=pltpu.VMEM(state.shape, state.dtype),
        in_specs=[pl.BlockSpec(memory_space=pl.ANY)] * operand_count,
        out_specs=pl.BlockSpec(memory_space=pltpu.VMEM),
        scratch_shapes=held
        + [
            pltpu.VMEM((3, tiles, block, 256), jnp.float32),
            pltpu.VMEM((3, tiles, block, 256), jnp.float32),
            pltpu.VMEM((3, 2, cap_curve, 256), jnp.float32),
            pltpu.VMEM((3, 2, cap_curve, 256), jnp.float32),
            pltpu.SemaphoreType.DMA((3, tiles)),
            pltpu.SemaphoreType.DMA((3, tiles)),
            pltpu.SemaphoreType.DMA((3, 2)),
            pltpu.SemaphoreType.DMA((3, 2)),
            pltpu.SemaphoreType.DMA((operand_count,)),
            pltpu.VMEM(state.shape, jnp.float32),
        ]
        + [
            pltpu.VMEM((value.shape[0] * times, value.shape[1]), half_type)
            for value, times in zip(operands[10:], (1, 1, 4, 4, 2, 2, 2))
        ],
        compiler_params=pltpu.CompilerParams(
            collective_id=0, has_side_effects=True, vmem_limit_bytes=60 * 1024 * 1024
        ),
    )(*operands)


def solution(mesh):
    return jax.shard_map(
        shards,
        mesh=mesh,
        in_specs=(
            P(None, ("curve", "tile"), None),
            P(("curve", "tile")),
            P(("curve", "tile"), None),
            P(("curve", "tile")),
            P(("curve", "tile"), None),
            P(("curve", "tile"), None),
            P(("curve", "tile")),
            P(("curve", "tile"), None),
            P(("curve", "tile"), None),
            P(("curve", "tile")),
        ),
        out_specs=P(None, ("curve", "tile"), None),
        check_vma=False,
    )
```

```python
import functools

import jax
import jax.numpy as jnp
import ml_dtypes
import numpy as np
from jax import lax
from jax.experimental import pallas as pl
from jax.experimental.pallas import tpu as pltpu
from jax.sharding import PartitionSpec as P

time_step = 0.002
half_type = jnp.bfloat16
MESH = pl.DeviceIdType.MESH
operand_count = 17
load_order = [0, 2, 4, 5, 3, 6, 7, 8, 9, 1, 10, 12, 14, 15, 16, 13, 11]
inner_nodes = [
    -0.8717401485096066,
    -0.5917001814331423,
    -0.20929921790247888,
    0.20929921790247888,
    0.5917001814331423,
    0.8717401485096066,
]


def legendre_seven(abscissa):
    before = abscissa * 0.0 + 1.0
    current = abscissa + 0.0
    for order in range(1, 7):
        before, current = (
            current,
            ((2 * order + 1) * abscissa * current - order * before) / (order + 1),
        )
    return current


def tables():
    points = np.array([-1.0] + inner_nodes + [1.0])
    values = legendre_seven(points)
    weights = 2.0 / (56 * values**2)
    deriv = np.zeros((8, 8))
    for row in range(8):
        for col in range(8):
            if row != col:
                deriv[row, col] = values[row] / (values[col] * (points[row] - points[col]))
    deriv[0, 0] = -14.0
    deriv[7, 7] = 14.0
    halves = []
    projections = []
    for side in range(2):
        targets = (points + 2.0 * side - 1.0) / 2.0
        interp = np.ones((8, 8))
        for col in range(8):
            for other in range(8):
                if other != col:
                    interp[:, col] *= (targets - points[other]) / (points[col] - points[other])
        halves.append(interp)
        projections.append(0.5 * (interp.T * weights[None, :]) / weights[:, None])
    pairs = [(a, b) for a in range(2) for b in range(2)]
    mortar = [np.kron(halves[a], halves[b]) for a, b in pairs]
    project = [np.kron(projections[a], projections[b]) for a, b in pairs]
    turn = np.zeros((8, 64, 64))
    for code in range(8):
        for s in range(8):
            for t in range(8):
                a, c = (t, s) if code & 4 else (s, t)
                a = 7 - a if code & 1 else a
                c = 7 - c if code & 2 else c
                turn[code, 8 * s + t, 8 * a + c] = 1.0
    eye = np.eye(64)
    send = mortar + [eye] + [turn[o].T for o in range(8)] + [np.zeros((64, 64))]
    send += [0.25 * eye - q @ m for q, m in zip(project, mortar)]
    take = [turn[o] for o in range(8)] + project + [eye, np.zeros((64, 64))]

    pick = np.zeros((512, 256))
    for s in range(8):
        for t in range(8):
            column = 8 * s + t
            pick[64 * s + t, column] = 1.0
            pick[64 * s + 8 * t, 64 + column] = 1.0
            pick[64 * s + 56 + t, 128 + column] = 1.0
            pick[64 * s + 8 * t + 7, 192 + column] = 1.0
    def parts(matrix):
        high = matrix.astype(ml_dtypes.bfloat16)
        low = (matrix - high.astype(np.float64)).astype(ml_dtypes.bfloat16)
        return high, low

    def stacked(mats):
        high, low = parts(np.concatenate([m.T for m in mats], axis=1))
        return np.concatenate([high, high, low, np.zeros_like(low)], axis=0)

    return [
        jnp.asarray(m.astype(ml_dtypes.bfloat16))
        for m in (
            pick,
            pick.T,
            stacked(send),
            stacked(take),
            np.concatenate(parts(np.kron(deriv.T, np.eye(64))), axis=0),
            np.concatenate(parts(np.kron(np.eye(4), np.kron(deriv.T, np.eye(8)))), axis=0),
            np.concatenate(parts(np.kron(np.eye(32), deriv.T)), axis=0),
        )
    ]


def dot(left, right):
    return jnp.dot(left, right, preferred_element_type=jnp.float32)


def split(value):
    high = value.astype(half_type)
    return high, (value - high.astype(jnp.float32)).astype(half_type)


def div_five(value):
    return (value * 52429) >> 18


def div_six(value):
    return (value * 43691) >> 18


def swap_halves(value):
    return pltpu.roll(value, 64, axis=1)


def section_kernel(
    sizes,
    *refs,
):
    given = refs[:operand_count]
    out_ref = refs[operand_count]
    held = refs[operand_count + 1 : 2 * operand_count + 1]
    (
        tile_out,
        tile_in,
        curve_out,
        curve_in,
        tile_send_sem,
        tile_recv_sem,
        curve_send_sem,
        curve_recv_sem,
        load_sem,
        held_state,
    ) = refs[2 * operand_count + 1 :]
    (
        state_ref,
        levels_ref,
        send_faces_ref,
        send_counts_ref,
        recv_faces_ref,
        recv_orients_ref,
        recv_counts_ref,
        curve_faces_ref,
        curve_orients_ref,
        curve_counts_ref,
        pick_ref,
        spread_ref,
        send_mat_ref,
        take_mat_ref,
        along_x_ref,
        along_y_ref,
        along_z_ref,
    ) = held
    loads = [
        pltpu.make_async_copy(source, target, load_sem.at[at])
        for at, (source, target) in enumerate(zip(given, held))
    ]
    for at in load_order:
        loads[at].start()
    curves, tiles, elements, cap_tile, cap_curve, half_rows = sizes
    block = 2 * half_rows
    tile_rows = tiles * block
    curve_rows = 2 * cap_curve
    b = lax.axis_index("curve")
    t = lax.axis_index("tile")
    to_peer = [lax.rem(t + off, tiles) for off in range(tiles)]
    from_peer = [lax.rem(t + tiles - off, tiles) for off in range(tiles)]
    has_prev = b > 0
    has_next = b < curves - 1

    barrier = pltpu.get_barrier_semaphore()
    for off in range(1, tiles):
        pl.semaphore_signal(barrier, inc=1, device_id=(b, to_peer[off]), device_id_type=MESH)

    @pl.when(has_prev)
    def _():
        pl.semaphore_signal(barrier, inc=1, device_id=(b - 1, t), device_id_type=MESH)

    @pl.when(has_next)
    def _():
        pl.semaphore_signal(barrier, inc=1, device_id=(b + 1, t), device_id_type=MESH)

    @pl.when(jnp.logical_not(has_prev))
    def _():
        curve_in[:, 0] = jnp.zeros_like(curve_in[:, 0])

    @pl.when(jnp.logical_not(has_next))
    def _():
        curve_in[:, 1] = jnp.zeros_like(curve_in[:, 1])

    for at in range(1, 10):
        loads[at].wait()

    def spread_down(live_rows, rows):
        column = jnp.sum(live_rows.astype(jnp.float32), axis=1, keepdims=True)
        return jnp.broadcast_to(column - 1.0, (rows, 128))

    tile_lane = lax.broadcasted_iota(jnp.int32, (block, cap_tile), 1)
    tile_sub = lax.broadcasted_iota(jnp.int32, (block, cap_tile), 0)
    tile_first = tile_sub < half_rows
    tile_own = tile_lane == (tile_sub & (half_rows - 1))

    def tile_key_rows(peer, send_first):
        row = pl.ds(peer, 1)
        sent = send_faces_ref[row, :] * 16 + 1
        got = recv_faces_ref[row, :] * 16 + recv_orients_ref[row, :] + 1
        row_lane = lax.broadcasted_iota(jnp.int32, (1, cap_tile), 1)
        sent = jnp.where(row_lane < send_counts_ref[peer], sent, 0)
        got = jnp.where(row_lane < recv_counts_ref[peer], got, 0)
        pair = (sent, got) if send_first else (got, sent)
        both = jnp.where(tile_first, pair[0], pair[1])
        return spread_down(jnp.where(tile_own, both, 0), block)

    def curve_key_rows(side):
        shape = (cap_curve, cap_curve)
        lane = lax.broadcasted_iota(jnp.int32, shape, 1)
        sub = lax.broadcasted_iota(jnp.int32, shape, 0)
        row = curve_faces_ref[side : side + 1, :] * 16 + curve_orients_ref[side : side + 1, :] + 1
        own = jnp.logical_and(lane == sub, lane < curve_counts_ref[side])
        return spread_down(jnp.where(own, row, 0), cap_curve)

    out_keys = jnp.concatenate([tile_key_rows(p, True) for p in to_peer], axis=0)
    in_keys = jnp.concatenate([tile_key_rows(p, False) for p in from_peer], axis=0)
    rim_keys = jnp.concatenate([curve_key_rows(side) for side in range(2)], axis=0)

    sub_iota = lax.broadcasted_iota(jnp.int32, (8, 128), 0)

    def down_rows(keys):
        return keys.astype(jnp.int32)

    def along_lanes(keys, times):
        count = keys.shape[0]
        width = times * count
        shape = (count, width)
        own = lax.broadcasted_iota(jnp.int32, shape, 1) % count == lax.broadcasted_iota(
            jnp.int32, shape, 0
        )
        wide = jnp.concatenate([keys] * (-(-width // 128)), axis=1)[:, :width]
        value = jnp.sum(jnp.where(own, wide, 0.0), axis=0, keepdims=True)
        return jnp.broadcast_to(value, (elements, width)).astype(jnp.int32)

    def decode(keys, from_send):
        live = keys >= 0
        raw = jnp.maximum(keys, 0) >> 4
        turned = jnp.maximum(keys, 0) & 15
        face_id = jnp.where(from_send, div_five(raw), raw)
        child = raw - 5 * face_id
        element = div_six(face_id)
        face = face_id - 6 * element
        return jnp.where(live, element, -1), face, child, turned

    def half_flags(shape, axis, first):
        at = lax.broadcasted_iota(jnp.int32, shape, axis)
        return (at & (block - 1)) < half_rows if first else (at & (block - 1)) >= half_rows

    lane_t = lax.broadcasted_iota(jnp.int32, (tile_rows, 128), 1)
    low_t = lane_t < 64
    out_is_send = half_flags((tile_rows, 128), 0, True)
    in_is_send = half_flags((tile_rows, 128), 0, False)
    out_elem, out_face, out_child, out_turn = decode(down_rows(out_keys), out_is_send)
    in_elem, in_face, in_child, in_turn = decode(down_rows(in_keys), in_is_send)
    out_y = out_face < 4
    in_y = in_face < 4
    out_code = jnp.where(out_is_send, out_child, 5 + out_turn)
    in_code = jnp.where(in_is_send, 8 + in_child, in_turn)
    upper_t = jnp.where(low_t, 0, 1)
    out_masks = [jnp.where(out_code == 2 * j + upper_t, 1.0, 0.0) for j in range(7)]
    extra_masks = [
        jnp.where(jnp.logical_and(out_is_send, out_code == 2 * j + upper_t), 1.0, 0.0)
        for j in range(2)
    ]
    out_sign = jnp.where(out_is_send, -1.0, 1.0)
    in_sign_half = jnp.where(in_is_send, 0.5, -0.5)
    out_match = low_t == out_y
    in_match = low_t == in_y
    in_low_faces = jnp.where(jnp.logical_and(in_match, jnp.logical_not(in_is_send)), 1.0, 0.0)
    in_high_faces = jnp.where(jnp.logical_and(in_match, in_is_send), 1.0, 0.0)
    out_high_faces = jnp.where(jnp.logical_and(out_match, out_is_send), 1.0, 0.0)

    rim_row = lax.broadcasted_iota(jnp.int32, (curve_rows, 128), 0)
    lane_c = lax.broadcasted_iota(jnp.int32, (curve_rows, 128), 1)
    low_c = lane_c < 64
    rim_elem, _, _, rim_turn = decode(down_rows(rim_keys), rim_row < 0)
    rim_first = rim_row < cap_curve
    rim_match = low_c == rim_first
    rim_sign = jnp.where(rim_first, 1.0, -1.0)
    upper_c = jnp.where(low_c, 0, 1)
    in_masks = [jnp.where(in_code == 2 * j + upper_t, 1.0, 0.0) for j in range(7)]
    rim_masks = [jnp.where(rim_turn == 2 * j + upper_c, 1.0, 0.0) for j in range(4)]
    rim_place = jnp.where(rim_match, 1.0, 0.0)

    def one_hot(flags):
        return jnp.where(flags, 1.0, 0.0).astype(half_type)

    gather_lane = lax.broadcasted_iota(jnp.int32, (tile_rows, 2 * elements), 1) % elements
    out_gather = one_hot(gather_lane == out_elem[:, : 2 * elements])
    rim_lane = lax.broadcasted_iota(jnp.int32, (curve_rows, 2 * elements), 1) % elements
    rim_gather = one_hot(rim_lane == rim_elem[:, : 2 * elements])

    lane_shape = (elements, 4 * tile_rows)
    lane_s = lax.broadcasted_iota(jnp.int32, lane_shape, 1)
    in_part = lane_s < 2 * tile_rows
    first_half = (lane_s & (block - 1)) < half_rows
    lane_from_send = first_half != in_part
    t_elem, t_face, _, _ = decode(
        jnp.where(in_part, along_lanes(in_keys, 4), along_lanes(out_keys, 4)), lane_from_send
    )
    t_hit = t_elem == lax.broadcasted_iota(jnp.int32, lane_shape, 0)
    tile_scatter = one_hot(t_hit)
    rim_shape = (elements, 2 * curve_rows)
    c_elem, c_face, _, _ = decode(
        along_lanes(rim_keys, 2), lax.broadcasted_iota(jnp.int32, rim_shape, 1) < 0
    )
    c_hit = c_elem == lax.broadcasted_iota(jnp.int32, rim_shape, 0)
    rim_scatter = one_hot(c_hit)

    def any_lane(flags):
        return jnp.max(jnp.where(flags, 1.0, 0.0), axis=1, keepdims=True)

    listed = [any_lane(jnp.logical_and(c_hit, c_face == f)) for f in (0, 1)]
    listed += [any_lane(jnp.logical_and(t_hit, t_face == f)) for f in (2, 3, 4, 5)]

    scale_blocks = []
    for start in range(0, elements, 8):
        value = jnp.zeros((8, 128), jnp.int32)
        for at in range(8):
            value = jnp.where(sub_iota == at, jnp.int32(1) << levels_ref[start + at], value)
        scale_blocks.append(value.astype(jnp.float32))
    scale = jnp.concatenate(scale_blocks, axis=0)
    scale = jnp.concatenate([scale] * 4, axis=1)
    vol_scale = scale * (-time_step)
    lift = scale * (28.0 * time_step)

    node = lax.broadcasted_iota(jnp.int32, (elements, 512), 1)
    vel_to_sum = []
    pres_to_vel = []
    own_damp = []
    side_damp = []
    for dim in range(3):
        place = (node >> (6 - 3 * dim)) & 7
        low_end = place == 0
        high_end = place == 7
        on_face = jnp.logical_or(low_end, high_end)
        known = jnp.where(low_end, listed[2 * dim], listed[2 * dim + 1])
        strong = jnp.where(on_face, lift * (1.0 - 0.5 * known), 0.0)
        weak = jnp.where(on_face, lift * (0.5 * known), 0.0)
        vel_to_sum.append(jnp.where(low_end, -strong, strong))
        pres_to_vel.append(jnp.where(low_end, -weak, weak))
        own_damp.append(strong)
        side_damp.append(weak)
    total_damp = side_damp[0] + side_damp[1] + side_damp[2]
    vel_damp = [own_damp[d] + (total_damp - side_damp[d]) for d in range(3)]

    def tile_copies(stage):
        return [
            pltpu.make_async_remote_copy(
                src_ref=tile_out.at[stage, off],
                dst_ref=tile_in.at[stage, off],
                send_sem=tile_send_sem.at[stage, off],
                recv_sem=tile_recv_sem.at[stage, off],
                device_id=(b, to_peer[off]),
                device_id_type=MESH,
            )
            for off in range(1, tiles)
        ]

    def curve_copy(stage, side):
        return pltpu.make_async_remote_copy(
            src_ref=curve_out.at[stage, side],
            dst_ref=curve_in.at[stage, 1 - side],
            send_sem=curve_send_sem.at[stage, side],
            recv_sem=curve_recv_sem.at[stage, 1 - side],
            device_id=(b - 1 + 2 * side, t),
            device_id_type=MESH,
        )

    def packed(first, second, low):
        return jnp.where(low, first, second)

    def pair_rows(value, low):
        high = value.astype(half_type).astype(jnp.float32)
        return jnp.concatenate([jnp.where(low, high, value - high), high], axis=1).astype(half_type)

    def rates(current, stage):
        parts = [split(value) for value in current]
        highs = [part[0] for part in parts]
        lows = [part[1] for part in parts]

        if stage == 0:
            loads[10].wait()
            loads[12].wait()
        low_e = lax.broadcasted_iota(jnp.int32, (elements, 128), 1) < 64
        ends = [split(jnp.where(low_e, v[:, :128], v[:, 384:])) for v in current]
        ends = jnp.concatenate([jnp.concatenate(e, axis=0) for e in ends], axis=1)
        rim = dot(rim_gather, ends)
        traces = dot(jnp.concatenate(highs + lows, axis=0), pick_ref[...]).astype(half_type)
        rim_vals = []
        for f in range(5):
            kept = jnp.where(rim_match, rim[:, 128 * f : 128 * f + 128], 0.0)
            rim_vals.append(kept + swap_halves(kept))
        sum_part = rim_sign * rim_vals[1] - rim_vals[0]
        vel_part = rim_sign * rim_vals[4] - rim_vals[1]
        rim_send = jnp.concatenate(
            [packed(sum_part, vel_part, low_c), packed(rim_vals[2], rim_vals[3], low_c)], axis=1
        )
        curve_out[stage] = rim_send.reshape(2, cap_curve, 256)
        if stage == 0:
            pl.semaphore_wait(
                barrier, tiles - 1 + has_prev.astype(jnp.int32) + has_next.astype(jnp.int32)
            )

        @pl.when(has_prev)
        def _():
            curve_copy(stage, 0).start()

        @pl.when(has_next)
        def _():
            curve_copy(stage, 1).start()

        columns = []
        for f in range(5):
            at = f * elements
            low_at = (5 + f) * elements
            columns.append(
                jnp.concatenate(
                    [traces[at : at + elements], traces[low_at : low_at + elements]], axis=0
                )
            )
        own = dot(out_gather, jnp.concatenate(columns, axis=1))
        own_rows = []
        for f in range(5):
            side = jnp.where(
                out_is_send, own[:, 256 * f + 128 : 256 * f + 256], own[:, 256 * f : 256 * f + 128]
            )
            kept = jnp.where(out_match, side, 0.0)
            own_rows.append(pair_rows(kept + swap_halves(kept), low_t))
        coded = dot(jnp.concatenate(own_rows, axis=0), send_mat_ref[...])

        def choose(source, rows_at, rows, masks, first):
            total = None
            for j, mask in enumerate(masks):
                at = 128 * (first + j)
                term = mask * source[rows_at : rows_at + rows, at : at + 128]
                total = term if total is None else total + term
            return total + swap_halves(total)

        mortar = [choose(coded, f * tile_rows, tile_rows, out_masks, 0) for f in range(5)]
        normal = jnp.where(out_y, mortar[2], mortar[3])
        other = jnp.where(out_y, mortar[3], mortar[2])
        sum_part = out_sign * normal - mortar[0]
        vel_part = out_sign * mortar[4] - normal
        tile_send = jnp.concatenate(
            [packed(sum_part, vel_part, low_t), packed(mortar[1], other, low_t)], axis=1
        )
        tile_send = tile_send.reshape(tiles, block, 256)
        tile_out[stage] = tile_send
        tile_in[stage, 0] = tile_send[0]
        copies = tile_copies(stage)
        for copy in copies:
            copy.start()

        rest = [choose(coded, f * tile_rows, tile_rows, extra_masks, 7) for f in range(5)]
        rest_n = jnp.where(out_y, rest[2], rest[3])
        rest_o = jnp.where(out_y, rest[3], rest[2])
        rest_p = 0.5 * (rest[4] + rest_n)
        rest_n = 0.5 * (rest_n + rest[4])
        rest_o = 0.5 * rest_o
        rest_fields = [
            0.5 * (rest[0] + jnp.where(out_y, rest[2], rest[3])),
            0.5 * rest[1],
            jnp.where(out_y, rest_n, rest_o),
            jnp.where(out_y, rest_o, rest_n),
            rest_p,
        ]
        rest_parts = [split(value * out_high_faces) for value in rest_fields]

        if stage == 0:
            loads[14].wait()
            loads[15].wait()
            loads[16].wait()
        grad = dot(
            jnp.concatenate([highs[1], highs[4], lows[1], lows[4]], axis=0), along_x_ref[:512]
        )
        n2 = 2 * elements
        grad_x = grad[:n2] + grad[n2:]
        grad_x = grad_x + dot(jnp.concatenate([highs[1], highs[4]], axis=0), along_x_ref[512:])

        def halves(f, source):
            return [source[f][:, :256], source[f][:, 256:]]

        def banded(f, mat_ref):
            high_rows = jnp.concatenate(halves(f, highs) + halves(4, highs), axis=0)
            low_rows = jnp.concatenate(halves(f, lows) + halves(4, lows), axis=0)
            first = dot(jnp.concatenate([high_rows, low_rows], axis=0), mat_ref[:256])
            n4 = 4 * elements
            total = first[:n4] + first[n4:] + dot(high_rows, mat_ref[256:])
            vel = jnp.concatenate([total[:elements], total[elements:n2]], axis=1)
            pres = jnp.concatenate([total[n2 : 3 * elements], total[3 * elements :]], axis=1)
            return vel, pres

        vel_y, pres_y = banded(2, along_y_ref)
        vel_z, pres_z = banded(3, along_z_ref)
        diverge = vol_scale * (grad_x[:elements] + vel_y + vel_z)
        to_sum = diverge
        for d in range(3):
            to_sum = to_sum + vel_to_sum[d] * current[1 + d]
        pres_grads = (grad_x[elements:], pres_y, pres_z)
        result = [to_sum - total_damp * current[0]]
        for d in range(3):
            result.append(
                vol_scale * pres_grads[d]
                + pres_to_vel[d] * current[4]
                - vel_damp[d] * current[1 + d]
            )
        result.append(to_sum - total_damp * current[4])

        if stage == 0:
            loads[13].wait()
            loads[11].wait()

        def take(arrived, rows, low, masks):
            fields = []
            for at in range(2):
                value = arrived[:, 128 * at : 128 * at + 128]
                turned = swap_halves(value)
                fields.append(pair_rows(jnp.where(low, value, turned), low))
                fields.append(pair_rows(jnp.where(low, turned, value), low))
            taken = dot(jnp.concatenate(fields, axis=0), take_mat_ref[:, : 128 * len(masks)])
            return [choose(taken, f * rows, rows, masks, 0) for f in range(4)]

        @pl.when(has_prev)
        def _():
            curve_copy(stage, 1).wait_recv()

        @pl.when(has_next)
        def _():
            curve_copy(stage, 0).wait_recv()

        rim_vals = take(curve_in[stage].reshape(curve_rows, 256), curve_rows, low_c, rim_masks)
        rim_cols = [jnp.concatenate(split(value * rim_place), axis=0) for value in rim_vals]
        placed = dot(rim_scatter, jnp.concatenate(rim_cols, axis=1))
        place_sum = -0.5 * placed[:, :128]
        place_vel = -0.5 * placed[:, 128:256]
        place_pres = jnp.where(low_e, place_vel, -place_vel)
        rim_fields = [
            place_sum,
            place_vel,
            0.5 * placed[:, 256:384],
            0.5 * placed[:, 384:512],
            place_pres,
        ]
        for f in range(5):
            rim_nodes = jnp.concatenate(
                [
                    jnp.where(low_e, rim_fields[f], 0.0),
                    jnp.zeros((elements, 256), jnp.float32),
                    jnp.where(low_e, 0.0, rim_fields[f]),
                ],
                axis=1,
            )
            result[f] = result[f] + lift * rim_nodes

        for copy in copies:
            copy.wait_recv()
        tile_vals = take(tile_in[stage].reshape(tile_rows, 256), tile_rows, low_t, in_masks)

        put_sum = -0.5 * tile_vals[0]
        put_n = -0.5 * tile_vals[1]
        put_o = 0.5 * tile_vals[3]
        put = [
            put_sum,
            0.5 * tile_vals[2],
            jnp.where(in_y, put_n, put_o),
            jnp.where(in_y, put_o, put_n),
            in_sign_half * tile_vals[1],
        ]
        zero_part = jnp.zeros((tile_rows, 128), half_type)
        columns = []
        for f in range(5):
            first = split(put[f] * in_low_faces)
            second = split(put[f] * in_high_faces)
            high, low = rest_parts[f]
            columns.append(jnp.concatenate([first[0], first[1], zero_part, zero_part], axis=0))
            columns.append(jnp.concatenate([second[0], second[1], high, low], axis=0))
        on_faces = dot(tile_scatter, jnp.concatenate(columns, axis=1))
        face_parts = [split(on_faces[:, 256 * f : 256 * f + 256]) for f in range(5)]
        spread = dot(
            jnp.concatenate([p[0] for p in face_parts] + [p[1] for p in face_parts], axis=0),
            spread_ref[...],
        )
        finished = []
        for f in range(5):
            at = f * elements
            low_at = (5 + f) * elements
            nodes = spread[at : at + elements] + spread[low_at : low_at + elements]
            finished.append(result[f] + lift * nodes)
        return finished

    loads[0].wait()
    held_state[...] = state_ref[...]

    for stage in range(3):
        current = [held_state[f] for f in range(5)]
        change = rates(current, stage)
        for f in range(5):
            moved = held_state[f] + change[f]
            if stage == 0:
                held_state[f] = moved
            elif stage == 1:
                held_state[f] = 0.75 * state_ref[f] + 0.25 * moved
            else:
                out_ref[f] = state_ref[f] / 3.0 + (2.0 / 3.0) * moved
    for stage in range(3):
        for copy in tile_copies(stage):
            copy.wait_send()

    @pl.when(has_prev)
    def _():
        for stage in range(3):
            curve_copy(stage, 0).wait_send()

    @pl.when(has_next)
    def _():
        for stage in range(3):
            curve_copy(stage, 1).wait_send()


def shards(
    state,
    levels,
    send_faces,
    send_counts,
    recv_faces,
    recv_orients,
    recv_counts,
    curve_faces,
    curve_orients,
    curve_counts,
):
    curves = lax.axis_size("curve")
    tiles, cap_tile = send_faces.shape
    cap_curve = curve_faces.shape[1]
    elements = state.shape[1]
    half_rows = -(-cap_tile // 4) * 4
    sizes = (curves, tiles, elements, cap_tile, cap_curve, half_rows)
    block = 2 * half_rows
    operands = [
        state,
        levels,
        send_faces,
        send_counts,
        recv_faces,
        recv_orients,
        recv_counts,
        curve_faces,
        curve_orients,
        curve_counts,
        *tables(),
    ]
    held = [
        pltpu.SMEM(value.shape, value.dtype)
        if value.ndim == 1
        else pltpu.VMEM(value.shape, value.dtype)
        for value in operands
    ]
    return pl.pallas_call(
        functools.partial(section_kernel, sizes),
        out_shape=pltpu.VMEM(state.shape, state.dtype),
        in_specs=[pl.BlockSpec(memory_space=pl.ANY)] * operand_count,
        out_specs=pl.BlockSpec(memory_space=pltpu.VMEM),
        scratch_shapes=held
        + [
            pltpu.VMEM((3, tiles, block, 256), jnp.float32),
            pltpu.VMEM((3, tiles, block, 256), jnp.float32),
            pltpu.VMEM((3, 2, cap_curve, 256), jnp.float32),
            pltpu.VMEM((3, 2, cap_curve, 256), jnp.float32),
            pltpu.SemaphoreType.DMA((3, tiles)),
            pltpu.SemaphoreType.DMA((3, tiles)),
            pltpu.SemaphoreType.DMA((3, 2)),
            pltpu.SemaphoreType.DMA((3, 2)),
            pltpu.SemaphoreType.DMA((operand_count,)),
            pltpu.VMEM(state.shape, jnp.float32),
        ],
        compiler_params=pltpu.CompilerParams(
            collective_id=0, has_side_effects=True, vmem_limit_bytes=60 * 1024 * 1024
        ),
    )(*operands)


def solution(mesh):
    return jax.shard_map(
        shards,
        mesh=mesh,
        in_specs=(
            P(None, ("curve", "tile"), None),
            P(("curve", "tile")),
            P(("curve", "tile"), None),
            P(("curve", "tile")),
            P(("curve", "tile"), None),
            P(("curve", "tile"), None),
            P(("curve", "tile")),
            P(("curve", "tile"), None),
            P(("curve", "tile"), None),
            P(("curve", "tile")),
        ),
        out_specs=P(None, ("curve", "tile"), None),
        check_vma=False,
    )
```

```python
import functools

import jax
import jax.numpy as jnp
import ml_dtypes
import numpy as np
from jax import lax
from jax.experimental import pallas as pl
from jax.experimental.pallas import tpu as pltpu
from jax.sharding import PartitionSpec as P

time_step = 0.002
half_type = jnp.bfloat16
MESH = pl.DeviceIdType.MESH
operand_count = 17
load_order = [0, 2, 4, 5, 3, 6, 7, 8, 9, 1, 10, 12, 14, 15, 16, 13, 11]
inner_nodes = [
    -0.8717401485096066,
    -0.5917001814331423,
    -0.20929921790247888,
    0.20929921790247888,
    0.5917001814331423,
    0.8717401485096066,
]


def legendre_seven(abscissa):
    before = abscissa * 0.0 + 1.0
    current = abscissa + 0.0
    for order in range(1, 7):
        before, current = (
            current,
            ((2 * order + 1) * abscissa * current - order * before) / (order + 1),
        )
    return current


def tables():
    points = np.array([-1.0] + inner_nodes + [1.0])
    values = legendre_seven(points)
    weights = 2.0 / (56 * values**2)
    deriv = np.zeros((8, 8))
    for row in range(8):
        for col in range(8):
            if row != col:
                deriv[row, col] = values[row] / (values[col] * (points[row] - points[col]))
    deriv[0, 0] = -14.0
    deriv[7, 7] = 14.0
    halves = []
    projections = []
    for side in range(2):
        targets = (points + 2.0 * side - 1.0) / 2.0
        interp = np.ones((8, 8))
        for col in range(8):
            for other in range(8):
                if other != col:
                    interp[:, col] *= (targets - points[other]) / (points[col] - points[other])
        halves.append(interp)
        projections.append(0.5 * (interp.T * weights[None, :]) / weights[:, None])
    pairs = [(a, b) for a in range(2) for b in range(2)]
    mortar = [np.kron(halves[a], halves[b]) for a, b in pairs]
    project = [np.kron(projections[a], projections[b]) for a, b in pairs]
    turn = np.zeros((8, 64, 64))
    for code in range(8):
        for s in range(8):
            for t in range(8):
                a, c = (t, s) if code & 4 else (s, t)
                a = 7 - a if code & 1 else a
                c = 7 - c if code & 2 else c
                turn[code, 8 * s + t, 8 * a + c] = 1.0
    eye = np.eye(64)
    send = mortar + [eye] + [turn[o].T for o in range(8)] + [np.zeros((64, 64))]
    send += [0.25 * eye - q @ m for q, m in zip(project, mortar)]
    take = [turn[o] for o in range(8)] + project + [eye, np.zeros((64, 64))]

    pick = np.zeros((512, 256))
    for s in range(8):
        for t in range(8):
            column = 8 * s + t
            pick[64 * s + t, column] = 1.0
            pick[64 * s + 8 * t, 64 + column] = 1.0
            pick[64 * s + 56 + t, 128 + column] = 1.0
            pick[64 * s + 8 * t + 7, 192 + column] = 1.0
    def parts(matrix):
        high = matrix.astype(ml_dtypes.bfloat16)
        low = (matrix - high.astype(np.float64)).astype(ml_dtypes.bfloat16)
        return high, low

    def stacked(mats):
        high, low = parts(np.concatenate([m.T for m in mats], axis=1))
        return np.concatenate([high, high, low, np.zeros_like(low)], axis=0)

    return [
        jnp.asarray(m.astype(ml_dtypes.bfloat16))
        for m in (
            pick,
            pick.T,
            np.concatenate(parts(np.concatenate([m.T for m in send], axis=1)), axis=0),
            stacked(take),
            np.concatenate(parts(np.kron(deriv.T, np.eye(64))), axis=0),
            np.concatenate(parts(np.kron(np.eye(4), np.kron(deriv.T, np.eye(8)))), axis=0),
            np.concatenate(parts(np.kron(np.eye(32), deriv.T)), axis=0),
        )
    ]


def dot(left, right):
    return jnp.dot(left, right, preferred_element_type=jnp.float32)


def split(value):
    high = value.astype(half_type)
    return high, (value - high.astype(jnp.float32)).astype(half_type)


def div_five(value):
    return (value * 52429) >> 18


def div_six(value):
    return (value * 43691) >> 18


def swap_halves(value):
    return pltpu.roll(value, 64, axis=1)


def section_kernel(
    sizes,
    *refs,
):
    given = refs[:operand_count]
    out_ref = refs[operand_count]
    held = refs[operand_count + 1 : 2 * operand_count + 1]
    (
        tile_out,
        tile_in,
        curve_out,
        curve_in,
        tile_send_sem,
        tile_recv_sem,
        curve_send_sem,
        curve_recv_sem,
        load_sem,
        held_state,
    ) = refs[2 * operand_count + 1 :]
    (
        state_ref,
        levels_ref,
        send_faces_ref,
        send_counts_ref,
        recv_faces_ref,
        recv_orients_ref,
        recv_counts_ref,
        curve_faces_ref,
        curve_orients_ref,
        curve_counts_ref,
        pick_ref,
        spread_ref,
        send_mat_ref,
        take_mat_ref,
        along_x_ref,
        along_y_ref,
        along_z_ref,
    ) = held
    loads = [
        pltpu.make_async_copy(source, target, load_sem.at[at])
        for at, (source, target) in enumerate(zip(given, held))
    ]
    for at in load_order:
        loads[at].start()
    curves, tiles, elements, cap_tile, cap_curve, half_rows = sizes
    block = 2 * half_rows
    tile_rows = tiles * block
    curve_rows = 2 * cap_curve
    b = lax.axis_index("curve")
    t = lax.axis_index("tile")
    to_peer = [lax.rem(t + off, tiles) for off in range(tiles)]
    from_peer = [lax.rem(t + tiles - off, tiles) for off in range(tiles)]
    has_prev = b > 0
    has_next = b < curves - 1

    barrier = pltpu.get_barrier_semaphore()
    for off in range(1, tiles):
        pl.semaphore_signal(barrier, inc=1, device_id=(b, to_peer[off]), device_id_type=MESH)

    @pl.when(has_prev)
    def _():
        pl.semaphore_signal(barrier, inc=1, device_id=(b - 1, t), device_id_type=MESH)

    @pl.when(has_next)
    def _():
        pl.semaphore_signal(barrier, inc=1, device_id=(b + 1, t), device_id_type=MESH)

    @pl.when(jnp.logical_not(has_prev))
    def _():
        curve_in[:, 0] = jnp.zeros_like(curve_in[:, 0])

    @pl.when(jnp.logical_not(has_next))
    def _():
        curve_in[:, 1] = jnp.zeros_like(curve_in[:, 1])

    for at in range(1, 10):
        loads[at].wait()

    def spread_down(live_rows, rows):
        column = jnp.sum(live_rows.astype(jnp.float32), axis=1, keepdims=True)
        return jnp.broadcast_to(column - 1.0, (rows, 128))

    tile_lane = lax.broadcasted_iota(jnp.int32, (block, cap_tile), 1)
    tile_sub = lax.broadcasted_iota(jnp.int32, (block, cap_tile), 0)
    tile_first = tile_sub < half_rows
    tile_own = tile_lane == (tile_sub & (half_rows - 1))

    def tile_key_rows(peer, send_first):
        row = pl.ds(peer, 1)
        sent = send_faces_ref[row, :] * 16 + 1
        got = recv_faces_ref[row, :] * 16 + recv_orients_ref[row, :] + 1
        row_lane = lax.broadcasted_iota(jnp.int32, (1, cap_tile), 1)
        sent = jnp.where(row_lane < send_counts_ref[peer], sent, 0)
        got = jnp.where(row_lane < recv_counts_ref[peer], got, 0)
        pair = (sent, got) if send_first else (got, sent)
        both = jnp.where(tile_first, pair[0], pair[1])
        return spread_down(jnp.where(tile_own, both, 0), block)

    def curve_key_rows(side):
        shape = (cap_curve, cap_curve)
        lane = lax.broadcasted_iota(jnp.int32, shape, 1)
        sub = lax.broadcasted_iota(jnp.int32, shape, 0)
        row = curve_faces_ref[side : side + 1, :] * 16 + curve_orients_ref[side : side + 1, :] + 1
        own = jnp.logical_and(lane == sub, lane < curve_counts_ref[side])
        return spread_down(jnp.where(own, row, 0), cap_curve)

    out_keys = jnp.concatenate([tile_key_rows(p, True) for p in to_peer], axis=0)
    in_keys = jnp.concatenate([tile_key_rows(p, False) for p in from_peer], axis=0)
    rim_keys = jnp.concatenate([curve_key_rows(side) for side in range(2)], axis=0)

    sub_iota = lax.broadcasted_iota(jnp.int32, (8, 128), 0)

    def down_rows(keys):
        return keys.astype(jnp.int32)

    def along_lanes(keys, times):
        count = keys.shape[0]
        width = times * count
        shape = (count, width)
        own = lax.broadcasted_iota(jnp.int32, shape, 1) % count == lax.broadcasted_iota(
            jnp.int32, shape, 0
        )
        wide = jnp.concatenate([keys] * (-(-width // 128)), axis=1)[:, :width]
        value = jnp.sum(jnp.where(own, wide, 0.0), axis=0, keepdims=True)
        return jnp.broadcast_to(value, (elements, width)).astype(jnp.int32)

    def decode(keys, from_send):
        live = keys >= 0
        raw = jnp.maximum(keys, 0) >> 4
        turned = jnp.maximum(keys, 0) & 15
        face_id = jnp.where(from_send, div_five(raw), raw)
        child = raw - 5 * face_id
        element = div_six(face_id)
        face = face_id - 6 * element
        return jnp.where(live, element, -1), face, child, turned

    def half_flags(shape, axis, first):
        at = lax.broadcasted_iota(jnp.int32, shape, axis)
        return (at & (block - 1)) < half_rows if first else (at & (block - 1)) >= half_rows

    lane_t = lax.broadcasted_iota(jnp.int32, (tile_rows, 128), 1)
    low_t = lane_t < 64
    out_is_send = half_flags((tile_rows, 128), 0, True)
    in_is_send = half_flags((tile_rows, 128), 0, False)
    out_elem, out_face, out_child, out_turn = decode(down_rows(out_keys), out_is_send)
    in_elem, in_face, in_child, in_turn = decode(down_rows(in_keys), in_is_send)
    out_y = out_face < 4
    in_y = in_face < 4
    out_code = jnp.where(out_is_send, out_child, 5 + out_turn)
    in_code = jnp.where(in_is_send, 8 + in_child, in_turn)
    upper_t = jnp.where(low_t, 0, 1)
    out_masks = [jnp.where(out_code == 2 * j + upper_t, 1.0, 0.0) for j in range(7)]
    extra_masks = [
        jnp.where(jnp.logical_and(out_is_send, out_code == 2 * j + upper_t), 1.0, 0.0)
        for j in range(2)
    ]
    out_sign = jnp.where(out_is_send, -1.0, 1.0)
    in_sign_half = jnp.where(in_is_send, 0.5, -0.5)
    out_match = low_t == out_y
    in_match = low_t == in_y
    in_low_faces = jnp.where(jnp.logical_and(in_match, jnp.logical_not(in_is_send)), 1.0, 0.0)
    in_high_faces = jnp.where(jnp.logical_and(in_match, in_is_send), 1.0, 0.0)
    out_high_faces = jnp.where(jnp.logical_and(out_match, out_is_send), 1.0, 0.0)

    rim_row = lax.broadcasted_iota(jnp.int32, (curve_rows, 128), 0)
    lane_c = lax.broadcasted_iota(jnp.int32, (curve_rows, 128), 1)
    low_c = lane_c < 64
    rim_elem, _, _, rim_turn = decode(down_rows(rim_keys), rim_row < 0)
    rim_first = rim_row < cap_curve
    rim_match = low_c == rim_first
    rim_sign = jnp.where(rim_first, 1.0, -1.0)
    upper_c = jnp.where(low_c, 0, 1)
    in_masks = [jnp.where(in_code == 2 * j + upper_t, 1.0, 0.0) for j in range(7)]
    rim_masks = [jnp.where(rim_turn == 2 * j + upper_c, 1.0, 0.0) for j in range(4)]
    rim_place = jnp.where(rim_match, 1.0, 0.0)

    def one_hot(flags):
        return jnp.where(flags, 1.0, 0.0).astype(half_type)

    gather_lane = lax.broadcasted_iota(jnp.int32, (tile_rows, elements), 1)
    out_gather = one_hot(gather_lane == out_elem[:, :elements])
    rim_lane = lax.broadcasted_iota(jnp.int32, (curve_rows, 2 * elements), 1) % elements
    rim_gather = one_hot(rim_lane == rim_elem[:, : 2 * elements])

    lane_shape = (elements, 4 * tile_rows)
    lane_s = lax.broadcasted_iota(jnp.int32, lane_shape, 1)
    in_part = lane_s < 2 * tile_rows
    first_half = (lane_s & (block - 1)) < half_rows
    lane_from_send = first_half != in_part
    t_elem, t_face, _, _ = decode(
        jnp.where(in_part, along_lanes(in_keys, 4), along_lanes(out_keys, 4)), lane_from_send
    )
    t_hit = t_elem == lax.broadcasted_iota(jnp.int32, lane_shape, 0)
    tile_scatter = one_hot(t_hit)
    rim_shape = (elements, 2 * curve_rows)
    c_elem, c_face, _, _ = decode(
        along_lanes(rim_keys, 2), lax.broadcasted_iota(jnp.int32, rim_shape, 1) < 0
    )
    c_hit = c_elem == lax.broadcasted_iota(jnp.int32, rim_shape, 0)
    rim_scatter = one_hot(c_hit)

    def any_lane(flags):
        return jnp.max(jnp.where(flags, 1.0, 0.0), axis=1, keepdims=True)

    listed = [any_lane(jnp.logical_and(c_hit, c_face == f)) for f in (0, 1)]
    listed += [any_lane(jnp.logical_and(t_hit, t_face == f)) for f in (2, 3, 4, 5)]

    scale_blocks = []
    for start in range(0, elements, 8):
        value = jnp.zeros((8, 128), jnp.int32)
        for at in range(8):
            value = jnp.where(sub_iota == at, jnp.int32(1) << levels_ref[start + at], value)
        scale_blocks.append(value.astype(jnp.float32))
    scale = jnp.concatenate(scale_blocks, axis=0)
    scale = jnp.concatenate([scale] * 4, axis=1)
    vol_scale = scale * (-time_step)
    lift = scale * (28.0 * time_step)

    node = lax.broadcasted_iota(jnp.int32, (elements, 512), 1)
    vel_to_sum = []
    pres_to_vel = []
    own_damp = []
    side_damp = []
    for dim in range(3):
        place = (node >> (6 - 3 * dim)) & 7
        low_end = place == 0
        high_end = place == 7
        on_face = jnp.logical_or(low_end, high_end)
        known = jnp.where(low_end, listed[2 * dim], listed[2 * dim + 1])
        strong = jnp.where(on_face, lift * (1.0 - 0.5 * known), 0.0)
        weak = jnp.where(on_face, lift * (0.5 * known), 0.0)
        vel_to_sum.append(jnp.where(low_end, -strong, strong))
        pres_to_vel.append(jnp.where(low_end, -weak, weak))
        own_damp.append(strong)
        side_damp.append(weak)
    total_damp = side_damp[0] + side_damp[1] + side_damp[2]
    vel_damp = [own_damp[d] + (total_damp - side_damp[d]) for d in range(3)]

    def tile_copies(stage):
        return [
            pltpu.make_async_remote_copy(
                src_ref=tile_out.at[stage, off],
                dst_ref=tile_in.at[stage, off],
                send_sem=tile_send_sem.at[stage, off],
                recv_sem=tile_recv_sem.at[stage, off],
                device_id=(b, to_peer[off]),
                device_id_type=MESH,
            )
            for off in range(1, tiles)
        ]

    def curve_copy(stage, side):
        return pltpu.make_async_remote_copy(
            src_ref=curve_out.at[stage, side],
            dst_ref=curve_in.at[stage, 1 - side],
            send_sem=curve_send_sem.at[stage, side],
            recv_sem=curve_recv_sem.at[stage, 1 - side],
            device_id=(b - 1 + 2 * side, t),
            device_id_type=MESH,
        )

    def packed(first, second, low):
        return jnp.where(low, first, second)

    def pair_rows(value, low):
        high = value.astype(half_type).astype(jnp.float32)
        return jnp.concatenate([jnp.where(low, high, value - high), high], axis=1).astype(half_type)

    def rates(current, stage):
        parts = [split(value) for value in current]
        highs = [part[0] for part in parts]
        lows = [part[1] for part in parts]

        if stage == 0:
            loads[10].wait()
            loads[12].wait()
        low_e = lax.broadcasted_iota(jnp.int32, (elements, 128), 1) < 64
        ends = [split(jnp.where(low_e, v[:, :128], v[:, 384:])) for v in current]
        ends = jnp.concatenate([jnp.concatenate(e, axis=0) for e in ends], axis=1)
        rim = dot(rim_gather, ends)
        traces = dot(jnp.concatenate(highs, axis=0), pick_ref[...]).astype(half_type)
        rim_vals = []
        for f in range(5):
            kept = jnp.where(rim_match, rim[:, 128 * f : 128 * f + 128], 0.0)
            rim_vals.append(kept + swap_halves(kept))
        sum_part = rim_sign * rim_vals[1] - rim_vals[0]
        vel_part = rim_sign * rim_vals[4] - rim_vals[1]
        rim_send = jnp.concatenate(
            [packed(sum_part, vel_part, low_c), packed(rim_vals[2], rim_vals[3], low_c)], axis=1
        )
        curve_out[stage] = rim_send.reshape(2, cap_curve, 256)
        if stage == 0:
            pl.semaphore_wait(
                barrier, tiles - 1 + has_prev.astype(jnp.int32) + has_next.astype(jnp.int32)
            )

        @pl.when(has_prev)
        def _():
            curve_copy(stage, 0).start()

        @pl.when(has_next)
        def _():
            curve_copy(stage, 1).start()

        columns = [traces[f * elements : (f + 1) * elements] for f in range(5)]
        own = dot(out_gather, jnp.concatenate(columns, axis=1))
        own_rows = []
        for f in range(5):
            side = jnp.where(
                out_is_send, own[:, 256 * f + 128 : 256 * f + 256], own[:, 256 * f : 256 * f + 128]
            )
            kept = jnp.where(out_match, side, 0.0)
            own_rows.append((kept + swap_halves(kept)).astype(half_type))
        coded = dot(jnp.concatenate(own_rows, axis=0), send_mat_ref[...])

        def choose(source, rows_at, rows, masks, first):
            total = None
            for j, mask in enumerate(masks):
                at = 128 * (first + j)
                term = mask * source[rows_at : rows_at + rows, at : at + 128]
                total = term if total is None else total + term
            return total + swap_halves(total)

        mortar = [choose(coded, f * tile_rows, tile_rows, out_masks, 0) for f in range(5)]
        normal = jnp.where(out_y, mortar[2], mortar[3])
        other = jnp.where(out_y, mortar[3], mortar[2])
        sum_part = out_sign * normal - mortar[0]
        vel_part = out_sign * mortar[4] - normal
        tile_send = jnp.concatenate(
            [packed(sum_part, vel_part, low_t), packed(mortar[1], other, low_t)], axis=1
        )
        tile_send = tile_send.reshape(tiles, block, 256)
        tile_out[stage] = tile_send
        tile_in[stage, 0] = tile_send[0]
        copies = tile_copies(stage)
        for copy in copies:
            copy.start()

        rest = [choose(coded, f * tile_rows, tile_rows, extra_masks, 7) for f in range(5)]
        rest_n = jnp.where(out_y, rest[2], rest[3])
        rest_o = jnp.where(out_y, rest[3], rest[2])
        rest_p = 0.5 * (rest[4] + rest_n)
        rest_n = 0.5 * (rest_n + rest[4])
        rest_o = 0.5 * rest_o
        rest_fields = [
            0.5 * (rest[0] + jnp.where(out_y, rest[2], rest[3])),
            0.5 * rest[1],
            jnp.where(out_y, rest_n, rest_o),
            jnp.where(out_y, rest_o, rest_n),
            rest_p,
        ]
        rest_parts = [split(value * out_high_faces) for value in rest_fields]

        if stage == 0:
            loads[14].wait()
            loads[15].wait()
            loads[16].wait()
        grad = dot(
            jnp.concatenate([highs[1], highs[4], lows[1], lows[4]], axis=0), along_x_ref[:512]
        )
        n2 = 2 * elements
        grad_x = grad[:n2] + grad[n2:]
        grad_x = grad_x + dot(jnp.concatenate([highs[1], highs[4]], axis=0), along_x_ref[512:])

        def halves(f, source):
            return [source[f][:, :256], source[f][:, 256:]]

        def banded(f, mat_ref):
            high_rows = jnp.concatenate(halves(f, highs) + halves(4, highs), axis=0)
            low_rows = jnp.concatenate(halves(f, lows) + halves(4, lows), axis=0)
            first = dot(jnp.concatenate([high_rows, low_rows], axis=0), mat_ref[:256])
            n4 = 4 * elements
            total = first[:n4] + first[n4:] + dot(high_rows, mat_ref[256:])
            vel = jnp.concatenate([total[:elements], total[elements:n2]], axis=1)
            pres = jnp.concatenate([total[n2 : 3 * elements], total[3 * elements :]], axis=1)
            return vel, pres

        vel_y, pres_y = banded(2, along_y_ref)
        vel_z, pres_z = banded(3, along_z_ref)
        diverge = vol_scale * (grad_x[:elements] + vel_y + vel_z)
        to_sum = diverge
        for d in range(3):
            to_sum = to_sum + vel_to_sum[d] * current[1 + d]
        pres_grads = (grad_x[elements:], pres_y, pres_z)
        result = [to_sum - total_damp * current[0]]
        for d in range(3):
            result.append(
                vol_scale * pres_grads[d]
                + pres_to_vel[d] * current[4]
                - vel_damp[d] * current[1 + d]
            )
        result.append(to_sum - total_damp * current[4])

        if stage == 0:
            loads[13].wait()
            loads[11].wait()

        @pl.when(has_prev)
        def _():
            curve_copy(stage, 1).wait_recv()

        @pl.when(has_next)
        def _():
            curve_copy(stage, 0).wait_recv()

        for copy in copies:
            copy.wait_recv()

        fields = []
        for at in range(2):
            span = slice(128 * at, 128 * at + 128)
            for source, rows, low in (
                (tile_in[stage], tile_rows, low_t),
                (curve_in[stage], curve_rows, low_c),
            ):
                value = source.reshape(rows, 256)[:, span]
                turned = swap_halves(value)
                fields.append(
                    (
                        pair_rows(jnp.where(low, value, turned), low),
                        pair_rows(jnp.where(low, turned, value), low),
                    )
                )
        stacked = [fields[0][0], fields[0][1], fields[2][0], fields[2][1]]
        stacked += [fields[1][0], fields[1][1], fields[3][0], fields[3][1]]
        taken = dot(jnp.concatenate(stacked, axis=0), take_mat_ref[...])
        tile_vals = [choose(taken, f * tile_rows, tile_rows, in_masks, 0) for f in range(4)]
        rim_at = 4 * tile_rows
        rim_vals = [
            choose(taken, rim_at + f * curve_rows, curve_rows, rim_masks, 0) for f in range(4)
        ]

        rim_cols = [jnp.concatenate(split(value * rim_place), axis=0) for value in rim_vals]
        placed = dot(rim_scatter, jnp.concatenate(rim_cols, axis=1))
        place_sum = -0.5 * placed[:, :128]
        place_vel = -0.5 * placed[:, 128:256]
        place_pres = jnp.where(low_e, place_vel, -place_vel)
        rim_fields = [
            place_sum,
            place_vel,
            0.5 * placed[:, 256:384],
            0.5 * placed[:, 384:512],
            place_pres,
        ]

        put_sum = -0.5 * tile_vals[0]
        put_n = -0.5 * tile_vals[1]
        put_o = 0.5 * tile_vals[3]
        put = [
            put_sum,
            0.5 * tile_vals[2],
            jnp.where(in_y, put_n, put_o),
            jnp.where(in_y, put_o, put_n),
            in_sign_half * tile_vals[1],
        ]
        zero_part = jnp.zeros((tile_rows, 128), half_type)
        columns = []
        for f in range(5):
            first = split(put[f] * in_low_faces)
            second = split(put[f] * in_high_faces)
            high, low = rest_parts[f]
            columns.append(jnp.concatenate([first[0], first[1], zero_part, zero_part], axis=0))
            columns.append(jnp.concatenate([second[0], second[1], high, low], axis=0))
        on_faces = dot(tile_scatter, jnp.concatenate(columns, axis=1))
        spread = dot(
            jnp.concatenate(
                [on_faces[:, 256 * f : 256 * f + 256].astype(half_type) for f in range(5)], axis=0
            ),
            spread_ref[...],
        )
        finished = []
        for f in range(5):
            nodes = spread[f * elements : (f + 1) * elements]
            first = nodes[:, :128] + jnp.where(low_e, rim_fields[f], 0.0)
            last = nodes[:, 384:] + jnp.where(low_e, 0.0, rim_fields[f])
            nodes = jnp.concatenate([first, nodes[:, 128:384], last], axis=1)
            finished.append(result[f] + lift * nodes)
        return finished

    loads[0].wait()
    held_state[...] = state_ref[...]

    for stage in range(3):
        current = [held_state[f] for f in range(5)]
        change = rates(current, stage)
        for f in range(5):
            moved = held_state[f] + change[f]
            if stage == 0:
                held_state[f] = moved
            elif stage == 1:
                held_state[f] = 0.75 * state_ref[f] + 0.25 * moved
            else:
                out_ref[f] = state_ref[f] / 3.0 + (2.0 / 3.0) * moved
    for stage in range(3):
        for copy in tile_copies(stage):
            copy.wait_send()

    @pl.when(has_prev)
    def _():
        for stage in range(3):
            curve_copy(stage, 0).wait_send()

    @pl.when(has_next)
    def _():
        for stage in range(3):
            curve_copy(stage, 1).wait_send()


def shards(
    state,
    levels,
    send_faces,
    send_counts,
    recv_faces,
    recv_orients,
    recv_counts,
    curve_faces,
    curve_orients,
    curve_counts,
):
    curves = lax.axis_size("curve")
    tiles, cap_tile = send_faces.shape
    cap_curve = curve_faces.shape[1]
    elements = state.shape[1]
    half_rows = -(-cap_tile // 4) * 4
    sizes = (curves, tiles, elements, cap_tile, cap_curve, half_rows)
    block = 2 * half_rows
    operands = [
        state,
        levels,
        send_faces,
        send_counts,
        recv_faces,
        recv_orients,
        recv_counts,
        curve_faces,
        curve_orients,
        curve_counts,
        *tables(),
    ]
    held = [
        pltpu.SMEM(value.shape, value.dtype)
        if value.ndim == 1
        else pltpu.VMEM(value.shape, value.dtype)
        for value in operands
    ]
    return pl.pallas_call(
        functools.partial(section_kernel, sizes),
        out_shape=pltpu.VMEM(state.shape, state.dtype),
        in_specs=[pl.BlockSpec(memory_space=pl.ANY)] * operand_count,
        out_specs=pl.BlockSpec(memory_space=pltpu.VMEM),
        scratch_shapes=held
        + [
            pltpu.VMEM((3, tiles, block, 256), jnp.float32),
            pltpu.VMEM((3, tiles, block, 256), jnp.float32),
            pltpu.VMEM((3, 2, cap_curve, 256), jnp.float32),
            pltpu.VMEM((3, 2, cap_curve, 256), jnp.float32),
            pltpu.SemaphoreType.DMA((3, tiles)),
            pltpu.SemaphoreType.DMA((3, tiles)),
            pltpu.SemaphoreType.DMA((3, 2)),
            pltpu.SemaphoreType.DMA((3, 2)),
            pltpu.SemaphoreType.DMA((operand_count,)),
            pltpu.VMEM(state.shape, jnp.float32),
        ],
        compiler_params=pltpu.CompilerParams(
            collective_id=0, has_side_effects=True, vmem_limit_bytes=60 * 1024 * 1024
        ),
    )(*operands)


def solution(mesh):
    return jax.shard_map(
        shards,
        mesh=mesh,
        in_specs=(
            P(None, ("curve", "tile"), None),
            P(("curve", "tile")),
            P(("curve", "tile"), None),
            P(("curve", "tile")),
            P(("curve", "tile"), None),
            P(("curve", "tile"), None),
            P(("curve", "tile")),
            P(("curve", "tile"), None),
            P(("curve", "tile"), None),
            P(("curve", "tile")),
        ),
        out_specs=P(None, ("curve", "tile"), None),
        check_vma=False,
    )
```

```python
import functools

import jax
import jax.numpy as jnp
import ml_dtypes
import numpy as np
from jax import lax
from jax.experimental import pallas as pl
from jax.experimental.pallas import tpu as pltpu
from jax.sharding import PartitionSpec as P

time_step = 0.002
half_type = jnp.bfloat16
MESH = pl.DeviceIdType.MESH
operand_count = 17
load_order = [0, 2, 4, 5, 3, 6, 7, 8, 9, 1, 10, 12, 14, 15, 16, 13, 11]
inner_nodes = [
    -0.8717401485096066,
    -0.5917001814331423,
    -0.20929921790247888,
    0.20929921790247888,
    0.5917001814331423,
    0.8717401485096066,
]


def legendre_seven(abscissa):
    before = abscissa * 0.0 + 1.0
    current = abscissa + 0.0
    for order in range(1, 7):
        before, current = (
            current,
            ((2 * order + 1) * abscissa * current - order * before) / (order + 1),
        )
    return current


def tables():
    points = np.array([-1.0] + inner_nodes + [1.0])
    values = legendre_seven(points)
    weights = 2.0 / (56 * values**2)
    deriv = np.zeros((8, 8))
    for row in range(8):
        for col in range(8):
            if row != col:
                deriv[row, col] = values[row] / (values[col] * (points[row] - points[col]))
    deriv[0, 0] = -14.0
    deriv[7, 7] = 14.0
    halves = []
    projections = []
    for side in range(2):
        targets = (points + 2.0 * side - 1.0) / 2.0
        interp = np.ones((8, 8))
        for col in range(8):
            for other in range(8):
                if other != col:
                    interp[:, col] *= (targets - points[other]) / (points[col] - points[other])
        halves.append(interp)
        projections.append(0.5 * (interp.T * weights[None, :]) / weights[:, None])
    pairs = [(a, b) for a in range(2) for b in range(2)]
    mortar = [np.kron(halves[a], halves[b]) for a, b in pairs]
    project = [np.kron(projections[a], projections[b]) for a, b in pairs]
    turn = np.zeros((8, 64, 64))
    for code in range(8):
        for s in range(8):
            for t in range(8):
                a, c = (t, s) if code & 4 else (s, t)
                a = 7 - a if code & 1 else a
                c = 7 - c if code & 2 else c
                turn[code, 8 * s + t, 8 * a + c] = 1.0
    eye = np.eye(64)
    send = mortar + [eye] + [turn[o].T for o in range(8)] + [np.zeros((64, 64))]
    send += [0.25 * eye - q @ m for q, m in zip(project, mortar)]
    take = [turn[o] for o in range(8)] + project + [eye, np.zeros((64, 64))]

    pick = np.zeros((512, 256))
    for s in range(8):
        for t in range(8):
            column = 8 * s + t
            pick[64 * s + t, column] = 1.0
            pick[64 * s + 8 * t, 64 + column] = 1.0
            pick[64 * s + 56 + t, 128 + column] = 1.0
            pick[64 * s + 8 * t + 7, 192 + column] = 1.0
    def parts(matrix):
        high = matrix.astype(ml_dtypes.bfloat16)
        low = (matrix - high.astype(np.float64)).astype(ml_dtypes.bfloat16)
        return high, low

    def stacked(mats):
        high, low = parts(np.concatenate([m.T for m in mats], axis=1))
        return np.concatenate([high, high, low, np.zeros_like(low)], axis=0)

    return [
        jnp.asarray(m.astype(ml_dtypes.bfloat16))
        for m in (
            pick,
            pick.T,
            np.concatenate(parts(np.concatenate([m.T for m in send], axis=1)), axis=0),
            stacked(take),
            np.concatenate(parts(np.kron(deriv.T, np.eye(64))), axis=0),
            np.concatenate(parts(np.kron(np.eye(4), np.kron(deriv.T, np.eye(8)))), axis=0),
            np.concatenate(parts(np.kron(np.eye(32), deriv.T)), axis=0),
        )
    ]


def dot(left, right):
    return jnp.dot(left, right, preferred_element_type=jnp.float32)


def split(value):
    high = value.astype(half_type)
    return high, (value - high.astype(jnp.float32)).astype(half_type)


def div_five(value):
    return (value * 52429) >> 18


def div_six(value):
    return (value * 43691) >> 18


def swap_halves(value):
    return pltpu.roll(value, 64, axis=1)


def section_kernel(
    sizes,
    *refs,
):
    given = refs[:operand_count]
    out_ref = refs[operand_count]
    held = refs[operand_count + 1 : 2 * operand_count + 1]
    (
        tile_out,
        tile_in,
        curve_out,
        curve_in,
        tile_send_sem,
        tile_recv_sem,
        curve_send_sem,
        curve_recv_sem,
        load_sem,
        held_state,
    ) = refs[2 * operand_count + 1 :]
    (
        state_ref,
        levels_ref,
        send_faces_ref,
        send_counts_ref,
        recv_faces_ref,
        recv_orients_ref,
        recv_counts_ref,
        curve_faces_ref,
        curve_orients_ref,
        curve_counts_ref,
        pick_ref,
        spread_ref,
        send_mat_ref,
        take_mat_ref,
        along_x_ref,
        along_y_ref,
        along_z_ref,
    ) = held
    loads = [
        pltpu.make_async_copy(source, target, load_sem.at[at])
        for at, (source, target) in enumerate(zip(given, held))
    ]
    for at in load_order:
        loads[at].start()
    curves, tiles, elements, cap_tile, cap_curve, half_rows = sizes
    block = 2 * half_rows
    tile_rows = tiles * block
    curve_rows = 2 * cap_curve
    b = lax.axis_index("curve")
    t = lax.axis_index("tile")
    to_peer = [lax.rem(t + off, tiles) for off in range(tiles)]
    from_peer = [lax.rem(t + tiles - off, tiles) for off in range(tiles)]
    has_prev = b > 0
    has_next = b < curves - 1

    barrier = pltpu.get_barrier_semaphore()
    for off in range(1, tiles):
        pl.semaphore_signal(barrier, inc=1, device_id=(b, to_peer[off]), device_id_type=MESH)

    @pl.when(has_prev)
    def _():
        pl.semaphore_signal(barrier, inc=1, device_id=(b - 1, t), device_id_type=MESH)

    @pl.when(has_next)
    def _():
        pl.semaphore_signal(barrier, inc=1, device_id=(b + 1, t), device_id_type=MESH)

    @pl.when(jnp.logical_not(has_prev))
    def _():
        curve_in[:, 0] = jnp.zeros_like(curve_in[:, 0])

    @pl.when(jnp.logical_not(has_next))
    def _():
        curve_in[:, 1] = jnp.zeros_like(curve_in[:, 1])

    for at in range(1, 10):
        loads[at].wait()

    def spread_down(live_rows, rows):
        column = jnp.sum(live_rows.astype(jnp.float32), axis=1, keepdims=True)
        return jnp.broadcast_to(column - 1.0, (rows, 128))

    tile_lane = lax.broadcasted_iota(jnp.int32, (block, cap_tile), 1)
    tile_sub = lax.broadcasted_iota(jnp.int32, (block, cap_tile), 0)
    tile_first = tile_sub < half_rows
    tile_own = tile_lane == (tile_sub & (half_rows - 1))

    def tile_key_rows(peer, send_first):
        row = pl.ds(peer, 1)
        sent = send_faces_ref[row, :] * 16 + 1
        got = recv_faces_ref[row, :] * 16 + recv_orients_ref[row, :] + 1
        row_lane = lax.broadcasted_iota(jnp.int32, (1, cap_tile), 1)
        sent = jnp.where(row_lane < send_counts_ref[peer], sent, 0)
        got = jnp.where(row_lane < recv_counts_ref[peer], got, 0)
        pair = (sent, got) if send_first else (got, sent)
        both = jnp.where(tile_first, pair[0], pair[1])
        return spread_down(jnp.where(tile_own, both, 0), block)

    def curve_key_rows(side):
        shape = (cap_curve, cap_curve)
        lane = lax.broadcasted_iota(jnp.int32, shape, 1)
        sub = lax.broadcasted_iota(jnp.int32, shape, 0)
        row = curve_faces_ref[side : side + 1, :] * 16 + curve_orients_ref[side : side + 1, :] + 1
        own = jnp.logical_and(lane == sub, lane < curve_counts_ref[side])
        return spread_down(jnp.where(own, row, 0), cap_curve)

    out_keys = jnp.concatenate([tile_key_rows(p, True) for p in to_peer], axis=0)
    rim_keys = jnp.concatenate([curve_key_rows(side) for side in range(2)], axis=0)

    sub_iota = lax.broadcasted_iota(jnp.int32, (8, 128), 0)

    def down_rows(keys):
        return keys.astype(jnp.int32)

    def along_lanes(keys, times):
        count = keys.shape[0]
        width = times * count
        shape = (count, width)
        own = lax.broadcasted_iota(jnp.int32, shape, 1) % count == lax.broadcasted_iota(
            jnp.int32, shape, 0
        )
        wide = jnp.concatenate([keys] * (-(-width // 128)), axis=1)[:, :width]
        value = jnp.sum(jnp.where(own, wide, 0.0), axis=0, keepdims=True)
        return jnp.broadcast_to(value, (elements, width)).astype(jnp.int32)

    def decode(keys, from_send):
        live = keys >= 0
        raw = jnp.maximum(keys, 0) >> 4
        turned = jnp.maximum(keys, 0) & 15
        face_id = jnp.where(from_send, div_five(raw), raw)
        child = raw - 5 * face_id
        element = div_six(face_id)
        face = face_id - 6 * element
        return jnp.where(live, element, -1), face, child, turned

    def half_flags(shape, axis, first):
        at = lax.broadcasted_iota(jnp.int32, shape, axis)
        return (at & (block - 1)) < half_rows if first else (at & (block - 1)) >= half_rows

    lane_t = lax.broadcasted_iota(jnp.int32, (tile_rows, 128), 1)
    low_t = lane_t < 64
    out_is_send = half_flags((tile_rows, 128), 0, True)
    out_elem, out_face, out_child, out_turn = decode(down_rows(out_keys), out_is_send)
    out_y = out_face < 4
    out_code = jnp.where(out_is_send, out_child, 5 + out_turn)
    upper_t = jnp.where(low_t, 0, 1)
    out_masks = [jnp.where(out_code == 2 * j + upper_t, 1.0, 0.0) for j in range(7)]
    out_sign = jnp.where(out_is_send, -1.0, 1.0)
    out_match = low_t == out_y

    rim_row = lax.broadcasted_iota(jnp.int32, (curve_rows, 128), 0)
    lane_c = lax.broadcasted_iota(jnp.int32, (curve_rows, 128), 1)
    low_c = lane_c < 64
    rim_elem, _, _, rim_turn = decode(down_rows(rim_keys), rim_row < 0)
    rim_first = rim_row < cap_curve
    rim_match = low_c == rim_first
    rim_sign = jnp.where(rim_first, 1.0, -1.0)

    def one_hot(flags):
        return jnp.where(flags, 1.0, 0.0).astype(half_type)

    gather_lane = lax.broadcasted_iota(jnp.int32, (tile_rows, elements), 1)
    out_gather = one_hot(gather_lane == out_elem[:, :elements])
    rim_lane = lax.broadcasted_iota(jnp.int32, (curve_rows, 2 * elements), 1) % elements
    rim_gather = one_hot(rim_lane == rim_elem[:, : 2 * elements])

    def late_tables():
        in_keys = jnp.concatenate([tile_key_rows(p, False) for p in from_peer], axis=0)
        in_is_send = half_flags((tile_rows, 128), 0, False)
        in_elem, in_face, in_child, in_turn = decode(down_rows(in_keys), in_is_send)
        in_y = in_face < 4
        in_code = jnp.where(in_is_send, 8 + in_child, in_turn)
        extra_masks = [
            jnp.where(jnp.logical_and(out_is_send, out_code == 2 * j + upper_t), 1.0, 0.0)
            for j in range(2)
        ]
        in_sign_half = jnp.where(in_is_send, 0.5, -0.5)
        in_match = low_t == in_y
        in_low_faces = jnp.where(jnp.logical_and(in_match, jnp.logical_not(in_is_send)), 1.0, 0.0)
        in_high_faces = jnp.where(jnp.logical_and(in_match, in_is_send), 1.0, 0.0)
        out_high_faces = jnp.where(jnp.logical_and(out_match, out_is_send), 1.0, 0.0)
        upper_c = jnp.where(low_c, 0, 1)
        in_masks = [jnp.where(in_code == 2 * j + upper_t, 1.0, 0.0) for j in range(7)]
        rim_masks = [jnp.where(rim_turn == 2 * j + upper_c, 1.0, 0.0) for j in range(4)]
        rim_place = jnp.where(rim_match, 1.0, 0.0)
        lane_shape = (elements, 4 * tile_rows)
        lane_s = lax.broadcasted_iota(jnp.int32, lane_shape, 1)
        in_part = lane_s < 2 * tile_rows
        first_half = (lane_s & (block - 1)) < half_rows
        lane_from_send = first_half != in_part
        t_elem, t_face, _, _ = decode(
            jnp.where(in_part, along_lanes(in_keys, 4), along_lanes(out_keys, 4)), lane_from_send
        )
        t_hit = t_elem == lax.broadcasted_iota(jnp.int32, lane_shape, 0)
        tile_scatter = one_hot(t_hit)
        rim_shape = (elements, 2 * curve_rows)
        c_elem, c_face, _, _ = decode(
            along_lanes(rim_keys, 2), lax.broadcasted_iota(jnp.int32, rim_shape, 1) < 0
        )
        c_hit = c_elem == lax.broadcasted_iota(jnp.int32, rim_shape, 0)
        rim_scatter = one_hot(c_hit)

        def any_lane(flags):
            return jnp.max(jnp.where(flags, 1.0, 0.0), axis=1, keepdims=True)

        listed = [any_lane(jnp.logical_and(c_hit, c_face == f)) for f in (0, 1)]
        listed += [any_lane(jnp.logical_and(t_hit, t_face == f)) for f in (2, 3, 4, 5)]

        scale_blocks = []
        for start in range(0, elements, 8):
            value = jnp.zeros((8, 128), jnp.int32)
            for at in range(8):
                value = jnp.where(sub_iota == at, jnp.int32(1) << levels_ref[start + at], value)
            scale_blocks.append(value.astype(jnp.float32))
        scale = jnp.concatenate(scale_blocks, axis=0)
        scale = jnp.concatenate([scale] * 4, axis=1)
        vol_scale = scale * (-time_step)
        lift = scale * (28.0 * time_step)

        node = lax.broadcasted_iota(jnp.int32, (elements, 512), 1)
        vel_to_sum = []
        pres_to_vel = []
        own_damp = []
        side_damp = []
        for dim in range(3):
            place = (node >> (6 - 3 * dim)) & 7
            low_end = place == 0
            high_end = place == 7
            on_face = jnp.logical_or(low_end, high_end)
            known = jnp.where(low_end, listed[2 * dim], listed[2 * dim + 1])
            strong = jnp.where(on_face, lift * (1.0 - 0.5 * known), 0.0)
            weak = jnp.where(on_face, lift * (0.5 * known), 0.0)
            vel_to_sum.append(jnp.where(low_end, -strong, strong))
            pres_to_vel.append(jnp.where(low_end, -weak, weak))
            own_damp.append(strong)
            side_damp.append(weak)
        total_damp = side_damp[0] + side_damp[1] + side_damp[2]
        vel_damp = [own_damp[d] + (total_damp - side_damp[d]) for d in range(3)]
        return {
            "extra_masks": extra_masks,
            "in_sign_half": in_sign_half,
            "in_y": in_y,
            "in_low_faces": in_low_faces,
            "in_high_faces": in_high_faces,
            "out_high_faces": out_high_faces,
            "in_masks": in_masks,
            "rim_masks": rim_masks,
            "rim_place": rim_place,
            "tile_scatter": tile_scatter,
            "rim_scatter": rim_scatter,
            "vol_scale": vol_scale,
            "lift": lift,
            "vel_to_sum": vel_to_sum,
            "pres_to_vel": pres_to_vel,
            "total_damp": total_damp,
            "vel_damp": vel_damp,
        }

    late = {}

    def tile_copies(stage):
        return [
            pltpu.make_async_remote_copy(
                src_ref=tile_out.at[stage, off],
                dst_ref=tile_in.at[stage, off],
                send_sem=tile_send_sem.at[stage, off],
                recv_sem=tile_recv_sem.at[stage, off],
                device_id=(b, to_peer[off]),
                device_id_type=MESH,
            )
            for off in range(1, tiles)
        ]

    def curve_copy(stage, side):
        return pltpu.make_async_remote_copy(
            src_ref=curve_out.at[stage, side],
            dst_ref=curve_in.at[stage, 1 - side],
            send_sem=curve_send_sem.at[stage, side],
            recv_sem=curve_recv_sem.at[stage, 1 - side],
            device_id=(b - 1 + 2 * side, t),
            device_id_type=MESH,
        )

    def packed(first, second, low):
        return jnp.where(low, first, second)

    def pair_rows(value, low):
        high = value.astype(half_type).astype(jnp.float32)
        return jnp.concatenate([jnp.where(low, high, value - high), high], axis=1).astype(half_type)

    def rates(current, stage):
        parts = [split(value) for value in current]
        highs = [part[0] for part in parts]
        lows = [part[1] for part in parts]

        if stage == 0:
            loads[10].wait()
            loads[12].wait()
        low_e = lax.broadcasted_iota(jnp.int32, (elements, 128), 1) < 64
        ends = [split(jnp.where(low_e, v[:, :128], v[:, 384:])) for v in current]
        ends = jnp.concatenate([jnp.concatenate(e, axis=0) for e in ends], axis=1)
        rim = dot(rim_gather, ends)
        traces = dot(jnp.concatenate(highs, axis=0), pick_ref[...]).astype(half_type)
        rim_vals = []
        for f in range(5):
            kept = jnp.where(rim_match, rim[:, 128 * f : 128 * f + 128], 0.0)
            rim_vals.append(kept + swap_halves(kept))
        sum_part = rim_sign * rim_vals[1] - rim_vals[0]
        vel_part = rim_sign * rim_vals[4] - rim_vals[1]
        rim_send = jnp.concatenate(
            [packed(sum_part, vel_part, low_c), packed(rim_vals[2], rim_vals[3], low_c)], axis=1
        )
        curve_out[stage] = rim_send.reshape(2, cap_curve, 256)
        if stage == 0:
            pl.semaphore_wait(
                barrier, tiles - 1 + has_prev.astype(jnp.int32) + has_next.astype(jnp.int32)
            )

        @pl.when(has_prev)
        def _():
            curve_copy(stage, 0).start()

        @pl.when(has_next)
        def _():
            curve_copy(stage, 1).start()

        columns = [traces[f * elements : (f + 1) * elements] for f in range(5)]
        own = dot(out_gather, jnp.concatenate(columns, axis=1))
        own_rows = []
        for f in range(5):
            side = jnp.where(
                out_is_send, own[:, 256 * f + 128 : 256 * f + 256], own[:, 256 * f : 256 * f + 128]
            )
            kept = jnp.where(out_match, side, 0.0)
            own_rows.append((kept + swap_halves(kept)).astype(half_type))
        own_rows = jnp.concatenate(own_rows, axis=0)
        coded = dot(own_rows, send_mat_ref[:, :896])

        def choose(source, rows_at, rows, masks, first):
            total = None
            for j, mask in enumerate(masks):
                at = 128 * (first + j)
                term = mask * source[rows_at : rows_at + rows, at : at + 128]
                total = term if total is None else total + term
            return total + swap_halves(total)

        mortar = [choose(coded, f * tile_rows, tile_rows, out_masks, 0) for f in range(5)]
        normal = jnp.where(out_y, mortar[2], mortar[3])
        other = jnp.where(out_y, mortar[3], mortar[2])
        sum_part = out_sign * normal - mortar[0]
        vel_part = out_sign * mortar[4] - normal
        tile_send = jnp.concatenate(
            [packed(sum_part, vel_part, low_t), packed(mortar[1], other, low_t)], axis=1
        )
        tile_send = tile_send.reshape(tiles, block, 256)
        tile_out[stage] = tile_send
        tile_in[stage, 0] = tile_send[0]
        copies = tile_copies(stage)
        for copy in copies:
            copy.start()

        if stage == 0:
            late.update(late_tables())
        apart = dot(own_rows, send_mat_ref[:, 896:])
        rest = [choose(apart, f * tile_rows, tile_rows, late["extra_masks"], 0) for f in range(5)]
        rest_n = jnp.where(out_y, rest[2], rest[3])
        rest_o = jnp.where(out_y, rest[3], rest[2])
        rest_p = 0.5 * (rest[4] + rest_n)
        rest_n = 0.5 * (rest_n + rest[4])
        rest_o = 0.5 * rest_o
        rest_fields = [
            0.5 * (rest[0] + jnp.where(out_y, rest[2], rest[3])),
            0.5 * rest[1],
            jnp.where(out_y, rest_n, rest_o),
            jnp.where(out_y, rest_o, rest_n),
            rest_p,
        ]
        rest_parts = [split(value * late["out_high_faces"]) for value in rest_fields]

        if stage == 0:
            loads[14].wait()
            loads[15].wait()
            loads[16].wait()
        grad = dot(
            jnp.concatenate([highs[1], highs[4], lows[1], lows[4]], axis=0), along_x_ref[:512]
        )
        n2 = 2 * elements
        grad_x = grad[:n2] + grad[n2:]
        grad_x = grad_x + dot(jnp.concatenate([highs[1], highs[4]], axis=0), along_x_ref[512:])

        def halves(f, source):
            return [source[f][:, :256], source[f][:, 256:]]

        def banded(f, mat_ref):
            high_rows = jnp.concatenate(halves(f, highs) + halves(4, highs), axis=0)
            low_rows = jnp.concatenate(halves(f, lows) + halves(4, lows), axis=0)
            first = dot(jnp.concatenate([high_rows, low_rows], axis=0), mat_ref[:256])
            n4 = 4 * elements
            total = first[:n4] + first[n4:] + dot(high_rows, mat_ref[256:])
            vel = jnp.concatenate([total[:elements], total[elements:n2]], axis=1)
            pres = jnp.concatenate([total[n2 : 3 * elements], total[3 * elements :]], axis=1)
            return vel, pres

        vel_y, pres_y = banded(2, along_y_ref)
        vel_z, pres_z = banded(3, along_z_ref)
        diverge = late["vol_scale"] * (grad_x[:elements] + vel_y + vel_z)
        to_sum = diverge
        for d in range(3):
            to_sum = to_sum + late["vel_to_sum"][d] * current[1 + d]
        pres_grads = (grad_x[elements:], pres_y, pres_z)
        result = [to_sum - late["total_damp"] * current[0]]
        for d in range(3):
            result.append(
                late["vol_scale"] * pres_grads[d]
                + late["pres_to_vel"][d] * current[4]
                - late["vel_damp"][d] * current[1 + d]
            )
        result.append(to_sum - late["total_damp"] * current[4])

        if stage == 0:
            loads[13].wait()
            loads[11].wait()

        @pl.when(has_prev)
        def _():
            curve_copy(stage, 1).wait_recv()

        @pl.when(has_next)
        def _():
            curve_copy(stage, 0).wait_recv()

        for copy in copies:
            copy.wait_recv()

        fields = []
        for at in range(2):
            span = slice(128 * at, 128 * at + 128)
            for source, rows, low in (
                (tile_in[stage], tile_rows, low_t),
                (curve_in[stage], curve_rows, low_c),
            ):
                value = source.reshape(rows, 256)[:, span]
                turned = swap_halves(value)
                fields.append(
                    (
                        pair_rows(jnp.where(low, value, turned), low),
                        pair_rows(jnp.where(low, turned, value), low),
                    )
                )
        stacked = [fields[0][0], fields[0][1], fields[2][0], fields[2][1]]
        stacked += [fields[1][0], fields[1][1], fields[3][0], fields[3][1]]
        taken = dot(jnp.concatenate(stacked, axis=0), take_mat_ref[...])
        tile_vals = [choose(taken, f * tile_rows, tile_rows, late["in_masks"], 0) for f in range(4)]
        rim_at = 4 * tile_rows
        rim_vals = [
            choose(taken, rim_at + f * curve_rows, curve_rows, late["rim_masks"], 0) for f in range(4)
        ]

        rim_cols = [jnp.concatenate(split(value * late["rim_place"]), axis=0) for value in rim_vals]
        placed = dot(late["rim_scatter"], jnp.concatenate(rim_cols, axis=1))
        place_sum = -0.5 * placed[:, :128]
        place_vel = -0.5 * placed[:, 128:256]
        place_pres = jnp.where(low_e, place_vel, -place_vel)
        rim_fields = [
            place_sum,
            place_vel,
            0.5 * placed[:, 256:384],
            0.5 * placed[:, 384:512],
            place_pres,
        ]

        put_sum = -0.5 * tile_vals[0]
        put_n = -0.5 * tile_vals[1]
        put_o = 0.5 * tile_vals[3]
        put = [
            put_sum,
            0.5 * tile_vals[2],
            jnp.where(late["in_y"], put_n, put_o),
            jnp.where(late["in_y"], put_o, put_n),
            late["in_sign_half"] * tile_vals[1],
        ]
        zero_part = jnp.zeros((tile_rows, 128), half_type)
        columns = []
        for f in range(5):
            first = split(put[f] * late["in_low_faces"])
            second = split(put[f] * late["in_high_faces"])
            high, low = rest_parts[f]
            columns.append(jnp.concatenate([first[0], first[1], zero_part, zero_part], axis=0))
            columns.append(jnp.concatenate([second[0], second[1], high, low], axis=0))
        on_faces = dot(late["tile_scatter"], jnp.concatenate(columns, axis=1))
        spread = dot(
            jnp.concatenate(
                [on_faces[:, 256 * f : 256 * f + 256].astype(half_type) for f in range(5)], axis=0
            ),
            spread_ref[...],
        )
        finished = []
        for f in range(5):
            nodes = spread[f * elements : (f + 1) * elements]
            first = nodes[:, :128] + jnp.where(low_e, rim_fields[f], 0.0)
            last = nodes[:, 384:] + jnp.where(low_e, 0.0, rim_fields[f])
            nodes = jnp.concatenate([first, nodes[:, 128:384], last], axis=1)
            finished.append(result[f] + late["lift"] * nodes)
        return finished

    loads[0].wait()
    held_state[...] = state_ref[...]

    for stage in range(3):
        current = [held_state[f] for f in range(5)]
        change = rates(current, stage)
        for f in range(5):
            moved = held_state[f] + change[f]
            if stage == 0:
                held_state[f] = moved
            elif stage == 1:
                held_state[f] = 0.75 * state_ref[f] + 0.25 * moved
            else:
                out_ref[f] = state_ref[f] / 3.0 + (2.0 / 3.0) * moved
    for stage in range(3):
        for copy in tile_copies(stage):
            copy.wait_send()

    @pl.when(has_prev)
    def _():
        for stage in range(3):
            curve_copy(stage, 0).wait_send()

    @pl.when(has_next)
    def _():
        for stage in range(3):
            curve_copy(stage, 1).wait_send()


def shards(
    state,
    levels,
    send_faces,
    send_counts,
    recv_faces,
    recv_orients,
    recv_counts,
    curve_faces,
    curve_orients,
    curve_counts,
):
    curves = lax.axis_size("curve")
    tiles, cap_tile = send_faces.shape
    cap_curve = curve_faces.shape[1]
    elements = state.shape[1]
    half_rows = -(-cap_tile // 4) * 4
    sizes = (curves, tiles, elements, cap_tile, cap_curve, half_rows)
    block = 2 * half_rows
    operands = [
        state,
        levels,
        send_faces,
        send_counts,
        recv_faces,
        recv_orients,
        recv_counts,
        curve_faces,
        curve_orients,
        curve_counts,
        *tables(),
    ]
    held = [
        pltpu.SMEM(value.shape, value.dtype)
        if value.ndim == 1
        else pltpu.VMEM(value.shape, value.dtype)
        for value in operands
    ]
    return pl.pallas_call(
        functools.partial(section_kernel, sizes),
        out_shape=pltpu.VMEM(state.shape, state.dtype),
        in_specs=[pl.BlockSpec(memory_space=pl.ANY)] * operand_count,
        out_specs=pl.BlockSpec(memory_space=pltpu.VMEM),
        scratch_shapes=held
        + [
            pltpu.VMEM((3, tiles, block, 256), jnp.float32),
            pltpu.VMEM((3, tiles, block, 256), jnp.float32),
            pltpu.VMEM((3, 2, cap_curve, 256), jnp.float32),
            pltpu.VMEM((3, 2, cap_curve, 256), jnp.float32),
            pltpu.SemaphoreType.DMA((3, tiles)),
            pltpu.SemaphoreType.DMA((3, tiles)),
            pltpu.SemaphoreType.DMA((3, 2)),
            pltpu.SemaphoreType.DMA((3, 2)),
            pltpu.SemaphoreType.DMA((operand_count,)),
            pltpu.VMEM(state.shape, jnp.float32),
        ],
        compiler_params=pltpu.CompilerParams(
            collective_id=0, has_side_effects=True, vmem_limit_bytes=60 * 1024 * 1024
        ),
    )(*operands)


def solution(mesh):
    return jax.shard_map(
        shards,
        mesh=mesh,
        in_specs=(
            P(None, ("curve", "tile"), None),
            P(("curve", "tile")),
            P(("curve", "tile"), None),
            P(("curve", "tile")),
            P(("curve", "tile"), None),
            P(("curve", "tile"), None),
            P(("curve", "tile")),
            P(("curve", "tile"), None),
            P(("curve", "tile"), None),
            P(("curve", "tile")),
        ),
        out_specs=P(None, ("curve", "tile"), None),
        check_vma=False,
    )
```
